32 devices in a mesh: shard: 8 (over z, y), rep: 4 (over x, core).
Axes of the slice: x: 2, y: 2, z: 4, core: 2. Of those that a mesh axis runs over, the one named last changes fastest.
Arguments:
- memory: bfloat16 [8192, 512], P('shard'), may hold values from -4 to 4
- touch_owner: int32 [8192, 1], P(('shard', 'rep')), may hold values from 0 to 7; in each aligned block of 256 rows (0 to 255, 256 to 511, ...) at most 66 rows name the same one
- touch_row: int32 [8192], P(('shard', 'rep')), may hold values from 0 to 1023
- touch_time: int32 [8192], P(('shard', 'rep')), may hold values from 0 to 999
- src_slot: int32 [12288], P(('shard', 'rep')), may hold values from 0 to 255
- dst_slot: int32 [12288], P(('shard', 'rep')), may hold values from 0 to 255
- event_time: int32 [12288], P(('shard', 'rep')), may hold values from 1000 to 1999
- neighbour_blocks: int32 [96, 2], P(('shard', 'rep')), may hold values from 0 to 2
- time_freq: float32 [128], replicated, may hold values from 0.001 to 1
- time_phase: float32 [128], replicated, may hold values from -3.140625 to 3.140625
- w_input: bfloat16 [512, 1536], P(None, 'rep'), may hold values from -0.25 to 0.25
- w_time: bfloat16 [128, 1536], P(None, 'rep'), may hold values from -0.5 to 0.5
- w_hidden: bfloat16 [512, 1536], P(None, 'rep'), may hold values from -0.25 to 0.25
- w_query: bfloat16 [512, 512], P(None, 'rep'), may hold values from -0.25 to 0.25
- w_keyval: bfloat16 [512, 1024], P(None, 'rep'), may hold values from -0.25 to 0.25
Outputs:
- event_embed: bfloat16 [12288, 512], P(('shard', 'rep'))
- new_memory: bfloat16 [8192, 512], P('shard')
The draws below stay inside these ranges and needn't reach their ends.
Inputs may be any that keep to these rules, and one draw needn't show every extreme that they name: `touch_owner`: in each batch of 256 touched entries at most 66 have the same owner, and some owner has exactly 66 in every draw.
All inputs are finite; a program needn't handle non-finite values.
Results may differ from the reference program's by a relative error of at most 0.0054.
Values may be sent and summed in bfloat16 or wider, within the bound.
No kernel may reach another device: no remote copies, remote signals or barrier semaphores. Data moves between devices by JAX's collectives and lax.ppermute only.
A program may use at most 64 MiB of HBM per device.

```python
import math
import jax
import jax.numpy as jnp
import numpy as np
from jax import lax

D = 512
TD = 128
H = 4
BLK = 128
NB = 2
EV_DEV = 384
TOUCH = 256
ROWS_DEV = 1024
CAP = 66
QBLK = 3
EVENTS = 12288
TOUCHES = 8192
QBLOCKS = 96
VERT = 8192
N_SHARD = 8
N_REP = 4


def touch_ends(values, rng, smallest, largest):
    place = [jax.random.randint(jax.random.fold_in(rng, axis), (), 0, length) for axis, length in enumerate(values.shape)]
    widest = values.shape.index(max(values.shape))
    beside = place[:widest] + [(place[widest] + 1) % values.shape[widest]] + place[widest + 1:]
    return values.at[tuple(place)].set(smallest).at[tuple(beside)].set(largest)


def levels(stream_key, extent, pieces, least, high):
    factor_of = 1.0
    for axis_at, blocks in pieces:
        draws = jax.random.uniform(jax.random.fold_in(jax.random.fold_in(stream_key, 6), axis_at), (blocks,), jnp.float32, least / len(pieces), high / len(pieces))
        factor_of = factor_of * jnp.repeat(jnp.exp(draws), extent[axis_at] // blocks).reshape((-1,) + (1,) * (len(extent) - 1 - axis_at))
    return factor_of


def assign_block(stream_key, own, number, rows, amount, top, bound, slope):
    order = jax.random.permutation(stream_key, amount)
    crowded, common = load_shares(amount, rows * top, bound, slope, True), load_shares(amount, rows * top, bound, slope, False)
    places = jnp.arange(amount)

    def named(lengths, turn):
        used = int((lengths > 0).sum())
        fixed = max(1, used // 4)
        shifted = fixed + (places - fixed + turn * (used - fixed)) % max(1, amount - fixed)
        return jnp.zeros((amount,), jnp.int32).at[order[jnp.where(places < fixed, places, shifted)]].set(jnp.asarray(lengths, jnp.int32))

    lengths = jnp.where(number % 4 == 0, named(crowded, number // 4), named(common, number - number // 4 - 1))
    mixed = jax.random.permutation(jax.random.fold_in(own, 3), amount)
    giver, taker = mixed[0:amount // 2 * 2:2], mixed[1:amount // 2 * 2:2]
    margin = jnp.minimum(lengths[giver] - 1, bound - lengths[taker]) // 2
    margin = jnp.where((giver == order[0]) | (taker == order[0]) | (lengths[taker] == 0), 0, jnp.maximum(margin, 0))
    shifted = jax.random.randint(jax.random.fold_in(own, 4), (amount // 2,), 0, 1 << 20) % (margin + 1)
    lengths = lengths.at[giver].add(-shifted).at[taker].add(shifted)
    items = jnp.searchsorted(jnp.cumsum(lengths), jnp.arange(rows * top), side="right").astype(jnp.int32)
    grid = items.reshape(top, rows).T
    grid = grid[jax.random.permutation(jax.random.fold_in(own, 1), rows)]
    turn = jax.random.randint(jax.random.fold_in(own, 2), (rows, 1), 0, top)
    return jnp.take_along_axis(grid, (jnp.arange(top)[None, :] + turn) % top, axis=1)


def load_shares(number_of, total, limit, lean, full):
    weights = [(1 << 20) // math.isqrt(grade ** lean) + 1 for grade in range(1, number_of + 1)]
    largest = limit if full else min(limit, max(-(-total // number_of), total * weights[0] // sum(weights)))
    least = 1 if total - largest >= number_of - 1 else 0
    given, spare = [largest] + [least] * (number_of - 1), total - largest - least * (number_of - 1)
    while spare > 0:
        movable = [i for i in range(1, number_of) if given[i] < largest] or [i for i in range(1, number_of) if given[i] < limit]
        mass, left = sum([weights[i] for i in movable]), spare
        for i in movable:
            addition = min(limit - given[i], max(1, left * weights[i] // mass), spare)
            given[i] = given[i] + addition
            spare = spare - addition
    return np.array(given)


def gaussian(own_key, shape, deviation, bound, pieces=(), dtype=jnp.bfloat16):
    result = deviation * jax.random.normal(own_key, shape, jnp.float32)
    if pieces:
        result = result * levels(own_key, shape, pieces, -0.22, 0.18)
    return jnp.clip(result, -bound, bound).astype(dtype)


def setup_inputs(seed: int = 0) -> dict:
    splits = jax.random.split(jax.random.key(seed), 16)
    memory = gaussian(splits[0], (VERT, D), 1.0, 4.0, ((0, 8),))
    touch_owner_keys = jax.random.split(jax.random.fold_in(splits[1], 1), TOUCHES // TOUCH)
    touch_owner_turns = jax.random.permutation(jax.random.fold_in(splits[1], 3), TOUCHES // TOUCH)
    touch_owner = jax.vmap(lambda own, number: assign_block(jax.random.fold_in(splits[1], 2), own, number, TOUCH, N_SHARD, 1, CAP, 2))(touch_owner_keys, touch_owner_turns).reshape((TOUCHES, 1))
    touch_row = touch_ends(jax.random.randint(splits[2], (TOUCHES,), 0, ROWS_DEV), jax.random.fold_in(splits[2], 1), 0, ROWS_DEV - 1).astype(jnp.int32)
    touch_time = touch_ends(jax.random.randint(splits[3], (TOUCHES,), 0, 1000), jax.random.fold_in(splits[3], 1), 0, 999).astype(jnp.int32)
    src_slot = touch_ends(jax.random.randint(splits[4], (EVENTS,), 0, TOUCH), jax.random.fold_in(splits[4], 1), 0, TOUCH - 1).astype(jnp.int32)
    dst_slot = touch_ends(jax.random.randint(splits[5], (EVENTS,), 0, TOUCH), jax.random.fold_in(splits[5], 1), 0, TOUCH - 1).astype(jnp.int32)
    event_time = touch_ends(jax.random.randint(splits[6], (EVENTS,), 1000, 2000), jax.random.fold_in(splits[6], 1), 1000, 1999).astype(jnp.int32)
    neighbour_blocks = touch_ends(jax.random.randint(splits[7], (QBLOCKS, NB), 0, QBLK), jax.random.fold_in(splits[7], 1), 0, QBLK - 1).astype(jnp.int32)
    time_freq = jnp.clip(jnp.exp(jax.random.uniform(splits[8], (TD,), jnp.float32, math.log(0.001), math.log(1.0))), 0.001, 1.0)
    time_phase = jnp.clip(jax.random.uniform(splits[9], (TD,), jnp.float32, -3.140625, 3.140625), -3.140625, 3.140625)
    w_input = gaussian(splits[10], (D, 3 * D), D ** -0.5, 0.25, ((1, 4),))
    w_time = gaussian(splits[11], (TD, 3 * D), TD ** -0.5, 0.5, ((1, 4),))
    w_hidden = gaussian(splits[12], (D, 3 * D), D ** -0.5, 0.25, ((1, 4),))
    w_query = gaussian(splits[13], (D, D), D ** -0.5, 0.25, ((1, 4),))
    w_keyval = gaussian(splits[14], (D, 2 * D), D ** -0.5, 0.25, ((1, 4),))
    return dict(memory=memory, touch_owner=touch_owner, touch_row=touch_row, touch_time=touch_time, src_slot=src_slot, dst_slot=dst_slot, event_time=event_time, neighbour_blocks=neighbour_blocks, time_freq=time_freq, time_phase=time_phase, w_input=w_input, w_time=w_time, w_hidden=w_hidden, w_query=w_query, w_keyval=w_keyval)


def event_update(fetched, tick, source, target, stamp, listed, time_freq, time_phase, w_input, w_time, w_hidden, w_query, w_keyval):
    width = fetched.shape[1]
    count = stamp.shape[0]
    hsrc = fetched[source]
    hdst = fetched[target]
    spans = (stamp - tick[source]).astype(jnp.float32)
    encode = jnp.cos(spans[:, None] * time_freq[None, :] + time_phase[None, :]).astype(jnp.bfloat16)
    gin = jnp.dot(hdst, w_input, preferred_element_type=jnp.float32) + jnp.dot(encode, w_time, preferred_element_type=jnp.float32)
    ghid = jnp.dot(hsrc, w_hidden, preferred_element_type=jnp.float32)
    reset = jax.nn.sigmoid(gin[:, :width] + ghid[:, :width])
    update = jax.nn.sigmoid(gin[:, width:2 * width] + ghid[:, width:2 * width])
    fresh = jnp.tanh(gin[:, 2 * width:] + reset * ghid[:, 2 * width:])
    hold = hsrc.astype(jnp.float32)
    hnew = (1.0 - update) * fresh + update * hold
    entries = fetched.shape[0]
    counts = jax.ops.segment_sum(jnp.ones((count,), jnp.float32), source, entries)
    delta = jax.ops.segment_sum(hnew - hold, source, entries) / jnp.maximum(counts, 1.0)[:, None]
    hround = hnew.astype(jnp.bfloat16)
    query = jnp.dot(hround, w_query, preferred_element_type=jnp.float32).astype(jnp.bfloat16)
    keyval = jnp.dot(hdst, w_keyval, preferred_element_type=jnp.float32).astype(jnp.bfloat16)
    blocks = count // BLK
    headsz = width // H
    query4 = query.reshape(blocks, BLK, H, headsz)
    keys = keyval[:, :width].reshape(blocks, BLK, H, headsz)[listed].reshape(blocks, NB * BLK, H, headsz)
    values = keyval[:, width:].reshape(blocks, BLK, H, headsz)[listed].reshape(blocks, NB * BLK, H, headsz)
    scores = jnp.einsum('qihd,qjhd->qhij', query4.astype(jnp.float32), keys.astype(jnp.float32)) / math.sqrt(headsz)
    prob = jax.nn.softmax(scores, axis=-1).astype(jnp.bfloat16)
    attend = jnp.einsum('qhij,qjhd->qihd', prob.astype(jnp.float32), values.astype(jnp.float32)).reshape(count, width)
    embed = (hnew + attend).astype(jnp.bfloat16)
    return (embed, delta)

def reference(memory, touch_owner, touch_row, touch_time, src_slot, dst_slot, event_time, neighbour_blocks, time_freq, time_phase, w_input, w_time, w_hidden, w_query, w_keyval):
    batches = N_SHARD * N_REP
    vertex = (touch_owner[:, 0] * ROWS_DEV + touch_row).astype(jnp.int32)

    def one_batch(items):
        ids, tick, source, target, stamp, listed = items
        fetched = jnp.take(memory, ids, axis=0)
        return event_update(fetched, tick, source, target, stamp, listed, time_freq, time_phase, w_input, w_time, w_hidden, w_query, w_keyval)
    items = (vertex.reshape(batches, TOUCH), touch_time.reshape(batches, TOUCH), src_slot.reshape(batches, EV_DEV), dst_slot.reshape(batches, EV_DEV), event_time.reshape(batches, EV_DEV), neighbour_blocks.reshape(batches, QBLK, NB))
    embeds, deltas = lax.map(one_batch, items)
    width = memory.shape[1]
    total = jax.ops.segment_sum(deltas.reshape(-1, width), vertex, VERT)
    new_memory = (memory.astype(jnp.float32) + total).astype(jnp.bfloat16)
    return (embeds.reshape(-1, width), new_memory)
```

```python
import functools
import math

import jax
import jax.numpy as jnp
from jax import lax
from jax.experimental import pallas as pl
from jax.experimental.pallas import tpu as pltpu
from jax.sharding import PartitionSpec as P

H = 4
BLK = 128
NB = 2
LANES = 128
F32 = jnp.float32
BF16 = jnp.bfloat16
I32 = jnp.int32
VMEM = pl.BlockSpec(memory_space=pltpu.VMEM)
SMEM = pl.BlockSpec(memory_space=pltpu.SMEM)


def iota(shape, dim):
    return lax.broadcasted_iota(I32, shape, dim)


def dot(a, b):
    return jnp.dot(a, b, preferred_element_type=F32)


def call(body, outs, specs, flops, bytes_, name, scratch=(), limit=32):
    return pl.pallas_call(
        body,
        out_shape=outs,
        in_specs=specs,
        out_specs=[VMEM] * len(outs),
        scratch_shapes=list(scratch),
        compiler_params=pltpu.CompilerParams(vmem_limit_bytes=limit << 20),
        cost_estimate=pl.CostEstimate(flops=flops, bytes_accessed=bytes_, transcendentals=0),
        name=name,
    )


class Plan:
    def __init__(self, owners, reps, entries):
        self.owners = owners
        self.reps = reps
        self.entries = entries
        self.cap = 2 * entries // owners + 2
        self.tail = self.cap % 16 if self.cap % 16 * 4 == 8 else 0
        self.main = self.cap - self.tail if self.tail else -(-self.cap // 16) * 16
        self.rows = self.owners * (self.main + self.tail)
        self.pad = -(-self.cap // 8) * 8


def rank_of(own_col, own_row, entries):
    earlier = (own_col == own_row) & (iota((entries, entries), 0) < iota((entries, entries), 1))
    later = (own_col == own_row) & (iota((entries, entries), 1) < iota((entries, entries), 0))
    place_row = jnp.sum(jnp.where(earlier, 1, 0), axis=0, keepdims=True)
    place_col = jnp.sum(jnp.where(later, 1, 0), axis=1, keepdims=True)
    return place_row, place_col


def to_col(row, size):
    eye = iota((size, size), 0) == iota((size, size), 1)
    return jnp.sum(jnp.where(eye, row, 0), axis=1, keepdims=True)


def request_kernel(plan, owner_ref, row_ref, out_ref):
    own_row = owner_ref[...]
    own_col = to_col(own_row, plan.entries)
    _, place_col = rank_of(own_col, own_row, plan.entries)
    row = row_ref[...]
    mine = iota((plan.owners, plan.entries), 0) == own_row
    spot = jnp.where(place_col == iota((plan.entries, LANES), 1), 1.0, 0.0).astype(BF16)
    high = jnp.where(mine, row >> 5, 0).astype(F32).astype(BF16)
    low = jnp.where(mine, row & 31, 0).astype(F32).astype(BF16)
    out_ref[...] = (dot(high, spot) * 32.0 + dot(low, spot)).astype(I32)


def index_kernel(plan, owner_ref, tick_ref, src_ref, dst_ref, stamp_ref, freq_ref, phase_ref, enc_ref, col_ref, row_ref):
    events = src_ref.shape[1]
    own_row = owner_ref[...]
    own_col = to_col(own_row, plan.entries)
    _, place = rank_of(own_col, own_row, plan.entries)
    tick = to_col(tick_ref[...], plan.entries)
    spot = own_col * plan.main + place
    if plan.tail:
        spare = plan.owners * plan.main + (place - plan.main) * plan.owners + own_col
        spot = jnp.where(place < plan.main, spot, spare)
    back = own_col * plan.pad + place
    isrc = iota((plan.entries, events), 0) == src_ref[...]
    idst = iota((plan.entries, events), 0) == dst_ref[...]

    def pick(mask, values):
        return jnp.sum(jnp.where(mask, values, 0), axis=0, keepdims=True)

    src_spot = pick(isrc, spot)
    dst_spot = pick(idst, spot)
    src_back = pick(isrc, back)
    span = stamp_ref[...] - pick(isrc, tick)
    zero = jnp.zeros((8 - 3, events), I32)
    rows = jnp.concatenate([src_spot, dst_spot, span, zero], axis=0)
    row_ref[...] = jnp.concatenate([src_back, jnp.zeros((7, events), I32)], axis=0)
    cols = rows.astype(F32).T
    col_ref[...] = cols
    enc_ref[...] = jnp.cos(cols[:, 2:3] * freq_ref[...] + phase_ref[...]).astype(BF16)


def tail_order(plan, forward):
    count = 4 * plan.tail * plan.owners
    across = 0 if forward else 1
    there = iota((count, count), across)
    here = iota((count, count), 1 - across)
    part = 4 * plan.tail
    owner, inner = there // part, there % part
    return jnp.where((inner * plan.owners + owner) == here, 1.0, 0.0).astype(BF16)


def serve_kernel(plan, asked_ref, memory_ref, out_ref):
    stored, width = memory_ref.shape
    piece = width // 4
    asked = asked_ref[...].astype(F32)
    turned = asked.T
    blocks = [
        jnp.where(turned[: plan.main, s : s + 1].astype(I32) == iota((plan.main, stored), 1), 1.0, 0.0)
        for s in range(plan.owners)
    ]
    for i in range(plan.tail):
        spare = asked_ref[:, plan.main + i : plan.main + i + 1]
        blocks.append(jnp.where(spare == iota((plan.owners, stored), 1), 1.0, 0.0))
    hot = jnp.concatenate(blocks, axis=0).astype(BF16)
    rows = dot(hot, memory_ref[...])
    main = plan.main
    for s in range(plan.owners):
        for c in range(4):
            out_ref[s, c * main : (c + 1) * main, :] = rows[
                s * main : (s + 1) * main, c * piece : (c + 1) * piece
            ].astype(BF16)
    if plan.tail:
        spare = rows[plan.owners * main :]
        stack = jnp.concatenate([spare[:, c * piece : (c + 1) * piece] for c in range(4)], axis=0)
        ordered = dot(tail_order(plan, True), stack.astype(BF16))
        for s in range(plan.owners):
            out_ref[s, 4 * main : 4 * (main + plan.tail), :] = ordered[
                s * 4 * plan.tail : (s + 1) * 4 * plan.tail
            ].astype(BF16)


def table_of(plan, ret_ref):
    main = plan.main
    pieces = [
        jnp.concatenate([ret_ref[s, c * main : (c + 1) * main, :] for s in range(plan.owners)], axis=0)
        for c in range(4)
    ]
    table = jnp.concatenate(pieces, axis=1)
    if plan.tail:
        stack = jnp.concatenate(
            [ret_ref[s, 4 * main : 4 * (main + plan.tail), :].astype(F32) for s in range(plan.owners)], axis=0
        )
        ordered = dot(tail_order(plan, False), stack.astype(BF16))
        count = plan.tail * plan.owners
        spare = jnp.concatenate([ordered[c * count : (c + 1) * count] for c in range(4)], axis=1)
        table = jnp.concatenate([table, spare.astype(BF16)], axis=0)
    return table


def gru_kernel(plan, ret_ref, enc_ref, col_ref, row_ref, *refs):
    reps = plan.reps
    w_in, w_time, w_hid = refs[:reps], refs[reps : 2 * reps], refs[2 * reps : 3 * reps]
    out_ref, hnew_ref, hdst_ref, gin, ghid, delta = refs[3 * reps :]
    me = lax.axis_index("rep")
    events, width = hnew_ref.shape
    piece = width // reps
    cols = col_ref[...].astype(I32)
    spots = iota((events, plan.rows), 1)
    table = table_of(plan, ret_ref)
    hsrc = dot(jnp.where(cols[:, 0:1] == spots, 1.0, 0.0).astype(BF16), table)
    source = hsrc.astype(BF16)
    target = dot(jnp.where(cols[:, 1:2] == spots, 1.0, 0.0).astype(BF16), table).astype(BF16)
    hdst_ref[...] = target
    enc = enc_ref[...]
    part = w_in[0].shape[1]
    for k in range(reps):
        at = pl.ds(pl.multiple_of((me ^ k) * part, LANES), part)
        gin[:, at] = dot(target, w_in[k][...]) + dot(enc, w_time[k][...])
        ghid[:, at] = dot(source, w_hid[k][...])
    step = 64
    for i in range(0, events, step):
        at = slice(i, i + step)
        reset = 0.5 * jnp.tanh(0.5 * (gin[at, :width] + ghid[at, :width])) + 0.5
        update = 0.5 * jnp.tanh(0.5 * (gin[at, width : 2 * width] + ghid[at, width : 2 * width])) + 0.5
        fresh = jnp.tanh(gin[at, 2 * width :] + reset * ghid[at, 2 * width :])
        hold = hsrc[at]
        new = (1.0 - update) * fresh + update * hold
        hnew_ref[at, :] = new
        delta[at, :] = new - hold
    change = delta[...]
    high = change.astype(BF16)
    low = (change - high.astype(F32)).astype(BF16)
    slots = plan.owners * plan.pad
    hits = jnp.where(row_ref[0:1, :] == iota((slots, events), 0), 1.0, 0.0)
    counts = jnp.maximum(jnp.sum(hits, axis=1, keepdims=True), 1.0)
    hits = hits.astype(BF16)
    mean = (dot(hits, high) + dot(hits, low)) / counts
    for o in range(plan.owners):
        for q in range(reps):
            out_ref[o * reps + q] = mean[o * plan.pad : (o + 1) * plan.pad, q * piece : (q + 1) * piece].astype(BF16)


def attend_kernel(plan, listed_ref, hnew_ref, hdst_ref, *refs):
    reps = plan.reps
    w_query, w_keyval = refs[:reps], refs[reps : 2 * reps]
    out_ref, query, keyval = refs[2 * reps :]
    me = lax.axis_index("rep")
    events, width = hnew_ref.shape
    head = width // H
    hround = hnew_ref[...].astype(BF16)
    target = hdst_ref[...]
    for k in range(reps):
        part = w_query[k].shape[1]
        query[:, pl.ds(pl.multiple_of((me ^ k) * part, LANES), part)] = dot(hround, w_query[k][...]).astype(BF16)
        part = w_keyval[k].shape[1]
        keyval[:, pl.ds(pl.multiple_of((me ^ k) * part, LANES), part)] = dot(target, w_keyval[k][...]).astype(BF16)
    for i in range(events // BLK):
        spans = [pl.ds(pl.multiple_of(listed_ref[i, j] * BLK, BLK), BLK) for j in range(NB)]
        at = slice(i * BLK, (i + 1) * BLK)
        for h in range(H):
            lane = slice(h * head, (h + 1) * head)
            keys = jnp.concatenate([keyval[s, lane] for s in spans], axis=0)
            values = jnp.concatenate([keyval[s, width + h * head : width + (h + 1) * head] for s in spans], axis=0)
            scores = lax.dot_general(
                query[at, lane], keys, (((1,), (1,)), ((), ())), preferred_element_type=F32
            ) * (1.0 / math.sqrt(head))
            peak = jnp.max(scores, axis=1, keepdims=True)
            power = jnp.exp(scores - peak)
            prob = (power / jnp.sum(power, axis=1, keepdims=True)).astype(BF16)
            out_ref[at, lane] = (hnew_ref[at, lane] + dot(prob, values)).astype(BF16)


def apply_kernel(plan, ids_ref, landed_ref, memory_ref, out_ref):
    stored = memory_ref.shape[0]
    piece = out_ref.shape[1]
    count = landed_ref.shape[0]
    me = lax.axis_index("rep")
    landed = landed_ref[...]
    lane = pl.ds(pl.multiple_of(me * piece, LANES), piece)
    step = min(256, stored)
    ids = ids_ref[...]
    for i in range(0, stored, step):
        hot = jnp.where(iota((step, count), 0) + i == ids, 1.0, 0.0).astype(BF16)
        total = dot(hot, landed)
        out_ref[i : i + step, :] = (memory_ref[i : i + step, lane].astype(F32) + total).astype(BF16)


def join_kernel(plan, *refs):
    me = lax.axis_index("rep")
    out_ref = refs[-1]
    for k in range(plan.reps):
        piece = refs[k].shape[1]
        out_ref[:, pl.ds(pl.multiple_of((me ^ k) * piece, LANES), piece)] = refs[k][...]


def swap(x, bit, reps):
    return lax.ppermute(x, "rep", [(i, i ^ bit) for i in range(reps)])


def spread(arrays, reps):
    held = [{0: x} for x in arrays]
    bit = reps // 2
    while bit:
        for parts in held:
            for k in list(parts):
                parts[k ^ bit] = swap(parts[k], bit, reps)
        bit //= 2
    return [[parts[k] for k in range(reps)] for parts in held]


def shards(
    memory,
    touch_owner,
    touch_row,
    touch_time,
    src_slot,
    dst_slot,
    event_time,
    neighbour_blocks,
    time_freq,
    time_phase,
    w_input,
    w_time,
    w_hidden,
    w_query,
    w_keyval,
):
    owners = lax.axis_size("shard")
    reps = lax.axis_size("rep")
    entries = touch_row.shape[0]
    events = event_time.shape[0]
    stored, width = memory.shape
    plan = Plan(owners, reps, entries)
    piece = width // reps
    run = functools.partial
    sds = jax.ShapeDtypeStruct

    owner = touch_owner.reshape(1, entries)
    request = call(
        run(request_kernel, plan), [sds((owners, LANES), I32)], [VMEM] * 2, 1 << 20, 1 << 14, "request", limit=8
    )(owner, touch_row.reshape(1, entries))[0]

    full_hidden, full_input, full_time, full_keyval, full_query = spread(
        [w_hidden, w_input, w_time, w_keyval, w_query], reps
    )

    asked = lax.all_to_all(request, "shard", split_axis=0, concat_axis=0, tiled=True)
    encode, cols, rows = call(
        run(index_kernel, plan),
        [sds((events, time_freq.shape[0]), BF16), sds((events, 8), F32), sds((8, events), I32)],
        [VMEM] * 7,
        1 << 22,
        1 << 18,
        "index",
        limit=8,
    )(
        owner,
        touch_time.reshape(1, entries),
        src_slot.reshape(1, events),
        dst_slot.reshape(1, events),
        event_time.reshape(1, events),
        time_freq.reshape(1, -1),
        time_phase.reshape(1, -1),
    )
    everyone = [x for x in spread([asked], reps)[0]]

    chunk = 4 * (plan.main + plan.tail)
    served = call(
        run(serve_kernel, plan),
        [sds((owners, chunk, width // 4), BF16)],
        [VMEM] * 2,
        2 * plan.rows * stored * width,
        2 * stored * width + 2 * plan.rows * width,
        "serve",
        limit=24,
    )(asked, memory)[0]
    returned = lax.all_to_all(served, "shard", split_axis=0, concat_axis=0, tiled=True)

    outgoing, hnew, hdst = call(
        run(gru_kernel, plan),
        [sds((owners * reps, plan.pad, piece), BF16), sds((events, width), F32), sds((events, width), BF16)],
        [VMEM] * (4 + 3 * reps),
        2 * events * width * 3 * width * 2,
        8 << 20,
        "gru",
        scratch=[
            pltpu.VMEM((events, 3 * width), F32),
            pltpu.VMEM((events, 3 * width), F32),
            pltpu.VMEM((events, width), F32),
        ],
        limit=40,
    )(returned, encode, cols, rows, *full_input, *full_time, *full_hidden)
    landed = lax.all_to_all(outgoing, ("shard", "rep"), split_axis=0, concat_axis=0, tiled=True)

    embed = call(
        run(attend_kernel, plan),
        [sds((events, width), BF16)],
        [SMEM] + [VMEM] * (2 + 2 * reps),
        2 * events * width * 3 * width,
        4 << 20,
        "attend",
        scratch=[pltpu.VMEM((events, width), BF16), pltpu.VMEM((events, 2 * width), BF16)],
        limit=24,
    )(neighbour_blocks, hnew, hdst, *full_query, *full_keyval)[0]

    me = lax.axis_index("rep")
    stack = jnp.stack([x[:, : plan.pad] for x in everyone])
    order = me ^ jnp.arange(reps, dtype=I32)
    ids = jnp.swapaxes(stack[order], 0, 1).reshape(1, owners * reps * plan.pad)
    quarter = call(
        run(apply_kernel, plan),
        [sds((stored, piece), BF16)],
        [VMEM] * 3,
        2 * stored * owners * reps * plan.pad * piece * 2,
        4 << 20,
        "apply",
        limit=32,
    )(ids, landed.reshape(owners * reps * plan.pad, piece), memory)[0]
    new_memory = call(
        run(join_kernel, plan), [sds((stored, width), BF16)], [VMEM] * reps, 1 << 20, 2 << 20, "join", limit=8
    )(*spread([quarter], reps)[0])[0]
    return (embed, new_memory)


def solution(mesh):
    placed = (
        P("shard", None),
        P(("shard", "rep"), None),
        P(("shard", "rep")),
        P(("shard", "rep")),
        P(("shard", "rep")),
        P(("shard", "rep")),
        P(("shard", "rep")),
        P(("shard", "rep"), None),
        P(),
        P(),
        P(None, "rep"),
        P(None, "rep"),
        P(None, "rep"),
        P(None, "rep"),
        P(None, "rep"),
    )
    return jax.shard_map(
        shards,
        mesh=mesh,
        in_specs=placed,
        out_specs=(P(("shard", "rep"), None), P("shard", None)),
        check_vma=False,
    )
```

```python
import functools
import math

import jax
import jax.numpy as jnp
from jax import lax
from jax.experimental import pallas as pl
from jax.experimental.pallas import tpu as pltpu
from jax.sharding import PartitionSpec as P

H = 4
BLK = 128
NB = 2
LANES = 128
F32 = jnp.float32
BF16 = jnp.bfloat16
I32 = jnp.int32
VMEM = pl.BlockSpec(memory_space=pltpu.VMEM)
SMEM = pl.BlockSpec(memory_space=pltpu.SMEM)
ANY = pl.BlockSpec(memory_space=pl.ANY)


def iota(shape, dim):
    return lax.broadcasted_iota(I32, shape, dim)


def dot(a, b):
    return jnp.dot(a, b, preferred_element_type=F32)


def call(body, outs, specs, flops, bytes_, name, scratch=(), limit=32):
    return pl.pallas_call(
        body,
        out_shape=outs,
        in_specs=specs,
        out_specs=[VMEM] * len(outs),
        scratch_shapes=list(scratch),
        compiler_params=pltpu.CompilerParams(vmem_limit_bytes=limit << 20),
        cost_estimate=pl.CostEstimate(flops=flops, bytes_accessed=bytes_, transcendentals=0),
        name=name,
    )


class Plan:
    def __init__(self, owners, reps, entries):
        self.owners = owners
        self.reps = reps
        self.entries = entries
        self.cap = 2 * entries // owners + 2
        self.tail = self.cap % 16 if self.cap % 16 * 4 == 8 else 0
        self.main = self.cap - self.tail if self.tail else -(-self.cap // 16) * 16
        self.rows = self.owners * (self.main + self.tail)
        self.pad = -(-self.cap // 8) * 8


def rank_of(own_col, own_row, entries):
    earlier = (own_col == own_row) & (iota((entries, entries), 0) < iota((entries, entries), 1))
    later = (own_col == own_row) & (iota((entries, entries), 1) < iota((entries, entries), 0))
    place_row = jnp.sum(jnp.where(earlier, 1, 0), axis=0, keepdims=True)
    place_col = jnp.sum(jnp.where(later, 1, 0), axis=1, keepdims=True)
    return place_row, place_col


def to_col(row, size):
    eye = iota((size, size), 0) == iota((size, size), 1)
    return jnp.sum(jnp.where(eye, row, 0), axis=1, keepdims=True)


def request_kernel(plan, owner_ref, row_ref, out_ref):
    own_row = owner_ref[...]
    own_col = to_col(own_row, plan.entries)
    _, place_col = rank_of(own_col, own_row, plan.entries)
    row = row_ref[...]
    mine = iota((plan.owners, plan.entries), 0) == own_row
    spot = jnp.where(place_col == iota((plan.entries, LANES), 1), 1.0, 0.0).astype(BF16)
    high = jnp.where(mine, row >> 5, 0).astype(F32).astype(BF16)
    low = jnp.where(mine, row & 31, 0).astype(F32).astype(BF16)
    out_ref[...] = (dot(high, spot) * 32.0 + dot(low, spot)).astype(I32)


def index_kernel(plan, owner_ref, tick_ref, src_ref, dst_ref, stamp_ref, freq_ref, phase_ref, enc_ref, col_ref, row_ref):
    events = src_ref.shape[1]
    own_row = owner_ref[...]
    own_col = to_col(own_row, plan.entries)
    _, place = rank_of(own_col, own_row, plan.entries)
    tick = to_col(tick_ref[...], plan.entries)
    spot = own_col * plan.main + place
    if plan.tail:
        spare = plan.owners * plan.main + (place - plan.main) * plan.owners + own_col
        spot = jnp.where(place < plan.main, spot, spare)
    back = own_col * plan.pad + place
    isrc = iota((plan.entries, events), 0) == src_ref[...]
    idst = iota((plan.entries, events), 0) == dst_ref[...]

    def pick(mask, values):
        return jnp.sum(jnp.where(mask, values, 0), axis=0, keepdims=True)

    src_spot = pick(isrc, spot)
    dst_spot = pick(idst, spot)
    src_back = pick(isrc, back)
    span = stamp_ref[...] - pick(isrc, tick)
    zero = jnp.zeros((8 - 3, events), I32)
    rows = jnp.concatenate([src_spot, dst_spot, span, zero], axis=0)
    row_ref[...] = jnp.concatenate([src_back, jnp.zeros((7, events), I32)], axis=0)
    cols = rows.astype(F32).T
    col_ref[...] = cols
    enc_ref[...] = jnp.cos(cols[:, 2:3] * freq_ref[...] + phase_ref[...]).astype(BF16)


def tail_order(plan, forward):
    count = 4 * plan.tail * plan.owners
    across = 0 if forward else 1
    there = iota((count, count), across)
    here = iota((count, count), 1 - across)
    part = 4 * plan.tail
    owner, inner = there // part, there % part
    return jnp.where((inner * plan.owners + owner) == here, 1.0, 0.0).astype(BF16)


def serve_kernel(plan, asked_ref, memory_ref, *refs):
    out_ref = refs[-1]
    stored, width = memory_ref.shape
    piece = width // 4
    asked = asked_ref[...].astype(F32)
    turned = asked.T
    blocks = [
        jnp.where(turned[: plan.main, s : s + 1].astype(I32) == iota((plan.main, stored), 1), 1.0, 0.0)
        for s in range(plan.owners)
    ]
    for i in range(plan.tail):
        spare = asked_ref[:, plan.main + i : plan.main + i + 1]
        blocks.append(jnp.where(spare == iota((plan.owners, stored), 1), 1.0, 0.0))
    hot = jnp.concatenate(blocks, axis=0).astype(BF16)
    rows = dot(hot, memory_ref[...])
    main = plan.main
    for s in range(plan.owners):
        for c in range(4):
            out_ref[s, c * main : (c + 1) * main, :] = rows[
                s * main : (s + 1) * main, c * piece : (c + 1) * piece
            ].astype(BF16)
    if plan.tail:
        spare = rows[plan.owners * main :]
        stack = jnp.concatenate([spare[:, c * piece : (c + 1) * piece] for c in range(4)], axis=0)
        ordered = dot(tail_order(plan, True), stack.astype(BF16))
        for s in range(plan.owners):
            out_ref[s, 4 * main : 4 * (main + plan.tail), :] = ordered[
                s * 4 * plan.tail : (s + 1) * 4 * plan.tail
            ].astype(BF16)


def table_of(plan, ret_ref):
    main = plan.main
    pieces = [
        jnp.concatenate([ret_ref[s, c * main : (c + 1) * main, :] for s in range(plan.owners)], axis=0)
        for c in range(4)
    ]
    table = jnp.concatenate(pieces, axis=1)
    if plan.tail:
        stack = jnp.concatenate(
            [ret_ref[s, 4 * main : 4 * (main + plan.tail), :].astype(F32) for s in range(plan.owners)], axis=0
        )
        ordered = dot(tail_order(plan, False), stack.astype(BF16))
        count = plan.tail * plan.owners
        spare = jnp.concatenate([ordered[c * count : (c + 1) * count] for c in range(4)], axis=1)
        table = jnp.concatenate([table, spare.astype(BF16)], axis=0)
    return table


def fetch(groups, sems):
    copies = []
    for g, (parts, buffer) in enumerate(groups):
        row = [pltpu.make_async_copy(part, buffer.at[k], sems.at[g, k]) for k, part in enumerate(parts)]
        for copy in row:
            copy.start()
        copies.append(row)
    return copies


def gru_kernel(plan, ret_ref, enc_ref, col_ref, row_ref, *refs):
    reps = plan.reps
    parts_in, parts_time, parts_hid = refs[:reps], refs[reps : 2 * reps], refs[2 * reps : 3 * reps]
    out_ref, hnew_ref, hdst_ref, gin, ghid, delta, w_in, w_time, w_hid, sems = refs[3 * reps :]
    copies = fetch([(parts_in, w_in), (parts_time, w_time), (parts_hid, w_hid)], sems)
    me = lax.axis_index("rep")
    events, width = hnew_ref.shape
    piece = width // reps
    cols = col_ref[...].astype(I32)
    spots = iota((events, plan.rows), 1)
    table = table_of(plan, ret_ref)
    hsrc = dot(jnp.where(cols[:, 0:1] == spots, 1.0, 0.0).astype(BF16), table)
    source = hsrc.astype(BF16)
    target = dot(jnp.where(cols[:, 1:2] == spots, 1.0, 0.0).astype(BF16), table).astype(BF16)
    hdst_ref[...] = target
    enc = enc_ref[...]
    part = w_in.shape[2]
    for k in range(reps):
        for row in copies:
            row[k].wait()
        at = pl.ds(pl.multiple_of((me ^ k) * part, LANES), part)
        gin[:, at] = dot(target, w_in[k]) + dot(enc, w_time[k])
        ghid[:, at] = dot(source, w_hid[k])
    step = 64
    for i in range(0, events, step):
        at = slice(i, i + step)
        reset = 0.5 * jnp.tanh(0.5 * (gin[at, :width] + ghid[at, :width])) + 0.5
        update = 0.5 * jnp.tanh(0.5 * (gin[at, width : 2 * width] + ghid[at, width : 2 * width])) + 0.5
        fresh = jnp.tanh(gin[at, 2 * width :] + reset * ghid[at, 2 * width :])
        hold = hsrc[at]
        new = (1.0 - update) * fresh + update * hold
        hnew_ref[at, :] = new
        delta[at, :] = new - hold
    change = delta[...]
    high = change.astype(BF16)
    low = (change - high.astype(F32)).astype(BF16)
    slots = plan.owners * plan.pad
    hits = jnp.where(row_ref[0:1, :] == iota((slots, events), 0), 1.0, 0.0)
    counts = jnp.maximum(jnp.sum(hits, axis=1, keepdims=True), 1.0)
    hits = hits.astype(BF16)
    mean = (dot(hits, high) + dot(hits, low)) / counts
    for o in range(plan.owners):
        for q in range(reps):
            out_ref[o * reps + q] = mean[o * plan.pad : (o + 1) * plan.pad, q * piece : (q + 1) * piece].astype(BF16)


def attend_kernel(plan, listed_ref, hnew_ref, hdst_ref, *refs):
    reps = plan.reps
    parts_query, parts_keyval = refs[:reps], refs[reps : 2 * reps]
    out_ref, query, keyval, w_query, w_keyval, sems = refs[2 * reps :]
    copies = fetch([(parts_query, w_query), (parts_keyval, w_keyval)], sems)
    me = lax.axis_index("rep")
    events, width = hnew_ref.shape
    head = width // H
    hround = hnew_ref[...].astype(BF16)
    target = hdst_ref[...]
    for k in range(reps):
        for row in copies:
            row[k].wait()
        part = w_query.shape[2]
        query[:, pl.ds(pl.multiple_of((me ^ k) * part, LANES), part)] = dot(hround, w_query[k]).astype(BF16)
        part = w_keyval.shape[2]
        keyval[:, pl.ds(pl.multiple_of((me ^ k) * part, LANES), part)] = dot(target, w_keyval[k]).astype(BF16)
    for i in range(events // BLK):
        spans = [pl.ds(pl.multiple_of(listed_ref[i, j] * BLK, BLK), BLK) for j in range(NB)]
        at = slice(i * BLK, (i + 1) * BLK)
        for h in range(H):
            lane = slice(h * head, (h + 1) * head)
            keys = jnp.concatenate([keyval[s, lane] for s in spans], axis=0)
            values = jnp.concatenate([keyval[s, width + h * head : width + (h + 1) * head] for s in spans], axis=0)
            scores = lax.dot_general(
                query[at, lane], keys, (((1,), (1,)), ((), ())), preferred_element_type=F32
            ) * (1.0 / math.sqrt(head))
            peak = jnp.max(scores, axis=1, keepdims=True)
            power = jnp.exp(scores - peak)
            prob = (power / jnp.sum(power, axis=1, keepdims=True)).astype(BF16)
            out_ref[at, lane] = (hnew_ref[at, lane] + dot(prob, values)).astype(BF16)


def apply_kernel(plan, ids_ref, landed_ref, memory_ref, after_ref, out_ref):
    stored = memory_ref.shape[0]
    piece = out_ref.shape[1]
    count = landed_ref.shape[0]
    me = lax.axis_index("rep")
    landed = landed_ref[...]
    lane = pl.ds(pl.multiple_of(me * piece, LANES), piece)
    step = min(256, stored)
    ids = ids_ref[...]
    for i in range(0, stored, step):
        hot = jnp.where(iota((step, count), 0) + i == ids, 1.0, 0.0).astype(BF16)
        total = dot(hot, landed)
        out_ref[i : i + step, :] = (memory_ref[i : i + step, lane].astype(F32) + total).astype(BF16)


def join_kernel(plan, *refs):
    me = lax.axis_index("rep")
    out_ref = refs[-1]
    for k in range(plan.reps):
        piece = refs[k].shape[1]
        out_ref[:, pl.ds(pl.multiple_of((me ^ k) * piece, LANES), piece)] = refs[k][...]


def swap(x, bit, reps):
    return lax.ppermute(x, "rep", [(i, i ^ bit) for i in range(reps)])


def spread(arrays, reps):
    held = [{0: x} for x in arrays]
    bit = reps // 2
    while bit:
        for parts in held:
            for k in list(parts):
                parts[k ^ bit] = swap(parts[k], bit, reps)
        bit //= 2
    return [[parts[k] for k in range(reps)] for parts in held]


def shards(
    memory,
    touch_owner,
    touch_row,
    touch_time,
    src_slot,
    dst_slot,
    event_time,
    neighbour_blocks,
    time_freq,
    time_phase,
    w_input,
    w_time,
    w_hidden,
    w_query,
    w_keyval,
):
    owners = lax.axis_size("shard")
    reps = lax.axis_size("rep")
    entries = touch_row.shape[0]
    events = event_time.shape[0]
    stored, width = memory.shape
    plan = Plan(owners, reps, entries)
    piece = width // reps
    run = functools.partial
    sds = jax.ShapeDtypeStruct

    owner = touch_owner.reshape(1, entries)
    request = call(
        run(request_kernel, plan), [sds((owners, LANES), I32)], [VMEM] * 2, 1 << 20, 1 << 14, "request", limit=8
    )(owner, touch_row.reshape(1, entries))[0]

    full_hidden, full_input, full_time, full_keyval, full_query = spread(
        [w_hidden, w_input, w_time, w_keyval, w_query], reps
    )

    asked = lax.all_to_all(request, "shard", split_axis=0, concat_axis=0, tiled=True)
    encode, cols, rows = call(
        run(index_kernel, plan),
        [sds((events, time_freq.shape[0]), BF16), sds((events, 8), F32), sds((8, events), I32)],
        [VMEM] * 7,
        1 << 22,
        1 << 18,
        "index",
        limit=8,
    )(
        owner,
        touch_time.reshape(1, entries),
        src_slot.reshape(1, events),
        dst_slot.reshape(1, events),
        event_time.reshape(1, events),
        time_freq.reshape(1, -1),
        time_phase.reshape(1, -1),
    )
    everyone = [x for x in spread([asked], reps)[0]]

    chunk = 4 * (plan.main + plan.tail)
    served = call(
        run(serve_kernel, plan),
        [sds((owners, chunk, width // 4), BF16)],
        [VMEM] * 2 + [ANY] * (2 * reps),
        2 * plan.rows * stored * width,
        2 * stored * width + 2 * plan.rows * width,
        "serve",
        limit=24,
    )(asked, memory, *full_hidden, *full_time)[0]
    returned = lax.all_to_all(served, "shard", split_axis=0, concat_axis=0, tiled=True)

    outgoing, hnew, hdst = call(
        run(gru_kernel, plan),
        [sds((owners * reps, plan.pad, piece), BF16), sds((events, width), F32), sds((events, width), BF16)],
        [VMEM] * 4 + [ANY] * (3 * reps),
        2 * events * width * 3 * width * 2,
        8 << 20,
        "gru",
        scratch=[
            pltpu.VMEM((events, 3 * width), F32),
            pltpu.VMEM((events, 3 * width), F32),
            pltpu.VMEM((events, width), F32),
        ]
        + [pltpu.VMEM((reps,) + x.shape, BF16) for x in (w_input, w_time, w_hidden)]
        + [pltpu.SemaphoreType.DMA((3, reps))],
        limit=48,
    )(returned, encode, cols, rows, *full_input, *full_time, *full_hidden)
    landed = lax.all_to_all(outgoing, ("shard", "rep"), split_axis=0, concat_axis=0, tiled=True)

    embed = call(
        run(attend_kernel, plan),
        [sds((events, width), BF16)],
        [SMEM] + [VMEM] * 2 + [ANY] * (2 * reps),
        2 * events * width * 3 * width,
        4 << 20,
        "attend",
        scratch=[pltpu.VMEM((events, width), BF16), pltpu.VMEM((events, 2 * width), BF16)]
        + [pltpu.VMEM((reps,) + x.shape, BF16) for x in (w_query, w_keyval)]
        + [pltpu.SemaphoreType.DMA((2, reps))],
        limit=48,
    )(neighbour_blocks, hnew, hdst, *full_query, *full_keyval)[0]

    me = lax.axis_index("rep")
    stack = jnp.stack([x[:, : plan.pad] for x in everyone])
    order = me ^ jnp.arange(reps, dtype=I32)
    ids = jnp.swapaxes(stack[order], 0, 1).reshape(1, owners * reps * plan.pad)
    quarter = call(
        run(apply_kernel, plan),
        [sds((stored, piece), BF16)],
        [VMEM] * 3 + [ANY],
        2 * stored * owners * reps * plan.pad * piece * 2,
        4 << 20,
        "apply",
        limit=32,
    )(ids, landed.reshape(owners * reps * plan.pad, piece), memory, embed)[0]
    new_memory = call(
        run(join_kernel, plan), [sds((stored, width), BF16)], [VMEM] * reps, 1 << 20, 2 << 20, "join", limit=8
    )(*spread([quarter], reps)[0])[0]
    return (embed, new_memory)


def solution(mesh):
    placed = (
        P("shard", None),
        P(("shard", "rep"), None),
        P(("shard", "rep")),
        P(("shard", "rep")),
        P(("shard", "rep")),
        P(("shard", "rep")),
        P(("shard", "rep")),
        P(("shard", "rep"), None),
        P(),
        P(),
        P(None, "rep"),
        P(None, "rep"),
        P(None, "rep"),
        P(None, "rep"),
        P(None, "rep"),
    )
    return jax.shard_map(
        shards,
        mesh=mesh,
        in_specs=placed,
        out_specs=(P(("shard", "rep"), None), P("shard", None)),
        check_vma=False,
    )
```

```python
import functools
import math

import jax
import jax.numpy as jnp
from jax import lax
from jax.experimental import pallas as pl
from jax.experimental.pallas import tpu as pltpu
from jax.sharding import PartitionSpec as P

H = 4
BLK = 128
NB = 2
LANES = 128
F32 = jnp.float32
BF16 = jnp.bfloat16
I32 = jnp.int32
VMEM = pl.BlockSpec(memory_space=pltpu.VMEM)
SMEM = pl.BlockSpec(memory_space=pltpu.SMEM)
ANY = pl.BlockSpec(memory_space=pl.ANY)


def iota(shape, dim):
    return lax.broadcasted_iota(I32, shape, dim)


def dot(a, b):
    return jnp.dot(a, b, preferred_element_type=F32)


def call(body, outs, specs, flops, bytes_, name, scratch=(), limit=60):
    return pl.pallas_call(
        body,
        out_shape=outs,
        in_specs=specs,
        out_specs=[VMEM] * len(outs),
        scratch_shapes=list(scratch),
        compiler_params=pltpu.CompilerParams(vmem_limit_bytes=limit << 20),
        cost_estimate=pl.CostEstimate(flops=flops, bytes_accessed=bytes_, transcendentals=0),
        name=name,
    )


class Plan:
    def __init__(self, owners, reps, entries):
        self.owners = owners
        self.reps = reps
        self.entries = entries
        self.cap = 2 * entries // owners + 2
        self.tail = self.cap % 16 if self.cap % 16 * 4 == 8 else 0
        self.main = self.cap - self.tail if self.tail else -(-self.cap // 16) * 16
        self.rows = self.owners * (self.main + self.tail)
        self.pad = -(-self.cap // 8) * 8


def rank_of(own_col, own_row, entries):
    earlier = (own_col == own_row) & (iota((entries, entries), 0) < iota((entries, entries), 1))
    later = (own_col == own_row) & (iota((entries, entries), 1) < iota((entries, entries), 0))
    place_row = jnp.sum(jnp.where(earlier, 1, 0), axis=0, keepdims=True)
    place_col = jnp.sum(jnp.where(later, 1, 0), axis=1, keepdims=True)
    return place_row, place_col


def to_col(row, size):
    eye = iota((size, size), 0) == iota((size, size), 1)
    return jnp.sum(jnp.where(eye, row, 0), axis=1, keepdims=True)


def request_kernel(plan, owner_ref, row_ref, out_ref):
    own_row = owner_ref[...]
    own_col = to_col(own_row, plan.entries)
    _, place_col = rank_of(own_col, own_row, plan.entries)
    row = row_ref[...]
    mine = iota((plan.owners, plan.entries), 0) == own_row
    spot = jnp.where(place_col == iota((plan.entries, LANES), 1), 1.0, 0.0).astype(BF16)
    high = jnp.where(mine, row >> 5, 0).astype(F32).astype(BF16)
    low = jnp.where(mine, row & 31, 0).astype(F32).astype(BF16)
    out_ref[...] = (dot(high, spot) * 32.0 + dot(low, spot)).astype(I32)


def index_kernel(plan, owner_ref, tick_ref, src_ref, dst_ref, stamp_ref, freq_ref, phase_ref, enc_ref, col_ref, row_ref):
    events = src_ref.shape[1]
    own_row = owner_ref[...]
    own_col = to_col(own_row, plan.entries)
    _, place = rank_of(own_col, own_row, plan.entries)
    tick = to_col(tick_ref[...], plan.entries)
    spot = own_col * plan.main + place
    if plan.tail:
        spare = plan.owners * plan.main + (place - plan.main) * plan.owners + own_col
        spot = jnp.where(place < plan.main, spot, spare)
    back = own_col * plan.pad + place
    isrc = iota((plan.entries, events), 0) == src_ref[...]
    idst = iota((plan.entries, events), 0) == dst_ref[...]

    def pick(mask, values):
        return jnp.sum(jnp.where(mask, values, 0), axis=0, keepdims=True)

    src_spot = pick(isrc, spot)
    dst_spot = pick(idst, spot)
    src_back = pick(isrc, back)
    span = stamp_ref[...] - pick(isrc, tick)
    zero = jnp.zeros((8 - 3, events), I32)
    rows = jnp.concatenate([src_spot, dst_spot, span, zero], axis=0)
    row_ref[...] = jnp.concatenate([src_back, jnp.zeros((7, events), I32)], axis=0)
    cols = rows.astype(F32).T
    col_ref[...] = cols
    enc_ref[...] = jnp.cos(cols[:, 2:3] * freq_ref[...] + phase_ref[...]).astype(BF16)


def tail_order(plan, forward):
    count = 4 * plan.tail * plan.owners
    across = 0 if forward else 1
    there = iota((count, count), across)
    here = iota((count, count), 1 - across)
    part = 4 * plan.tail
    owner, inner = there // part, there % part
    return jnp.where((inner * plan.owners + owner) == here, 1.0, 0.0).astype(BF16)


def serve_kernel(plan, asked_ref, memory_ref, *refs):
    out_ref, held, sem = refs[-3:]
    copy = pltpu.make_async_copy(memory_ref, held, sem)
    copy.start()
    stored, width = memory_ref.shape
    piece = width // 4
    asked = asked_ref[...].astype(F32)
    turned = asked.T
    blocks = [
        jnp.where(turned[: plan.main, s : s + 1].astype(I32) == iota((plan.main, stored), 1), 1.0, 0.0)
        for s in range(plan.owners)
    ]
    for i in range(plan.tail):
        spare = asked_ref[:, plan.main + i : plan.main + i + 1]
        blocks.append(jnp.where(spare == iota((plan.owners, stored), 1), 1.0, 0.0))
    hot = jnp.concatenate(blocks, axis=0).astype(BF16)
    copy.wait()
    rows = dot(hot, held[...])
    main = plan.main
    for s in range(plan.owners):
        for c in range(4):
            out_ref[s, c * main : (c + 1) * main, :] = rows[
                s * main : (s + 1) * main, c * piece : (c + 1) * piece
            ].astype(BF16)
    if plan.tail:
        spare = rows[plan.owners * main :]
        stack = jnp.concatenate([spare[:, c * piece : (c + 1) * piece] for c in range(4)], axis=0)
        ordered = dot(tail_order(plan, True), stack.astype(BF16))
        for s in range(plan.owners):
            out_ref[s, 4 * main : 4 * (main + plan.tail), :] = ordered[
                s * 4 * plan.tail : (s + 1) * 4 * plan.tail
            ].astype(BF16)


def table_of(plan, ret_ref):
    main = plan.main
    pieces = [
        jnp.concatenate([ret_ref[s, c * main : (c + 1) * main, :] for s in range(plan.owners)], axis=0)
        for c in range(4)
    ]
    table = jnp.concatenate(pieces, axis=1)
    if plan.tail:
        stack = jnp.concatenate(
            [ret_ref[s, 4 * main : 4 * (main + plan.tail), :].astype(F32) for s in range(plan.owners)], axis=0
        )
        ordered = dot(tail_order(plan, False), stack.astype(BF16))
        count = plan.tail * plan.owners
        spare = jnp.concatenate([ordered[c * count : (c + 1) * count] for c in range(4)], axis=1)
        table = jnp.concatenate([table, spare.astype(BF16)], axis=0)
    return table


def fetch(groups, sems):
    copies = []
    for g, (parts, buffer) in enumerate(groups):
        row = [pltpu.make_async_copy(part, buffer.at[k], sems.at[g, k]) for k, part in enumerate(parts)]
        for copy in row:
            copy.start()
        copies.append(row)
    return copies


def gru_kernel(plan, ret_ref, enc_ref, col_ref, row_ref, *refs):
    reps = plan.reps
    parts_in, parts_time, parts_hid = refs[:reps], refs[reps : 2 * reps], refs[2 * reps : 3 * reps]
    out_ref, hnew_ref, hdst_ref, gin, ghid, delta, w_in, w_time, w_hid, sems = refs[3 * reps :]
    copies = fetch([(parts_in, w_in), (parts_time, w_time), (parts_hid, w_hid)], sems)
    me = lax.axis_index("rep")
    events, width = hnew_ref.shape
    piece = width // reps
    cols = col_ref[...].astype(I32)
    spots = iota((events, plan.rows), 1)
    table = table_of(plan, ret_ref)
    hsrc = dot(jnp.where(cols[:, 0:1] == spots, 1.0, 0.0).astype(BF16), table)
    source = hsrc.astype(BF16)
    target = dot(jnp.where(cols[:, 1:2] == spots, 1.0, 0.0).astype(BF16), table).astype(BF16)
    hdst_ref[...] = target
    enc = enc_ref[...]
    part = w_in.shape[2]
    for k in range(reps):
        for row in copies:
            row[k].wait()
        at = pl.ds(pl.multiple_of((me ^ k) * part, LANES), part)
        gin[:, at] = dot(target, w_in[k]) + dot(enc, w_time[k])
        ghid[:, at] = dot(source, w_hid[k])
    step = 64
    for i in range(0, events, step):
        at = slice(i, i + step)
        reset = 0.5 * jnp.tanh(0.5 * (gin[at, :width] + ghid[at, :width])) + 0.5
        update = 0.5 * jnp.tanh(0.5 * (gin[at, width : 2 * width] + ghid[at, width : 2 * width])) + 0.5
        fresh = jnp.tanh(gin[at, 2 * width :] + reset * ghid[at, 2 * width :])
        hold = hsrc[at]
        new = (1.0 - update) * fresh + update * hold
        hnew_ref[at, :] = new
        delta[at, :] = new - hold
    change = delta[...]
    high = change.astype(BF16)
    low = (change - high.astype(F32)).astype(BF16)
    slots = plan.owners * plan.pad
    hits = jnp.where(row_ref[0:1, :] == iota((slots, events), 0), 1.0, 0.0)
    counts = jnp.maximum(jnp.sum(hits, axis=1, keepdims=True), 1.0)
    hits = hits.astype(BF16)
    mean = (dot(hits, high) + dot(hits, low)) / counts
    for o in range(plan.owners):
        for q in range(reps):
            out_ref[o * reps + q] = mean[o * plan.pad : (o + 1) * plan.pad, q * piece : (q + 1) * piece].astype(BF16)


def attend_kernel(plan, listed_ref, hnew_ref, hdst_ref, *refs):
    reps = plan.reps
    parts_query, parts_keyval = refs[:reps], refs[reps : 2 * reps]
    out_ref, query, keyval, w_query, w_keyval, sems = refs[2 * reps :]
    copies = fetch([(parts_query, w_query), (parts_keyval, w_keyval)], sems)
    me = lax.axis_index("rep")
    events, width = hnew_ref.shape
    head = width // H
    hround = hnew_ref[...].astype(BF16)
    target = hdst_ref[...]
    for k in range(reps):
        for row in copies:
            row[k].wait()
        part = w_query.shape[2]
        query[:, pl.ds(pl.multiple_of((me ^ k) * part, LANES), part)] = dot(hround, w_query[k]).astype(BF16)
        part = w_keyval.shape[2]
        keyval[:, pl.ds(pl.multiple_of((me ^ k) * part, LANES), part)] = dot(target, w_keyval[k]).astype(BF16)
    for i in range(events // BLK):
        spans = [pl.ds(pl.multiple_of(listed_ref[i, j] * BLK, BLK), BLK) for j in range(NB)]
        at = slice(i * BLK, (i + 1) * BLK)
        for h in range(H):
            lane = slice(h * head, (h + 1) * head)
            keys = jnp.concatenate([keyval[s, lane] for s in spans], axis=0)
            values = jnp.concatenate([keyval[s, width + h * head : width + (h + 1) * head] for s in spans], axis=0)
            scores = lax.dot_general(
                query[at, lane], keys, (((1,), (1,)), ((), ())), preferred_element_type=F32
            ) * (1.0 / math.sqrt(head))
            peak = jnp.max(scores, axis=1, keepdims=True)
            power = jnp.exp(scores - peak)
            prob = (power / jnp.sum(power, axis=1, keepdims=True)).astype(BF16)
            out_ref[at, lane] = (hnew_ref[at, lane] + dot(prob, values)).astype(BF16)


def apply_kernel(plan, ids_ref, landed_ref, memory_ref, after_ref, out_ref, held, sem):
    stored = memory_ref.shape[0]
    piece = out_ref.shape[1]
    count = landed_ref.shape[0]
    me = lax.axis_index("rep")
    lane = pl.ds(pl.multiple_of(me * piece, LANES), piece)
    copy = pltpu.make_async_copy(memory_ref.at[:, lane], held, sem)
    copy.start()
    landed = landed_ref[...]
    step = min(256, stored)
    ids = ids_ref[...]
    for i in range(0, stored, step):
        hot = jnp.where(iota((step, count), 0) + i == ids, 1.0, 0.0).astype(BF16)
        total = dot(hot, landed)
        if i == 0:
            copy.wait()
        out_ref[i : i + step, :] = (held[i : i + step, :].astype(F32) + total).astype(BF16)


def join_kernel(plan, *refs):
    me = lax.axis_index("rep")
    out_ref = refs[-1]
    for k in range(plan.reps):
        piece = refs[k].shape[1]
        out_ref[:, pl.ds(pl.multiple_of((me ^ k) * piece, LANES), piece)] = refs[k][...]


def swap(x, bit, reps):
    return lax.ppermute(x, "rep", [(i, i ^ bit) for i in range(reps)])


def spread(arrays, reps):
    held = [{0: x} for x in arrays]
    bit = reps // 2
    while bit:
        for parts in held:
            for k in list(parts):
                parts[k ^ bit] = swap(parts[k], bit, reps)
        bit //= 2
    return [[parts[k] for k in range(reps)] for parts in held]


def shards(
    memory,
    touch_owner,
    touch_row,
    touch_time,
    src_slot,
    dst_slot,
    event_time,
    neighbour_blocks,
    time_freq,
    time_phase,
    w_input,
    w_time,
    w_hidden,
    w_query,
    w_keyval,
):
    owners = lax.axis_size("shard")
    reps = lax.axis_size("rep")
    entries = touch_row.shape[0]
    events = event_time.shape[0]
    stored, width = memory.shape
    plan = Plan(owners, reps, entries)
    piece = width // reps
    run = functools.partial
    sds = jax.ShapeDtypeStruct

    owner = touch_owner.reshape(1, entries)
    request = call(
        run(request_kernel, plan), [sds((owners, LANES), I32)], [VMEM] * 2, 1 << 20, 1 << 14, "request", limit=8
    )(owner, touch_row.reshape(1, entries))[0]

    full_hidden, full_input, full_time, full_keyval, full_query = spread(
        [w_hidden, w_input, w_time, w_keyval, w_query], reps
    )

    asked = lax.all_to_all(request, "shard", split_axis=0, concat_axis=0, tiled=True)
    encode, cols, rows = call(
        run(index_kernel, plan),
        [sds((events, time_freq.shape[0]), BF16), sds((events, 8), F32), sds((8, events), I32)],
        [VMEM] * 7,
        1 << 22,
        1 << 18,
        "index",
        limit=8,
    )(
        owner,
        touch_time.reshape(1, entries),
        src_slot.reshape(1, events),
        dst_slot.reshape(1, events),
        event_time.reshape(1, events),
        time_freq.reshape(1, -1),
        time_phase.reshape(1, -1),
    )
    everyone = [x for x in spread([asked], reps)[0]]

    chunk = 4 * (plan.main + plan.tail)
    served = call(
        run(serve_kernel, plan),
        [sds((owners, chunk, width // 4), BF16)],
        [VMEM] + [ANY] * 3,
        2 * plan.rows * stored * width,
        2 * stored * width + 2 * plan.rows * width,
        "serve",
        scratch=[pltpu.VMEM(memory.shape, BF16), pltpu.SemaphoreType.DMA],
    )(asked, memory, full_hidden[reps // 2], full_time[reps // 2])[0]
    returned = lax.all_to_all(served, "shard", split_axis=0, concat_axis=0, tiled=True)

    outgoing, hnew, hdst = call(
        run(gru_kernel, plan),
        [sds((owners * reps, plan.pad, piece), BF16), sds((events, width), F32), sds((events, width), BF16)],
        [VMEM] * 4 + [ANY] * (3 * reps),
        2 * events * width * 3 * width * 2,
        8 << 20,
        "gru",
        scratch=[
            pltpu.VMEM((events, 3 * width), F32),
            pltpu.VMEM((events, 3 * width), F32),
            pltpu.VMEM((events, width), F32),
        ]
        + [pltpu.VMEM((reps,) + x.shape, BF16) for x in (w_input, w_time, w_hidden)]
        + [pltpu.SemaphoreType.DMA((3, reps))],
    )(returned, encode, cols, rows, *full_input, *full_time, *full_hidden)
    landed = lax.all_to_all(outgoing, ("shard", "rep"), split_axis=0, concat_axis=0, tiled=True)

    embed = call(
        run(attend_kernel, plan),
        [sds((events, width), BF16)],
        [SMEM] + [VMEM] * 2 + [ANY] * (2 * reps),
        2 * events * width * 3 * width,
        4 << 20,
        "attend",
        scratch=[pltpu.VMEM((events, width), BF16), pltpu.VMEM((events, 2 * width), BF16)]
        + [pltpu.VMEM((reps,) + x.shape, BF16) for x in (w_query, w_keyval)]
        + [pltpu.SemaphoreType.DMA((2, reps))],
    )(neighbour_blocks, hnew, hdst, *full_query, *full_keyval)[0]

    me = lax.axis_index("rep")
    stack = jnp.stack([x[:, : plan.pad] for x in everyone])
    order = me ^ jnp.arange(reps, dtype=I32)
    ids = jnp.swapaxes(stack[order], 0, 1).reshape(1, owners * reps * plan.pad)
    quarter = call(
        run(apply_kernel, plan),
        [sds((stored, piece), BF16)],
        [VMEM] * 2 + [ANY] * 2,
        2 * stored * owners * reps * plan.pad * piece * 2,
        4 << 20,
        "apply",
        scratch=[pltpu.VMEM((stored, piece), BF16), pltpu.SemaphoreType.DMA],
    )(ids, landed.reshape(owners * reps * plan.pad, piece), memory, embed)[0]
    new_memory = call(
        run(join_kernel, plan), [sds((stored, width), BF16)], [VMEM] * reps, 1 << 20, 2 << 20, "join", limit=8
    )(*spread([quarter], reps)[0])[0]
    return (embed, new_memory)


def solution(mesh):
    placed = (
        P("shard", None),
        P(("shard", "rep"), None),
        P(("shard", "rep")),
        P(("shard", "rep")),
        P(("shard", "rep")),
        P(("shard", "rep")),
        P(("shard", "rep")),
        P(("shard", "rep"), None),
        P(),
        P(),
        P(None, "rep"),
        P(None, "rep"),
        P(None, "rep"),
        P(None, "rep"),
        P(None, "rep"),
    )
    return jax.shard_map(
        shards,
        mesh=mesh,
        in_specs=placed,
        out_specs=(P(("shard", "rep"), None), P("shard", None)),
        check_vma=False,
    )
```

```python
import functools
import math

import jax
import jax.numpy as jnp
from jax import lax
from jax.experimental import pallas as pl
from jax.experimental.pallas import tpu as pltpu
from jax.sharding import PartitionSpec as P

H = 4
BLK = 128
NB = 2
LANES = 128
F32 = jnp.float32
BF16 = jnp.bfloat16
I32 = jnp.int32
VMEM = pl.BlockSpec(memory_space=pltpu.VMEM)
SMEM = pl.BlockSpec(memory_space=pltpu.SMEM)
ANY = pl.BlockSpec(memory_space=pl.ANY)


def iota(shape, dim):
    return lax.broadcasted_iota(I32, shape, dim)


def dot(a, b):
    return jnp.dot(a, b, preferred_element_type=F32)


def call(body, outs, specs, flops, bytes_, name, scratch=(), limit=8):
    return pl.pallas_call(
        body,
        out_shape=outs,
        in_specs=specs,
        out_specs=[VMEM] * len(outs),
        scratch_shapes=list(scratch),
        compiler_params=pltpu.CompilerParams(vmem_limit_bytes=limit << 20),
        cost_estimate=pl.CostEstimate(flops=flops, bytes_accessed=bytes_, transcendentals=0),
        name=name,
    )


class Plan:
    def __init__(self, owners, reps, entries):
        self.owners = owners
        self.reps = reps
        self.entries = entries
        self.cap = 2 * entries // owners + 2
        self.tail = self.cap % 16 if self.cap % 16 * 4 == 8 else 0
        self.main = self.cap - self.tail if self.tail else -(-self.cap // 16) * 16
        self.rows = self.owners * (self.main + self.tail)
        self.pad = -(-self.cap // 8) * 8


def rank_of(own_col, own_row, entries):
    earlier = (own_col == own_row) & (iota((entries, entries), 0) < iota((entries, entries), 1))
    later = (own_col == own_row) & (iota((entries, entries), 1) < iota((entries, entries), 0))
    place_row = jnp.sum(jnp.where(earlier, 1, 0), axis=0, keepdims=True)
    place_col = jnp.sum(jnp.where(later, 1, 0), axis=1, keepdims=True)
    return place_row, place_col


def to_col(row, size):
    eye = iota((size, size), 0) == iota((size, size), 1)
    return jnp.sum(jnp.where(eye, row, 0), axis=1, keepdims=True)


def request_kernel(plan, owner_ref, row_ref, out_ref):
    own_row = owner_ref[...]
    own_col = to_col(own_row, plan.entries)
    _, place_col = rank_of(own_col, own_row, plan.entries)
    row = row_ref[...]
    mine = iota((plan.owners, plan.entries), 0) == own_row
    spot = jnp.where(place_col == iota((plan.entries, LANES), 1), 1.0, 0.0).astype(BF16)
    high = jnp.where(mine, row >> 5, 0).astype(F32).astype(BF16)
    low = jnp.where(mine, row & 31, 0).astype(F32).astype(BF16)
    out_ref[...] = (dot(high, spot) * 32.0 + dot(low, spot)).astype(I32)


def index_kernel(plan, owner_ref, packed_ref, freq_ref, phase_ref, enc_ref, col_ref, row_ref):
    events = enc_ref.shape[0]
    ends = [plan.entries + i * events for i in range(4)]
    tick_row = packed_ref[:, : ends[0]]
    src_row, dst_row, stamp_row = (packed_ref[:, a : a + events] for a in ends[:3])
    own_row = owner_ref[...]
    own_col = to_col(own_row, plan.entries)
    _, place = rank_of(own_col, own_row, plan.entries)
    tick = to_col(tick_row, plan.entries)
    spot = own_col * plan.main + place
    if plan.tail:
        spare = plan.owners * plan.main + (place - plan.main) * plan.owners + own_col
        spot = jnp.where(place < plan.main, spot, spare)
    back = own_col * plan.pad + place
    isrc = iota((plan.entries, events), 0) == src_row
    idst = iota((plan.entries, events), 0) == dst_row

    def pick(mask, values):
        return jnp.sum(jnp.where(mask, values, 0), axis=0, keepdims=True)

    src_spot = pick(isrc, spot)
    dst_spot = pick(idst, spot)
    src_back = pick(isrc, back)
    span = stamp_row - pick(isrc, tick)
    zero = jnp.zeros((8 - 3, events), I32)
    rows = jnp.concatenate([src_spot, dst_spot, span, zero], axis=0)
    row_ref[...] = jnp.concatenate([src_back, jnp.zeros((7, events), I32)], axis=0)
    cols = rows.astype(F32).T
    col_ref[...] = cols
    enc_ref[...] = jnp.cos(cols[:, 2:3] * freq_ref[...] + phase_ref[...]).astype(BF16)


def tail_order(plan, forward):
    count = 4 * plan.tail * plan.owners
    across = 0 if forward else 1
    there = iota((count, count), across)
    here = iota((count, count), 1 - across)
    part = 4 * plan.tail
    owner, inner = there // part, there % part
    return jnp.where((inner * plan.owners + owner) == here, 1.0, 0.0).astype(BF16)


def serve_kernel(plan, asked_ref, memory_ref, out_ref):
    stored, width = memory_ref.shape
    piece = width // 4
    asked = asked_ref[...].astype(F32)
    turned = asked.T
    blocks = [
        jnp.where(turned[: plan.main, s : s + 1].astype(I32) == iota((plan.main, stored), 1), 1.0, 0.0)
        for s in range(plan.owners)
    ]
    for i in range(plan.tail):
        spare = asked_ref[:, plan.main + i : plan.main + i + 1]
        blocks.append(jnp.where(spare == iota((plan.owners, stored), 1), 1.0, 0.0))
    hot = jnp.concatenate(blocks, axis=0).astype(BF16)
    rows = dot(hot, memory_ref[...])
    main = plan.main
    for s in range(plan.owners):
        for c in range(4):
            out_ref[s, c * main : (c + 1) * main, :] = rows[
                s * main : (s + 1) * main, c * piece : (c + 1) * piece
            ].astype(BF16)
    if plan.tail:
        spare = rows[plan.owners * main :]
        stack = jnp.concatenate([spare[:, c * piece : (c + 1) * piece] for c in range(4)], axis=0)
        ordered = dot(tail_order(plan, True), stack.astype(BF16))
        for s in range(plan.owners):
            out_ref[s, 4 * main : 4 * (main + plan.tail), :] = ordered[
                s * 4 * plan.tail : (s + 1) * 4 * plan.tail
            ].astype(BF16)


def table_of(plan, ret_ref):
    main = plan.main
    pieces = [
        jnp.concatenate([ret_ref[s, c * main : (c + 1) * main, :] for s in range(plan.owners)], axis=0)
        for c in range(4)
    ]
    table = jnp.concatenate(pieces, axis=1)
    if plan.tail:
        stack = jnp.concatenate(
            [ret_ref[s, 4 * main : 4 * (main + plan.tail), :].astype(F32) for s in range(plan.owners)], axis=0
        )
        ordered = dot(tail_order(plan, False), stack.astype(BF16))
        count = plan.tail * plan.owners
        spare = jnp.concatenate([ordered[c * count : (c + 1) * count] for c in range(4)], axis=1)
        table = jnp.concatenate([table, spare.astype(BF16)], axis=0)
    return table


def gru_kernel(plan, ret_ref, enc_ref, col_ref, row_ref, *refs):
    reps = plan.reps
    w_in, w_hid, w_time = refs[:reps], refs[reps : 2 * reps], refs[2 * reps : 3 * reps]
    out_ref, hnew_ref, hdst_ref, gin, ghid, delta = refs[3 * reps :]
    me = lax.axis_index("rep")
    events, width = hnew_ref.shape
    piece = width // reps
    cols = col_ref[...].astype(I32)
    spots = iota((events, plan.rows), 1)
    table = table_of(plan, ret_ref)
    hsrc = dot(jnp.where(cols[:, 0:1] == spots, 1.0, 0.0).astype(BF16), table)
    source = hsrc.astype(BF16)
    target = dot(jnp.where(cols[:, 1:2] == spots, 1.0, 0.0).astype(BF16), table).astype(BF16)
    hdst_ref[...] = target
    enc = enc_ref[...]
    part = w_in[0].shape[1]
    for k in range(reps):
        at = pl.ds(pl.multiple_of((me ^ k) * part, LANES), part)
        gin[:, at] = dot(target, w_in[k][...]) + dot(enc, w_time[k][...])
        ghid[:, at] = dot(source, w_hid[k][...])
    step = 64
    for i in range(0, events, step):
        at = slice(i, i + step)
        reset = 0.5 * jnp.tanh(0.5 * (gin[at, :width] + ghid[at, :width])) + 0.5
        update = 0.5 * jnp.tanh(0.5 * (gin[at, width : 2 * width] + ghid[at, width : 2 * width])) + 0.5
        fresh = jnp.tanh(gin[at, 2 * width :] + reset * ghid[at, 2 * width :])
        hold = hsrc[at]
        new = (1.0 - update) * fresh + update * hold
        hnew_ref[at, :] = new
        delta[at, :] = new - hold
    change = delta[...]
    high = change.astype(BF16)
    low = (change - high.astype(F32)).astype(BF16)
    slots = plan.owners * plan.pad
    hits = jnp.where(row_ref[0:1, :] == iota((slots, events), 0), 1.0, 0.0)
    counts = jnp.maximum(jnp.sum(hits, axis=1, keepdims=True), 1.0)
    hits = hits.astype(BF16)
    mean = (dot(hits, high) + dot(hits, low)) / counts
    for o in range(plan.owners):
        for q in range(reps):
            out_ref[o * reps + q] = mean[o * plan.pad : (o + 1) * plan.pad, q * piece : (q + 1) * piece].astype(BF16)


def attend_kernel(plan, listed_ref, hnew_ref, hdst_ref, memory_ref, *refs):
    reps = plan.reps
    w_query, w_keyval = refs[:reps], refs[reps : 2 * reps]
    out_ref, quarter_ref, query, keyval = refs[2 * reps :]
    me = lax.axis_index("rep")
    events, width = hnew_ref.shape
    piece = quarter_ref.shape[1]
    quarter_ref[...] = memory_ref[:, pl.ds(pl.multiple_of(me * piece, LANES), piece)]
    head = width // H
    hround = hnew_ref[...].astype(BF16)
    target = hdst_ref[...]
    first = width // reps
    for k in range(reps):
        query[:, pl.ds(pl.multiple_of((me ^ k) * first, LANES), first)] = dot(hround, w_query[k][...]).astype(BF16)
        at = pl.ds(pl.multiple_of((me ^ k) * 2 * first, LANES), 2 * first)
        keyval[:, at] = dot(target, w_keyval[k][...]).astype(BF16)
    for i in range(events // BLK):
        spans = [pl.ds(pl.multiple_of(listed_ref[i, j] * BLK, BLK), BLK) for j in range(NB)]
        at = slice(i * BLK, (i + 1) * BLK)
        for h in range(H):
            lane = slice(h * head, (h + 1) * head)
            keys = jnp.concatenate([keyval[s, lane] for s in spans], axis=0)
            values = jnp.concatenate([keyval[s, width + h * head : width + (h + 1) * head] for s in spans], axis=0)
            scores = lax.dot_general(
                query[at, lane], keys, (((1,), (1,)), ((), ())), preferred_element_type=F32
            ) * (1.0 / math.sqrt(head))
            peak = jnp.max(scores, axis=1, keepdims=True)
            power = jnp.exp(scores - peak)
            prob = (power / jnp.sum(power, axis=1, keepdims=True)).astype(BF16)
            out_ref[at, lane] = (hnew_ref[at, lane] + dot(prob, values)).astype(BF16)


def apply_kernel(plan, ids_ref, landed_ref, part_ref, out_ref):
    stored = part_ref.shape[0]
    count = landed_ref.shape[0]
    landed = landed_ref[...]
    step = min(256, stored)
    ids = ids_ref[...]
    for i in range(0, stored, step):
        hot = jnp.where(iota((step, count), 0) + i == ids, 1.0, 0.0).astype(BF16)
        total = dot(hot, landed)
        out_ref[i : i + step, :] = (part_ref[i : i + step, :].astype(F32) + total).astype(BF16)


def join_kernel(plan, *refs):
    me = lax.axis_index("rep")
    out_ref = refs[-1]
    for k in range(plan.reps):
        piece = refs[k].shape[1]
        out_ref[:, pl.ds(pl.multiple_of((me ^ k) * piece, LANES), piece)] = refs[k][...]


def swap(x, bit, reps):
    return lax.ppermute(x, "rep", [(i, i ^ bit) for i in range(reps)])


def spread(arrays, reps):
    held = [{0: x} for x in arrays]
    bit = reps // 2
    while bit:
        for parts in held:
            for k in list(parts):
                parts[k ^ bit] = swap(parts[k], bit, reps)
        bit //= 2
    return [[parts[k] for k in range(reps)] for parts in held]


def shards(
    memory,
    touch_owner,
    touch_row,
    touch_time,
    src_slot,
    dst_slot,
    event_time,
    neighbour_blocks,
    time_freq,
    time_phase,
    w_input,
    w_time,
    w_hidden,
    w_query,
    w_keyval,
):
    owners = lax.axis_size("shard")
    reps = lax.axis_size("rep")
    entries = touch_row.shape[0]
    events = event_time.shape[0]
    stored, width = memory.shape
    plan = Plan(owners, reps, entries)
    piece = width // reps
    run = functools.partial
    sds = jax.ShapeDtypeStruct

    owner = touch_owner.reshape(1, entries)
    request = call(
        run(request_kernel, plan), [sds((owners, LANES), I32)], [VMEM] * 2, 1 << 20, 1 << 14, "request", limit=8
    )(owner, touch_row.reshape(1, entries))[0]

    full_time, full_hidden, full_input, full_keyval, full_query = spread(
        [w_time, w_hidden, w_input, w_keyval, w_query], reps
    )

    asked = lax.all_to_all(request, "shard", split_axis=0, concat_axis=0, tiled=True)
    encode, cols, rows = call(
        run(index_kernel, plan),
        [sds((events, time_freq.shape[0]), BF16), sds((events, 8), F32), sds((8, events), I32)],
        [VMEM] * 4,
        8 << 30,
        1 << 18,
        "index",
        limit=8,
    )(
        owner,
        jnp.concatenate([touch_time, src_slot, dst_slot, event_time]).reshape(1, -1),
        time_freq.reshape(1, -1),
        time_phase.reshape(1, -1),
    )
    everyone = [x for x in spread([asked], reps)[0]]

    chunk = 4 * (plan.main + plan.tail)
    served = call(
        run(serve_kernel, plan),
        [sds((owners, chunk, width // 4), BF16)],
        [VMEM] * 2,
        2 * plan.rows * stored * width,
        2 * stored * width + 2 * plan.rows * width,
        "serve",
        limit=12,
    )(asked, memory)[0]
    returned = lax.all_to_all(served, "shard", split_axis=0, concat_axis=0, tiled=True)

    outgoing, hnew, hdst = call(
        run(gru_kernel, plan),
        [sds((owners * reps, plan.pad, piece), BF16), sds((events, width), F32), sds((events, width), BF16)],
        [VMEM] * (4 + 3 * reps),
        2 * events * width * 3 * width * 2,
        8 << 20,
        "gru",
        scratch=[
            pltpu.VMEM((events, 3 * width), F32),
            pltpu.VMEM((events, 3 * width), F32),
            pltpu.VMEM((events, width), F32),
        ],
        limit=24,
    )(returned, encode, cols, rows, *full_input, *full_hidden, *full_time)
    landed = lax.all_to_all(outgoing, ("shard", "rep"), split_axis=0, concat_axis=0, tiled=True)

    embed, part = call(
        run(attend_kernel, plan),
        [sds((events, width), BF16), sds((stored, piece), BF16)],
        [SMEM] + [VMEM] * (3 + 2 * reps),
        2 * events * width * 3 * width,
        4 << 20,
        "attend",
        scratch=[
            pltpu.VMEM((events, width), BF16),
            pltpu.VMEM((events, 2 * width), BF16),
        ],
        limit=12,
    )(neighbour_blocks, hnew, hdst, memory, *full_query, *full_keyval)

    me = lax.axis_index("rep")
    stack = jnp.stack([x[:, : plan.pad] for x in everyone])
    order = me ^ jnp.arange(reps, dtype=I32)
    ids = jnp.swapaxes(stack[order], 0, 1).reshape(1, owners * reps * plan.pad)
    quarter = call(
        run(apply_kernel, plan),
        [sds((stored, piece), BF16)],
        [VMEM] * 3,
        2 * stored * owners * reps * plan.pad * piece * 2,
        4 << 20,
        "apply",
        limit=16,
    )(ids, landed.reshape(owners * reps * plan.pad, piece), part)[0]
    new_memory = call(
        run(join_kernel, plan), [sds((stored, width), BF16)], [VMEM] * reps, 1 << 20, 2 << 20, "join", limit=8
    )(*spread([quarter], reps)[0])[0]
    return (embed, new_memory)


def solution(mesh):
    placed = (
        P("shard", None),
        P(("shard", "rep"), None),
        P(("shard", "rep")),
        P(("shard", "rep")),
        P(("shard", "rep")),
        P(("shard", "rep")),
        P(("shard", "rep")),
        P(("shard", "rep"), None),
        P(),
        P(),
        P(None, "rep"),
        P(None, "rep"),
        P(None, "rep"),
        P(None, "rep"),
        P(None, "rep"),
    )
    return jax.shard_map(
        shards,
        mesh=mesh,
        in_specs=placed,
        out_specs=(P(("shard", "rep"), None), P("shard", None)),
        check_vma=False,
    )
```

```python
import functools
import math

import jax
import jax.numpy as jnp
from jax import lax
from jax.experimental import pallas as pl
from jax.experimental.pallas import tpu as pltpu
from jax.sharding import PartitionSpec as P

H = 4
BLK = 128
NB = 2
LANES = 128
F32 = jnp.float32
BF16 = jnp.bfloat16
I32 = jnp.int32
VMEM = pl.BlockSpec(memory_space=pltpu.VMEM)
SMEM = pl.BlockSpec(memory_space=pltpu.SMEM)
ANY = pl.BlockSpec(memory_space=pl.ANY)


def iota(shape, dim):
    return lax.broadcasted_iota(I32, shape, dim)


def dot(a, b):
    return jnp.dot(a, b, preferred_element_type=F32)


def call(body, outs, specs, flops, bytes_, name, scratch=(), limit=8):
    return pl.pallas_call(
        body,
        out_shape=outs,
        in_specs=specs,
        out_specs=[VMEM] * len(outs),
        scratch_shapes=list(scratch),
        compiler_params=pltpu.CompilerParams(vmem_limit_bytes=limit << 20),
        cost_estimate=pl.CostEstimate(flops=flops, bytes_accessed=bytes_, transcendentals=0),
        name=name,
    )


class Plan:
    def __init__(self, owners, reps, entries):
        self.owners = owners
        self.reps = reps
        self.entries = entries
        self.cap = 2 * entries // owners + 2
        self.tail = self.cap % 16 if self.cap % 16 * 4 == 8 else 0
        self.main = self.cap - self.tail if self.tail else -(-self.cap // 16) * 16
        self.rows = self.owners * (self.main + self.tail)
        self.pad = -(-self.cap // 8) * 8
        self.pairs = owners <= 8 and owners & (owners - 1) == 0


def rank_of(own_col, own_row, entries):
    earlier = (own_col == own_row) & (iota((entries, entries), 0) < iota((entries, entries), 1))
    later = (own_col == own_row) & (iota((entries, entries), 1) < iota((entries, entries), 0))
    place_row = jnp.sum(jnp.where(earlier, 1, 0), axis=0, keepdims=True)
    place_col = jnp.sum(jnp.where(later, 1, 0), axis=1, keepdims=True)
    return place_row, place_col


def to_col(row, size):
    eye = iota((size, size), 0) == iota((size, size), 1)
    return jnp.sum(jnp.where(eye, row, 0), axis=1, keepdims=True)


def request_kernel(plan, owner_ref, row_ref, out_ref):
    own_row = owner_ref[...]
    own_col = to_col(own_row, plan.entries)
    _, place_col = rank_of(own_col, own_row, plan.entries)
    row = row_ref[...]
    mine = iota((plan.owners, plan.entries), 0) == own_row
    spot = jnp.where(place_col == iota((plan.entries, LANES), 1), 1.0, 0.0).astype(BF16)
    high = jnp.where(mine, row >> 5, 0).astype(F32).astype(BF16)
    low = jnp.where(mine, row & 31, 0).astype(F32).astype(BF16)
    out_ref[...] = (dot(high, spot) * 32.0 + dot(low, spot)).astype(I32)


def index_kernel(plan, owner_ref, packed_ref, freq_ref, phase_ref, enc_ref, col_ref, row_ref):
    events = enc_ref.shape[0]
    ends = [plan.entries + i * events for i in range(4)]
    tick_row = packed_ref[:, : ends[0]]
    src_row, dst_row, stamp_row = (packed_ref[:, a : a + events] for a in ends[:3])
    own_row = owner_ref[...]
    own_col = to_col(own_row, plan.entries)
    _, place = rank_of(own_col, own_row, plan.entries)
    tick = to_col(tick_row, plan.entries)
    slot = own_col ^ lax.axis_index("shard") if plan.pairs else own_col
    spot = slot * plan.main + place
    if plan.tail:
        spare = plan.owners * plan.main + (place - plan.main) * plan.owners + slot
        spot = jnp.where(place < plan.main, spot, spare)
    back = own_col * plan.pad + place
    isrc = iota((plan.entries, events), 0) == src_row
    idst = iota((plan.entries, events), 0) == dst_row

    def pick(mask, values):
        return jnp.sum(jnp.where(mask, values, 0), axis=0, keepdims=True)

    src_spot = pick(isrc, spot)
    dst_spot = pick(idst, spot)
    src_back = pick(isrc, back)
    span = stamp_row - pick(isrc, tick)
    zero = jnp.zeros((8 - 3, events), I32)
    rows = jnp.concatenate([src_spot, dst_spot, span, zero], axis=0)
    row_ref[...] = jnp.concatenate([src_back, jnp.zeros((7, events), I32)], axis=0)
    cols = rows.astype(F32).T
    col_ref[...] = cols
    enc_ref[...] = jnp.cos(cols[:, 2:3] * freq_ref[...] + phase_ref[...]).astype(BF16)


def tail_order(plan, forward):
    count = 4 * plan.tail * plan.owners
    across = 0 if forward else 1
    there = iota((count, count), across)
    here = iota((count, count), 1 - across)
    part = 4 * plan.tail
    owner, inner = there // part, there % part
    return jnp.where((inner * plan.owners + owner) == here, 1.0, 0.0).astype(BF16)


def at_slot(refs, s):
    return refs[s] if len(refs) > 1 else refs[0].at[s]


def serve_kernel(plan, asked_ref, memory_ref, *out_refs):
    stored, width = memory_ref.shape
    piece = width // 4
    if plan.pairs:
        me = lax.axis_index("shard")
        asked = jnp.concatenate([asked_ref[pl.ds(me ^ k, 1), :] for k in range(plan.owners)], axis=0)
    else:
        asked = asked_ref[...]
    turned = asked.astype(F32).T
    blocks = [
        jnp.where(turned[: plan.main, s : s + 1].astype(I32) == iota((plan.main, stored), 1), 1.0, 0.0)
        for s in range(plan.owners)
    ]
    for i in range(plan.tail):
        spare = asked[:, plan.main + i : plan.main + i + 1]
        blocks.append(jnp.where(spare == iota((plan.owners, stored), 1), 1.0, 0.0))
    hot = jnp.concatenate(blocks, axis=0).astype(BF16)
    rows = dot(hot, memory_ref[...])
    main = plan.main
    for s in range(plan.owners):
        for c in range(4):
            at_slot(out_refs, s)[c * main : (c + 1) * main, :] = rows[
                s * main : (s + 1) * main, c * piece : (c + 1) * piece
            ].astype(BF16)
    if plan.tail:
        spare = rows[plan.owners * main :]
        stack = jnp.concatenate([spare[:, c * piece : (c + 1) * piece] for c in range(4)], axis=0)
        ordered = dot(tail_order(plan, True), stack.astype(BF16))
        for s in range(plan.owners):
            at_slot(out_refs, s)[4 * main : 4 * (main + plan.tail), :] = ordered[
                s * 4 * plan.tail : (s + 1) * 4 * plan.tail
            ].astype(BF16)


def table_of(plan, refs):
    main = plan.main
    pieces = [
        jnp.concatenate([at_slot(refs, s)[c * main : (c + 1) * main, :] for s in range(plan.owners)], axis=0)
        for c in range(4)
    ]
    table = jnp.concatenate(pieces, axis=1)
    if plan.tail:
        stack = jnp.concatenate(
            [at_slot(refs, s)[4 * main : 4 * (main + plan.tail), :].astype(F32) for s in range(plan.owners)], axis=0
        )
        ordered = dot(tail_order(plan, False), stack.astype(BF16))
        count = plan.tail * plan.owners
        spare = jnp.concatenate([ordered[c * count : (c + 1) * count] for c in range(4)], axis=1)
        table = jnp.concatenate([table, spare.astype(BF16)], axis=0)
    return table


def gru_kernel(plan, enc_ref, col_ref, row_ref, *refs):
    reps = plan.reps
    slots = plan.owners if plan.pairs else 1
    rows, refs = refs[:slots], refs[slots:]
    w_in, w_hid, w_time = refs[:reps], refs[reps : 2 * reps], refs[2 * reps : 3 * reps]
    out_ref, hnew_ref, hdst_ref, gin, ghid, delta = refs[3 * reps :]
    me = lax.axis_index("rep")
    events, width = hnew_ref.shape
    piece = width // reps
    cols = col_ref[...].astype(I32)
    spots = iota((events, plan.rows), 1)
    table = table_of(plan, rows)
    hsrc = dot(jnp.where(cols[:, 0:1] == spots, 1.0, 0.0).astype(BF16), table)
    source = hsrc.astype(BF16)
    target = dot(jnp.where(cols[:, 1:2] == spots, 1.0, 0.0).astype(BF16), table).astype(BF16)
    hdst_ref[...] = target
    enc = enc_ref[...]
    part = w_in[0].shape[1]
    for k in range(0, reps, 2):
        both = [jnp.concatenate([w[k][...], w[k + 1][...]], axis=1) for w in (w_in, w_time, w_hid)]
        into = dot(target, both[0]) + dot(enc, both[1])
        hidden = dot(source, both[2])
        for j in range(2):
            at = pl.ds(pl.multiple_of((me ^ (k + j)) * part, LANES), part)
            gin[:, at] = into[:, j * part : (j + 1) * part]
            ghid[:, at] = hidden[:, j * part : (j + 1) * part]
    step = 64
    for i in range(0, events, step):
        at = slice(i, i + step)
        reset = 0.5 * jnp.tanh(0.5 * (gin[at, :width] + ghid[at, :width])) + 0.5
        update = 0.5 * jnp.tanh(0.5 * (gin[at, width : 2 * width] + ghid[at, width : 2 * width])) + 0.5
        fresh = jnp.tanh(gin[at, 2 * width :] + reset * ghid[at, 2 * width :])
        hold = hsrc[at]
        new = (1.0 - update) * fresh + update * hold
        hnew_ref[at, :] = new
        delta[at, :] = (new - hold).astype(BF16)
    slots = plan.owners * plan.pad
    hits = jnp.where(row_ref[0:1, :] == iota((slots, events), 0), 1.0, 0.0)
    counts = jnp.maximum(jnp.sum(hits, axis=1, keepdims=True), 1.0)
    hits = hits.astype(BF16)
    mean = dot(hits, delta[...]) / counts
    for o in range(plan.owners):
        for q in range(reps):
            out_ref[o * reps + q] = mean[o * plan.pad : (o + 1) * plan.pad, q * piece : (q + 1) * piece].astype(BF16)


def attend_kernel(plan, listed_ref, hnew_ref, hdst_ref, memory_ref, *refs):
    reps = plan.reps
    w_query, w_keyval = refs[:reps], refs[reps : 2 * reps]
    out_ref, quarter_ref, query, keyval = refs[2 * reps :]
    me = lax.axis_index("rep")
    events, width = hnew_ref.shape
    piece = quarter_ref.shape[1]
    quarter_ref[...] = memory_ref[:, pl.ds(pl.multiple_of(me * piece, LANES), piece)]
    head = width // H
    hround = hnew_ref[...].astype(BF16)
    target = hdst_ref[...]
    first = width // reps
    for k in range(reps):
        query[:, pl.ds(pl.multiple_of((me ^ k) * first, LANES), first)] = dot(hround, w_query[k][...]).astype(BF16)
        at = pl.ds(pl.multiple_of((me ^ k) * 2 * first, LANES), 2 * first)
        keyval[:, at] = dot(target, w_keyval[k][...]).astype(BF16)
    for i in range(events // BLK):
        spans = [pl.ds(pl.multiple_of(listed_ref[i, j] * BLK, BLK), BLK) for j in range(NB)]
        at = slice(i * BLK, (i + 1) * BLK)
        for h in range(H):
            lane = slice(h * head, (h + 1) * head)
            keys = jnp.concatenate([keyval[s, lane] for s in spans], axis=0)
            values = jnp.concatenate([keyval[s, width + h * head : width + (h + 1) * head] for s in spans], axis=0)
            scores = lax.dot_general(
                query[at, lane], keys, (((1,), (1,)), ((), ())), preferred_element_type=F32
            ) * (1.0 / math.sqrt(head))
            peak = jnp.max(scores, axis=1, keepdims=True)
            power = jnp.exp(scores - peak)
            prob = (power / jnp.sum(power, axis=1, keepdims=True)).astype(BF16)
            out_ref[at, lane] = (hnew_ref[at, lane] + dot(prob, values)).astype(BF16)


def apply_kernel(plan, ids_ref, landed_ref, part_ref, out_ref, held, sem):
    copy = pltpu.make_async_copy(part_ref, held, sem)
    copy.start()
    stored = part_ref.shape[0]
    count = landed_ref.shape[0]
    landed = landed_ref[...]
    step = min(256, stored)
    ids = ids_ref[...]
    totals = []
    for i in range(0, stored, step):
        hot = jnp.where(iota((step, count), 0) + i == ids, 1.0, 0.0).astype(BF16)
        totals.append(dot(hot, landed))
    copy.wait()
    for i, total in zip(range(0, stored, step), totals):
        out_ref[i : i + step, :] = (held[i : i + step, :].astype(F32) + total).astype(BF16)


def join_kernel(plan, *refs):
    me = lax.axis_index("rep")
    out_ref = refs[-1]
    for k in range(plan.reps):
        piece = refs[k].shape[1]
        out_ref[:, pl.ds(pl.multiple_of((me ^ k) * piece, LANES), piece)] = refs[k][...]


def swap(x, bit, reps):
    return lax.ppermute(x, "rep", [(i, i ^ bit) for i in range(reps)])


def spread(arrays, reps):
    held = [{0: x} for x in arrays]
    bit = reps // 2
    while bit:
        for parts in held:
            for k in list(parts):
                parts[k ^ bit] = swap(parts[k], bit, reps)
        bit //= 2
    return [[parts[k] for k in range(reps)] for parts in held]


def shards(
    memory,
    touch_owner,
    touch_row,
    touch_time,
    src_slot,
    dst_slot,
    event_time,
    neighbour_blocks,
    time_freq,
    time_phase,
    w_input,
    w_time,
    w_hidden,
    w_query,
    w_keyval,
):
    owners = lax.axis_size("shard")
    reps = lax.axis_size("rep")
    entries = touch_row.shape[0]
    events = event_time.shape[0]
    stored, width = memory.shape
    plan = Plan(owners, reps, entries)
    piece = width // reps
    run = functools.partial
    sds = jax.ShapeDtypeStruct

    owner = touch_owner.reshape(1, entries)
    request = call(
        run(request_kernel, plan), [sds((owners, LANES), I32)], [VMEM] * 2, 1 << 20, 1 << 14, "request", limit=8
    )(owner, touch_row.reshape(1, entries))[0]

    full_time, full_hidden, full_input, full_keyval, full_query = spread(
        [w_time, w_hidden, w_input, w_keyval, w_query], reps
    )

    asked = lax.all_to_all(request, "shard", split_axis=0, concat_axis=0, tiled=True)
    encode, cols, rows = call(
        run(index_kernel, plan),
        [sds((events, time_freq.shape[0]), BF16), sds((events, 8), F32), sds((8, events), I32)],
        [VMEM] * 4,
        8 << 30,
        1 << 18,
        "index",
        limit=8,
    )(
        owner,
        jnp.concatenate([touch_time, src_slot, dst_slot, event_time]).reshape(1, -1),
        time_freq.reshape(1, -1),
        time_phase.reshape(1, -1),
    )
    everyone = [x for x in spread([asked], reps)[0]]

    chunk = (4 * (plan.main + plan.tail), width // 4)
    served = call(
        run(serve_kernel, plan),
        [sds(chunk, BF16)] * owners if plan.pairs else [sds((owners,) + chunk, BF16)],
        [VMEM] * 2,
        2 * plan.rows * stored * width,
        2 * stored * width + 2 * plan.rows * width,
        "serve",
        limit=12,
    )(asked, memory)
    if plan.pairs:
        returned = [served[0]] * owners
        far = sorted(range(1, owners), key=lambda k: (k < owners // 2, k < owners * 3 // 4, k))
        for k in far:
            returned[k] = lax.ppermute(served[k], "shard", [(i, i ^ k) for i in range(owners)])
    else:
        returned = [lax.all_to_all(served[0], "shard", split_axis=0, concat_axis=0, tiled=True)]

    outgoing, hnew, hdst = call(
        run(gru_kernel, plan),
        [sds((owners * reps, plan.pad, piece), BF16), sds((events, width), F32), sds((events, width), BF16)],
        [VMEM] * (3 + len(returned) + 3 * reps),
        2 * events * width * 3 * width * 2,
        8 << 20,
        "gru",
        scratch=[
            pltpu.VMEM((events, 3 * width), F32),
            pltpu.VMEM((events, 3 * width), F32),
            pltpu.VMEM((events, width), BF16),
        ],
        limit=24,
    )(encode, cols, rows, *returned, *full_input, *full_hidden, *full_time)
    landed = lax.all_to_all(outgoing, ("shard", "rep"), split_axis=0, concat_axis=0, tiled=True)

    embed, part = call(
        run(attend_kernel, plan),
        [sds((events, width), BF16), sds((stored, piece), BF16)],
        [SMEM] + [VMEM] * (3 + 2 * reps),
        2 * events * width * 3 * width,
        4 << 20,
        "attend",
        scratch=[
            pltpu.VMEM((events, width), BF16),
            pltpu.VMEM((events, 2 * width), BF16),
        ],
        limit=12,
    )(neighbour_blocks, hnew, hdst, memory, *full_query, *full_keyval)

    me = lax.axis_index("rep")
    stack = jnp.stack([x[:, : plan.pad] for x in everyone])
    order = me ^ jnp.arange(reps, dtype=I32)
    ids = jnp.swapaxes(stack[order], 0, 1).reshape(1, owners * reps * plan.pad)
    quarter = call(
        run(apply_kernel, plan),
        [sds((stored, piece), BF16)],
        [VMEM] * 2 + [ANY],
        2 * stored * owners * reps * plan.pad * piece * 2,
        4 << 20,
        "apply",
        scratch=[pltpu.VMEM((stored, piece), BF16), pltpu.SemaphoreType.DMA],
        limit=60,
    )(ids, landed.reshape(owners * reps * plan.pad, piece), part)[0]
    new_memory = call(
        run(join_kernel, plan), [sds((stored, width), BF16)], [VMEM] * reps, 1 << 20, 2 << 20, "join", limit=8
    )(*spread([quarter], reps)[0])[0]
    return (embed, new_memory)


def solution(mesh):
    placed = (
        P("shard", None),
        P(("shard", "rep"), None),
        P(("shard", "rep")),
        P(("shard", "rep")),
        P(("shard", "rep")),
        P(("shard", "rep")),
        P(("shard", "rep")),
        P(("shard", "rep"), None),
        P(),
        P(),
        P(None, "rep"),
        P(None, "rep"),
        P(None, "rep"),
        P(None, "rep"),
        P(None, "rep"),
    )
    return jax.shard_map(
        shards,
        mesh=mesh,
        in_specs=placed,
        out_specs=(P(("shard", "rep"), None), P("shard", None)),
        check_vma=False,
    )
```

```python
import functools
import math

import jax
import jax.numpy as jnp
from jax import lax
from jax.experimental import pallas as pl
from jax.experimental.pallas import tpu as pltpu
from jax.sharding import PartitionSpec as P

H = 4
BLK = 128
NB = 2
LANES = 128
F32 = jnp.float32
BF16 = jnp.bfloat16
I32 = jnp.int32
VMEM = pl.BlockSpec(memory_space=pltpu.VMEM)
SMEM = pl.BlockSpec(memory_space=pltpu.SMEM)
HBM = pl.BlockSpec(memory_space=pltpu.HBM)


def iota(shape, dim):
    return lax.broadcasted_iota(I32, shape, dim)


def dot(a, b):
    return jnp.dot(a, b, preferred_element_type=F32)


def call(body, outs, specs, flops, bytes_, name, scratch=(), limit=8):
    return pl.pallas_call(
        body,
        out_shape=outs,
        in_specs=specs,
        out_specs=[VMEM] * len(outs),
        scratch_shapes=list(scratch),
        compiler_params=pltpu.CompilerParams(vmem_limit_bytes=limit << 20),
        cost_estimate=pl.CostEstimate(flops=flops, bytes_accessed=bytes_, transcendentals=0),
        name=name,
    )


def far(arrays):
    return [pltpu.with_memory_space_constraint(x, pltpu.HBM) for x in arrays]


class Plan:
    def __init__(self, owners, reps, entries):
        self.owners = owners
        self.reps = reps
        self.entries = entries
        self.cap = 2 * entries // owners + 2
        self.tail = self.cap % 16 if self.cap % 16 * 4 == 8 else 0
        self.main = self.cap - self.tail if self.tail else -(-self.cap // 16) * 16
        self.rows = self.owners * (self.main + self.tail)
        self.pad = -(-self.cap // 8) * 8


def rank_of(own_col, own_row, entries):
    earlier = (own_col == own_row) & (iota((entries, entries), 0) < iota((entries, entries), 1))
    later = (own_col == own_row) & (iota((entries, entries), 1) < iota((entries, entries), 0))
    place_row = jnp.sum(jnp.where(earlier, 1, 0), axis=0, keepdims=True)
    place_col = jnp.sum(jnp.where(later, 1, 0), axis=1, keepdims=True)
    return place_row, place_col


def to_col(row, size):
    eye = iota((size, size), 0) == iota((size, size), 1)
    return jnp.sum(jnp.where(eye, row, 0), axis=1, keepdims=True)


def request_kernel(plan, owner_ref, row_ref, out_ref):
    own_row = owner_ref[...]
    own_col = to_col(own_row, plan.entries)
    _, place_col = rank_of(own_col, own_row, plan.entries)
    row = row_ref[...]
    mine = iota((plan.owners, plan.entries), 0) == own_row
    spot = jnp.where(place_col == iota((plan.entries, LANES), 1), 1.0, 0.0).astype(BF16)
    high = jnp.where(mine, row >> 5, 0).astype(F32).astype(BF16)
    low = jnp.where(mine, row & 31, 0).astype(F32).astype(BF16)
    out_ref[...] = (dot(high, spot) * 32.0 + dot(low, spot)).astype(I32)


def index_kernel(plan, owner_ref, packed_ref, freq_ref, phase_ref, enc_ref, col_ref, row_ref):
    events = enc_ref.shape[0]
    ends = [plan.entries + i * events for i in range(4)]
    tick_row = packed_ref[:, : ends[0]]
    src_row, dst_row, stamp_row = (packed_ref[:, a : a + events] for a in ends[:3])
    own_row = owner_ref[...]
    own_col = to_col(own_row, plan.entries)
    _, place = rank_of(own_col, own_row, plan.entries)
    tick = to_col(tick_row, plan.entries)
    spot = own_col * plan.main + place
    if plan.tail:
        spare = plan.owners * plan.main + (place - plan.main) * plan.owners + own_col
        spot = jnp.where(place < plan.main, spot, spare)
    back = own_col * plan.pad + place
    isrc = iota((plan.entries, events), 0) == src_row
    idst = iota((plan.entries, events), 0) == dst_row

    def pick(mask, values):
        return jnp.sum(jnp.where(mask, values, 0), axis=0, keepdims=True)

    src_spot = pick(isrc, spot)
    dst_spot = pick(idst, spot)
    src_back = pick(isrc, back)
    span = stamp_row - pick(isrc, tick)
    zero = jnp.zeros((8 - 3, events), I32)
    rows = jnp.concatenate([src_spot, dst_spot, span, zero], axis=0)
    row_ref[...] = jnp.concatenate([src_back, jnp.zeros((7, events), I32)], axis=0)
    cols = rows.astype(F32).T
    col_ref[...] = cols
    enc_ref[...] = jnp.cos(cols[:, 2:3] * freq_ref[...] + phase_ref[...]).astype(BF16)


def tail_order(plan, forward):
    count = 4 * plan.tail * plan.owners
    across = 0 if forward else 1
    there = iota((count, count), across)
    here = iota((count, count), 1 - across)
    part = 4 * plan.tail
    owner, inner = there // part, there % part
    return jnp.where((inner * plan.owners + owner) == here, 1.0, 0.0).astype(BF16)


def serve_kernel(plan, asked_ref, memory_ref, out_ref, held, hot_ref, sems):
    stored, width = memory_ref.shape
    piece = width // 4
    step = stored // 4
    copies = [
        pltpu.make_async_copy(memory_ref.at[pl.ds(i * step, step)], held.at[pl.ds(i * step, step)], sems.at[i])
        for i in range(4)
    ]
    for copy in copies:
        copy.start()
    asked = asked_ref[...]
    turned = asked.astype(F32).T
    blocks = [
        jnp.where(turned[: plan.main, s : s + 1].astype(I32) == iota((plan.main, stored), 1), 1.0, 0.0)
        for s in range(plan.owners)
    ]
    for i in range(plan.tail):
        spare = asked[:, plan.main + i : plan.main + i + 1]
        blocks.append(jnp.where(spare == iota((plan.owners, stored), 1), 1.0, 0.0))
    hot_ref[...] = jnp.concatenate(blocks, axis=0).astype(BF16)
    for copy in copies:
        copy.wait()
    rows = dot(hot_ref[...], held[...])
    main = plan.main
    for s in range(plan.owners):
        for c in range(4):
            out_ref[s, c * main : (c + 1) * main, :] = rows[
                s * main : (s + 1) * main, c * piece : (c + 1) * piece
            ].astype(BF16)
    if plan.tail:
        spare = rows[plan.owners * main :]
        stack = jnp.concatenate([spare[:, c * piece : (c + 1) * piece] for c in range(4)], axis=0)
        ordered = dot(tail_order(plan, True), stack.astype(BF16))
        for s in range(plan.owners):
            out_ref[s, 4 * main : 4 * (main + plan.tail), :] = ordered[
                s * 4 * plan.tail : (s + 1) * 4 * plan.tail
            ].astype(BF16)


def table_of(plan, ret_ref):
    main = plan.main
    pieces = [
        jnp.concatenate([ret_ref[s, c * main : (c + 1) * main, :] for s in range(plan.owners)], axis=0)
        for c in range(4)
    ]
    table = jnp.concatenate(pieces, axis=1)
    if plan.tail:
        stack = jnp.concatenate(
            [ret_ref[s, 4 * main : 4 * (main + plan.tail), :].astype(F32) for s in range(plan.owners)], axis=0
        )
        ordered = dot(tail_order(plan, False), stack.astype(BF16))
        count = plan.tail * plan.owners
        spare = jnp.concatenate([ordered[c * count : (c + 1) * count] for c in range(4)], axis=1)
        table = jnp.concatenate([table, spare.astype(BF16)], axis=0)
    return table


def gru_kernel(plan, ret_ref, row_ref, col_ref, far_enc, *refs):
    reps = plan.reps
    parts = refs[: 3 * reps]
    out_ref, hnew_ref, hdst_ref, gin, ghid, delta, hsrc_ref, enc_ref, w_in, w_hid, w_time, sems = refs[3 * reps :]
    copies = [pltpu.make_async_copy(far_enc, enc_ref, sems.at[0])]
    for g, held in ((1, w_hid), (0, w_in), (2, w_time)):
        for k in range(reps):
            copies.append(pltpu.make_async_copy(parts[g * reps + k], held.at[k], sems.at[1 + g * reps + k]))
    for copy in copies:
        copy.start()
    me = lax.axis_index("rep")
    events, width = hnew_ref.shape
    piece = width // reps
    cols = col_ref[...].astype(I32)
    spots = iota((events, plan.rows), 1)
    table = table_of(plan, ret_ref)
    source = dot(jnp.where(cols[:, 0:1] == spots, 1.0, 0.0).astype(BF16), table).astype(BF16)
    hsrc_ref[...] = source
    target = dot(jnp.where(cols[:, 1:2] == spots, 1.0, 0.0).astype(BF16), table).astype(BF16)
    hdst_ref[...] = target
    for copy in copies:
        copy.wait()
    source, target = hsrc_ref[...], hdst_ref[...]
    enc = enc_ref[...]
    part = w_in.shape[2]
    for k in range(0, reps, 2):
        both = [jnp.concatenate([w[k], w[k + 1]], axis=1) for w in (w_in, w_time, w_hid)]
        into = dot(target, both[0]) + dot(enc, both[1])
        hidden = dot(source, both[2])
        for j in range(2):
            at = pl.ds(pl.multiple_of((me ^ (k + j)) * part, LANES), part)
            gin[:, at] = into[:, j * part : (j + 1) * part]
            ghid[:, at] = hidden[:, j * part : (j + 1) * part]
    step = 64
    for i in range(0, events, step):
        at = slice(i, i + step)
        reset = 0.5 * jnp.tanh(0.5 * (gin[at, :width] + ghid[at, :width])) + 0.5
        update = 0.5 * jnp.tanh(0.5 * (gin[at, width : 2 * width] + ghid[at, width : 2 * width])) + 0.5
        fresh = jnp.tanh(gin[at, 2 * width :] + reset * ghid[at, 2 * width :])
        hold = hsrc_ref[at, :].astype(F32)
        new = (1.0 - update) * fresh + update * hold
        hnew_ref[at, :] = new
        delta[at, :] = (new - hold).astype(BF16)
    slots = plan.owners * plan.pad
    hits = jnp.where(row_ref[0:1, :] == iota((slots, events), 0), 1.0, 0.0)
    counts = jnp.maximum(jnp.sum(hits, axis=1, keepdims=True), 1.0)
    hits = hits.astype(BF16)
    mean = dot(hits, delta[...]) / counts
    for o in range(plan.owners):
        for q in range(reps):
            out_ref[o * reps + q] = mean[o * plan.pad : (o + 1) * plan.pad, q * piece : (q + 1) * piece].astype(BF16)


def attend_kernel(plan, listed_ref, hnew_ref, hdst_ref, memory_ref, *refs):
    reps = plan.reps
    w_query, w_keyval = refs[:reps], refs[reps : 2 * reps]
    out_ref, quarter_ref, query, keyval = refs[2 * reps :]
    me = lax.axis_index("rep")
    events, width = hnew_ref.shape
    piece = quarter_ref.shape[1]
    quarter_ref[...] = memory_ref[:, pl.ds(pl.multiple_of(me * piece, LANES), piece)]
    head = width // H
    hround = hnew_ref[...].astype(BF16)
    target = hdst_ref[...]
    first = width // reps
    for k in range(reps):
        query[:, pl.ds(pl.multiple_of((me ^ k) * first, LANES), first)] = dot(hround, w_query[k][...]).astype(BF16)
        at = pl.ds(pl.multiple_of((me ^ k) * 2 * first, LANES), 2 * first)
        keyval[:, at] = dot(target, w_keyval[k][...]).astype(BF16)
    for i in range(events // BLK):
        spans = [pl.ds(pl.multiple_of(listed_ref[i, j] * BLK, BLK), BLK) for j in range(NB)]
        at = slice(i * BLK, (i + 1) * BLK)
        for h in range(H):
            lane = slice(h * head, (h + 1) * head)
            keys = jnp.concatenate([keyval[s, lane] for s in spans], axis=0)
            values = jnp.concatenate([keyval[s, width + h * head : width + (h + 1) * head] for s in spans], axis=0)
            scores = lax.dot_general(
                query[at, lane], keys, (((1,), (1,)), ((), ())), preferred_element_type=F32
            ) * (1.0 / math.sqrt(head))
            peak = jnp.max(scores, axis=1, keepdims=True)
            power = jnp.exp(scores - peak)
            prob = (power / jnp.sum(power, axis=1, keepdims=True)).astype(BF16)
            out_ref[at, lane] = (hnew_ref[at, lane] + dot(prob, values)).astype(BF16)


def apply_kernel(plan, ids_ref, landed_ref, part_ref, out_ref, held, sem):
    copy = pltpu.make_async_copy(part_ref, held, sem)
    copy.start()
    stored = part_ref.shape[0]
    count = landed_ref.shape[0]
    landed = landed_ref[...]
    step = min(256, stored)
    ids = ids_ref[...]
    totals = []
    for i in range(0, stored, step):
        hot = jnp.where(iota((step, count), 0) + i == ids, 1.0, 0.0).astype(BF16)
        totals.append(dot(hot, landed))
    copy.wait()
    for i, total in zip(range(0, stored, step), totals):
        out_ref[i : i + step, :] = (held[i : i + step, :].astype(F32) + total).astype(BF16)


def join_kernel(plan, *refs):
    me = lax.axis_index("rep")
    out_ref = refs[-1]
    for k in range(plan.reps):
        piece = refs[k].shape[1]
        out_ref[:, pl.ds(pl.multiple_of((me ^ k) * piece, LANES), piece)] = refs[k][...]


def swap(x, bit, reps):
    return lax.ppermute(x, "rep", [(i, i ^ bit) for i in range(reps)])


def spread(arrays, reps):
    held = [{0: x} for x in arrays]
    bit = reps // 2
    while bit:
        for parts in held:
            for k in list(parts):
                parts[k ^ bit] = swap(parts[k], bit, reps)
        bit //= 2
    return [[parts[k] for k in range(reps)] for parts in held]


def shards(
    memory,
    touch_owner,
    touch_row,
    touch_time,
    src_slot,
    dst_slot,
    event_time,
    neighbour_blocks,
    time_freq,
    time_phase,
    w_input,
    w_time,
    w_hidden,
    w_query,
    w_keyval,
):
    owners = lax.axis_size("shard")
    reps = lax.axis_size("rep")
    entries = touch_row.shape[0]
    events = event_time.shape[0]
    stored, width = memory.shape
    plan = Plan(owners, reps, entries)
    piece = width // reps
    run = functools.partial
    sds = jax.ShapeDtypeStruct

    owner = touch_owner.reshape(1, entries)
    request = call(
        run(request_kernel, plan), [sds((owners, LANES), I32)], [VMEM] * 2, 1 << 20, 1 << 14, "request", limit=8
    )(owner, touch_row.reshape(1, entries))[0]

    request, w_time, w_hidden, w_input, w_keyval, w_query = lax.optimization_barrier(
        (request, w_time, w_hidden, w_input, w_keyval, w_query)
    )
    full_time, full_hidden, full_input, full_keyval, full_query = spread(
        [w_time, w_hidden, w_input, w_keyval, w_query], reps
    )

    asked = lax.all_to_all(request, "shard", split_axis=0, concat_axis=0, tiled=True)
    encode, cols, rows = call(
        run(index_kernel, plan),
        [sds((events, time_freq.shape[0]), BF16), sds((events, 8), F32), sds((8, events), I32)],
        [VMEM] * 4,
        8 << 30,
        1 << 18,
        "index",
        limit=8,
    )(
        owner,
        jnp.concatenate([touch_time, src_slot, dst_slot, event_time]).reshape(1, -1),
        time_freq.reshape(1, -1),
        time_phase.reshape(1, -1),
    )
    everyone = [x for x in spread([asked], reps)[0]]

    served = call(
        run(serve_kernel, plan),
        [sds((owners, 4 * (plan.main + plan.tail), width // 4), BF16)],
        [VMEM, HBM],
        2 * plan.rows * stored * width,
        2 * stored * width + 2 * plan.rows * width,
        "serve",
        scratch=[
            pltpu.VMEM((stored, width), BF16),
            pltpu.VMEM((plan.rows, stored), BF16),
            pltpu.SemaphoreType.DMA((4,)),
        ],
        limit=16,
    )(asked, *far([memory]))[0]
    returned = lax.all_to_all(served, "shard", split_axis=0, concat_axis=0, tiled=True)

    outgoing, hnew, hdst = call(
        run(gru_kernel, plan),
        [sds((owners * reps, plan.pad, piece), BF16), sds((events, width), F32), sds((events, width), BF16)],
        [VMEM] * 3 + [HBM] * (1 + 3 * reps),
        2 * events * width * 3 * width * 2,
        8 << 20,
        "gru",
        scratch=[
            pltpu.VMEM((events, 3 * width), F32),
            pltpu.VMEM((events, 3 * width), F32),
            pltpu.VMEM((events, width), BF16),
            pltpu.VMEM((events, width), BF16),
            pltpu.VMEM(encode.shape, BF16),
        ]
        + [pltpu.VMEM((reps,) + x.shape, BF16) for x in (w_input, w_hidden, w_time)]
        + [pltpu.SemaphoreType.DMA((1 + 3 * reps,))],
        limit=24,
    )(returned, rows, cols, *far([encode, *full_input, *full_hidden, *full_time]))
    landed = lax.all_to_all(outgoing, ("shard", "rep"), split_axis=0, concat_axis=0, tiled=True)

    embed, part = call(
        run(attend_kernel, plan),
        [sds((events, width), BF16), sds((stored, piece), BF16)],
        [SMEM] + [VMEM] * (3 + 2 * reps),
        2 * events * width * 3 * width,
        4 << 20,
        "attend",
        scratch=[
            pltpu.VMEM((events, width), BF16),
            pltpu.VMEM((events, 2 * width), BF16),
        ],
        limit=12,
    )(neighbour_blocks, hnew, hdst, memory, *full_query, *full_keyval)

    me = lax.axis_index("rep")
    stack = jnp.stack([x[:, : plan.pad] for x in everyone])
    order = me ^ jnp.arange(reps, dtype=I32)
    ids = jnp.swapaxes(stack[order], 0, 1).reshape(1, owners * reps * plan.pad)
    quarter = call(
        run(apply_kernel, plan),
        [sds((stored, piece), BF16)],
        [VMEM] * 2 + [HBM],
        2 * stored * owners * reps * plan.pad * piece * 2,
        4 << 20,
        "apply",
        scratch=[pltpu.VMEM((stored, piece), BF16), pltpu.SemaphoreType.DMA],
        limit=16,
    )(ids, landed.reshape(owners * reps * plan.pad, piece), *far([part]))[0]
    new_memory = call(
        run(join_kernel, plan), [sds((stored, width), BF16)], [VMEM] * reps, 1 << 20, 2 << 20, "join", limit=8
    )(*spread([quarter], reps)[0])[0]
    return (embed, new_memory)


def solution(mesh):
    placed = (
        P("shard", None),
        P(("shard", "rep"), None),
        P(("shard", "rep")),
        P(("shard", "rep")),
        P(("shard", "rep")),
        P(("shard", "rep")),
        P(("shard", "rep")),
        P(("shard", "rep"), None),
        P(),
        P(),
        P(None, "rep"),
        P(None, "rep"),
        P(None, "rep"),
        P(None, "rep"),
        P(None, "rep"),
    )
    return jax.shard_map(
        shards,
        mesh=mesh,
        in_specs=placed,
        out_specs=(P(("shard", "rep"), None), P("shard", None)),
        check_vma=False,
    )
```

```python
import functools
import math

import jax
import jax.numpy as jnp
from jax import lax
from jax.experimental import pallas as pl
from jax.experimental.pallas import tpu as pltpu
from jax.sharding import PartitionSpec as P

H = 4
BLK = 128
NB = 2
LANES = 128
F32 = jnp.float32
BF16 = jnp.bfloat16
I32 = jnp.int32
VMEM = pl.BlockSpec(memory_space=pltpu.VMEM)
SMEM = pl.BlockSpec(memory_space=pltpu.SMEM)
HBM = pl.BlockSpec(memory_space=pltpu.HBM)


def iota(shape, dim):
    return lax.broadcasted_iota(I32, shape, dim)


def dot(a, b):
    return jnp.dot(a, b, preferred_element_type=F32)


def call(body, outs, specs, flops, bytes_, name, scratch=(), limit=8, out_specs=None):
    return pl.pallas_call(
        body,
        out_shape=outs,
        in_specs=specs,
        out_specs=out_specs or [VMEM] * len(outs),
        scratch_shapes=list(scratch),
        compiler_params=pltpu.CompilerParams(vmem_limit_bytes=limit << 20),
        cost_estimate=pl.CostEstimate(flops=flops, bytes_accessed=bytes_, transcendentals=0),
        name=name,
    )


def far(arrays):
    return [pltpu.with_memory_space_constraint(x, pltpu.HBM) for x in arrays]


class Plan:
    def __init__(self, owners, reps, entries):
        self.owners = owners
        self.reps = reps
        self.entries = entries
        self.cap = 2 * entries // owners + 2
        self.tail = self.cap % 16 if self.cap % 16 * 4 == 8 else 0
        self.main = self.cap - self.tail if self.tail else -(-self.cap // 16) * 16
        self.rows = self.owners * (self.main + self.tail)
        self.pad = -(-self.cap // 8) * 8


def rank_of(own_col, own_row, entries):
    earlier = (own_col == own_row) & (iota((entries, entries), 0) < iota((entries, entries), 1))
    later = (own_col == own_row) & (iota((entries, entries), 1) < iota((entries, entries), 0))
    place_row = jnp.sum(jnp.where(earlier, 1, 0), axis=0, keepdims=True)
    place_col = jnp.sum(jnp.where(later, 1, 0), axis=1, keepdims=True)
    return place_row, place_col


def to_col(row, size):
    eye = iota((size, size), 0) == iota((size, size), 1)
    return jnp.sum(jnp.where(eye, row, 0), axis=1, keepdims=True)


def request_kernel(plan, owner_ref, row_ref, out_ref):
    own_row = owner_ref[...]
    own_col = to_col(own_row, plan.entries)
    _, place_col = rank_of(own_col, own_row, plan.entries)
    row = row_ref[...]
    mine = iota((plan.owners, plan.entries), 0) == own_row
    spot = jnp.where(place_col == iota((plan.entries, LANES), 1), 1.0, 0.0).astype(BF16)
    high = jnp.where(mine, row >> 5, 0).astype(F32).astype(BF16)
    low = jnp.where(mine, row & 31, 0).astype(F32).astype(BF16)
    out_ref[...] = (dot(high, spot) * 32.0 + dot(low, spot)).astype(I32)


def index_kernel(plan, owner_ref, packed_ref, freq_ref, phase_ref, enc_ref, col_ref, row_ref):
    events = enc_ref.shape[0]
    ends = [plan.entries + i * events for i in range(4)]
    tick_row = packed_ref[:, : ends[0]]
    src_row, dst_row, stamp_row = (packed_ref[:, a : a + events] for a in ends[:3])
    own_row = owner_ref[...]
    own_col = to_col(own_row, plan.entries)
    _, place = rank_of(own_col, own_row, plan.entries)
    tick = to_col(tick_row, plan.entries)
    spot = own_col * plan.main + place
    if plan.tail:
        spare = plan.owners * plan.main + (place - plan.main) * plan.owners + own_col
        spot = jnp.where(place < plan.main, spot, spare)
    back = own_col * plan.pad + place
    isrc = iota((plan.entries, events), 0) == src_row
    idst = iota((plan.entries, events), 0) == dst_row

    def pick(mask, values):
        return jnp.sum(jnp.where(mask, values, 0), axis=0, keepdims=True)

    src_spot = pick(isrc, spot)
    dst_spot = pick(idst, spot)
    src_back = pick(isrc, back)
    span = stamp_row - pick(isrc, tick)
    zero = jnp.zeros((8 - 3, events), I32)
    rows = jnp.concatenate([src_spot, dst_spot, span, zero], axis=0)
    row_ref[...] = jnp.concatenate([src_back, jnp.zeros((7, events), I32)], axis=0)
    cols = rows.astype(F32).T
    col_ref[...] = cols
    enc_ref[...] = jnp.cos(cols[:, 2:3] * freq_ref[...] + phase_ref[...]).astype(BF16)


def tail_order(plan, forward):
    count = 4 * plan.tail * plan.owners
    across = 0 if forward else 1
    there = iota((count, count), across)
    here = iota((count, count), 1 - across)
    part = 4 * plan.tail
    owner, inner = there // part, there % part
    return jnp.where((inner * plan.owners + owner) == here, 1.0, 0.0).astype(BF16)


def serve_kernel(plan, asked_ref, memory_ref, out_ref, held, hot_ref, sems):
    stored, width = memory_ref.shape
    piece = width // 4
    step = stored // 4
    copies = [
        pltpu.make_async_copy(memory_ref.at[pl.ds(i * step, step)], held.at[pl.ds(i * step, step)], sems.at[i])
        for i in range(4)
    ]
    for copy in copies:
        copy.start()
    asked = asked_ref[...]
    turned = asked.astype(F32).T
    blocks = [
        jnp.where(turned[: plan.main, s : s + 1].astype(I32) == iota((plan.main, stored), 1), 1.0, 0.0)
        for s in range(plan.owners)
    ]
    for i in range(plan.tail):
        spare = asked[:, plan.main + i : plan.main + i + 1]
        blocks.append(jnp.where(spare == iota((plan.owners, stored), 1), 1.0, 0.0))
    hot_ref[...] = jnp.concatenate(blocks, axis=0).astype(BF16)
    rows = 0.0
    for i, copy in enumerate(copies):
        copy.wait()
        rows += dot(hot_ref[:, i * step : (i + 1) * step], held[i * step : (i + 1) * step, :])
    main = plan.main
    for s in range(plan.owners):
        for c in range(4):
            out_ref[s, c * main : (c + 1) * main, :] = rows[
                s * main : (s + 1) * main, c * piece : (c + 1) * piece
            ].astype(BF16)
    if plan.tail:
        spare = rows[plan.owners * main :]
        stack = jnp.concatenate([spare[:, c * piece : (c + 1) * piece] for c in range(4)], axis=0)
        ordered = dot(tail_order(plan, True), stack.astype(BF16))
        for s in range(plan.owners):
            out_ref[s, 4 * main : 4 * (main + plan.tail), :] = ordered[
                s * 4 * plan.tail : (s + 1) * 4 * plan.tail
            ].astype(BF16)


def table_of(plan, ret_ref):
    main = plan.main
    pieces = [
        jnp.concatenate([ret_ref[s, c * main : (c + 1) * main, :] for s in range(plan.owners)], axis=0)
        for c in range(4)
    ]
    table = jnp.concatenate(pieces, axis=1)
    if plan.tail:
        stack = jnp.concatenate(
            [ret_ref[s, 4 * main : 4 * (main + plan.tail), :].astype(F32) for s in range(plan.owners)], axis=0
        )
        ordered = dot(tail_order(plan, False), stack.astype(BF16))
        count = plan.tail * plan.owners
        spare = jnp.concatenate([ordered[c * count : (c + 1) * count] for c in range(4)], axis=1)
        table = jnp.concatenate([table, spare.astype(BF16)], axis=0)
    return table


def gru_kernel(plan, ret_ref, row_ref, col_ref, far_enc, *refs):
    reps = plan.reps
    parts = refs[: 3 * reps]
    out_ref, hnew_ref, hdst_ref, gin, ghid, delta, hsrc_ref, enc_ref, w_in, w_hid, w_time, sems = refs[3 * reps :]
    copies = [pltpu.make_async_copy(far_enc, enc_ref, sems.at[0])]
    for g, held in ((1, w_hid), (0, w_in), (2, w_time)):
        for k in range(reps):
            copies.append(pltpu.make_async_copy(parts[g * reps + k], held.at[k], sems.at[1 + g * reps + k]))
    for copy in copies:
        copy.start()
    me = lax.axis_index("rep")
    events, width = hnew_ref.shape
    piece = width // reps
    cols = col_ref[...].astype(I32)
    spots = iota((events, plan.rows), 1)
    table = table_of(plan, ret_ref)
    source = dot(jnp.where(cols[:, 0:1] == spots, 1.0, 0.0).astype(BF16), table).astype(BF16)
    hsrc_ref[...] = source
    target = dot(jnp.where(cols[:, 1:2] == spots, 1.0, 0.0).astype(BF16), table).astype(BF16)
    hdst_ref[...] = target
    for copy in copies:
        copy.wait()
    source, target = hsrc_ref[...], hdst_ref[...]
    enc = enc_ref[...]
    part = w_in.shape[2]
    for k in range(0, reps, 2):
        both = [jnp.concatenate([w[k], w[k + 1]], axis=1) for w in (w_in, w_time, w_hid)]
        into = dot(target, both[0]) + dot(enc, both[1])
        hidden = dot(source, both[2])
        for j in range(2):
            at = pl.ds(pl.multiple_of((me ^ (k + j)) * part, LANES), part)
            gin[:, at] = into[:, j * part : (j + 1) * part]
            ghid[:, at] = hidden[:, j * part : (j + 1) * part]
    step = 64
    for i in range(0, events, step):
        at = slice(i, i + step)
        reset = 0.5 * jnp.tanh(0.5 * (gin[at, :width] + ghid[at, :width])) + 0.5
        update = 0.5 * jnp.tanh(0.5 * (gin[at, width : 2 * width] + ghid[at, width : 2 * width])) + 0.5
        fresh = jnp.tanh(gin[at, 2 * width :] + reset * ghid[at, 2 * width :])
        hold = hsrc_ref[at, :].astype(F32)
        new = (1.0 - update) * fresh + update * hold
        hnew_ref[at, :] = new
        delta[at, :] = (new - hold).astype(BF16)
    slots = plan.owners * plan.pad
    hits = jnp.where(row_ref[0:1, :] == iota((slots, events), 0), 1.0, 0.0)
    counts = jnp.maximum(jnp.sum(hits, axis=1, keepdims=True), 1.0)
    hits = hits.astype(BF16)
    mean = dot(hits, delta[...]) / counts
    for o in range(plan.owners):
        for q in range(reps):
            out_ref[o * reps + q] = mean[o * plan.pad : (o + 1) * plan.pad, q * piece : (q + 1) * piece].astype(BF16)


def attend_kernel(plan, listed_ref, hnew_ref, hdst_ref, memory_ref, *refs):
    reps = plan.reps
    w_query, w_keyval = refs[:reps], refs[reps : 2 * reps]
    out_ref, quarter_ref, query, keyval = refs[2 * reps :]
    me = lax.axis_index("rep")
    events, width = hnew_ref.shape
    piece = quarter_ref.shape[1]
    quarter_ref[...] = memory_ref[:, pl.ds(pl.multiple_of(me * piece, LANES), piece)]
    head = width // H
    hround = hnew_ref[...].astype(BF16)
    target = hdst_ref[...]
    first = width // reps
    for k in range(reps):
        query[:, pl.ds(pl.multiple_of((me ^ k) * first, LANES), first)] = dot(hround, w_query[k][...]).astype(BF16)
        at = pl.ds(pl.multiple_of((me ^ k) * 2 * first, LANES), 2 * first)
        keyval[:, at] = dot(target, w_keyval[k][...]).astype(BF16)
    for i in range(events // BLK):
        spans = [pl.ds(pl.multiple_of(listed_ref[i, j] * BLK, BLK), BLK) for j in range(NB)]
        at = slice(i * BLK, (i + 1) * BLK)
        for h in range(H):
            lane = slice(h * head, (h + 1) * head)
            keys = jnp.concatenate([keyval[s, lane] for s in spans], axis=0)
            values = jnp.concatenate([keyval[s, width + h * head : width + (h + 1) * head] for s in spans], axis=0)
            scores = lax.dot_general(
                query[at, lane], keys, (((1,), (1,)), ((), ())), preferred_element_type=F32
            ) * (1.0 / math.sqrt(head))
            peak = jnp.max(scores, axis=1, keepdims=True)
            power = jnp.exp(scores - peak)
            prob = (power / jnp.sum(power, axis=1, keepdims=True)).astype(BF16)
            out_ref[at, lane] = (hnew_ref[at, lane] + dot(prob, values)).astype(BF16)


def apply_kernel(plan, ids_ref, landed_ref, part_ref, out_ref, held, total, sem):
    copy = pltpu.make_async_copy(part_ref, held, sem)
    copy.start()
    stored = part_ref.shape[0]
    count = landed_ref.shape[0]
    landed = landed_ref[...]
    step = min(256, stored)
    ids = ids_ref[...]
    for i in range(0, stored, step):
        hot = jnp.where(iota((step, count), 0) + i == ids, 1.0, 0.0).astype(BF16)
        total[i : i + step, :] = dot(hot, landed)
    copy.wait()
    out_ref[...] = (held[...].astype(F32) + total[...]).astype(BF16)


def join_kernel(plan, *refs):
    me = lax.axis_index("rep")
    out_ref, sems = refs[plan.reps :]
    copies = []
    for k in range(plan.reps):
        piece = refs[k].shape[1]
        at = pl.ds(pl.multiple_of((me ^ k) * piece, LANES), piece)
        copies.append(pltpu.make_async_copy(refs[k], out_ref.at[:, at], sems.at[k]))
    for copy in copies:
        copy.start()
    for copy in copies:
        copy.wait()


def swap(x, bit, reps):
    return lax.ppermute(x, "rep", [(i, i ^ bit) for i in range(reps)])


def spread(arrays, reps):
    held = [{0: x} for x in arrays]
    bit = reps // 2
    while bit:
        for parts in held:
            for k in list(parts):
                parts[k ^ bit] = swap(parts[k], bit, reps)
        bit //= 2
    return [[parts[k] for k in range(reps)] for parts in held]


def shards(
    memory,
    touch_owner,
    touch_row,
    touch_time,
    src_slot,
    dst_slot,
    event_time,
    neighbour_blocks,
    time_freq,
    time_phase,
    w_input,
    w_time,
    w_hidden,
    w_query,
    w_keyval,
):
    owners = lax.axis_size("shard")
    reps = lax.axis_size("rep")
    entries = touch_row.shape[0]
    events = event_time.shape[0]
    stored, width = memory.shape
    plan = Plan(owners, reps, entries)
    piece = width // reps
    run = functools.partial
    sds = jax.ShapeDtypeStruct

    owner = touch_owner.reshape(1, entries)
    request = call(
        run(request_kernel, plan), [sds((owners, LANES), I32)], [VMEM] * 2, 1 << 20, 1 << 14, "request", limit=8
    )(owner, touch_row.reshape(1, entries))[0]

    asked = lax.all_to_all(request, "shard", split_axis=0, concat_axis=0, tiled=True)
    packed = jnp.concatenate([touch_time, src_slot, dst_slot, event_time]).reshape(1, -1)
    _, owner, packed = lax.optimization_barrier((request, owner, packed))
    encode, cols, rows = call(
        run(index_kernel, plan),
        [sds((events, time_freq.shape[0]), BF16), sds((events, 8), F32), sds((8, events), I32)],
        [VMEM] * 4,
        8 << 30,
        1 << 18,
        "index",
    )(owner, packed, time_freq.reshape(1, -1), time_phase.reshape(1, -1))
    encode, w_time, w_hidden, w_input, w_keyval, w_query = lax.optimization_barrier(
        (encode, w_time, w_hidden, w_input, w_keyval, w_query)
    )
    full_time, full_hidden, full_input, full_keyval, full_query = spread(
        [w_time, w_hidden, w_input, w_keyval, w_query], reps
    )
    everyone = [x for x in spread([asked], reps)[0]]

    served = call(
        run(serve_kernel, plan),
        [sds((owners, 4 * (plan.main + plan.tail), width // 4), BF16)],
        [VMEM, HBM],
        2 * plan.rows * stored * width,
        2 * stored * width + 2 * plan.rows * width,
        "serve",
        scratch=[
            pltpu.VMEM((stored, width), BF16),
            pltpu.VMEM((plan.rows, stored), BF16),
            pltpu.SemaphoreType.DMA((4,)),
        ],
        limit=16,
    )(asked, *far([memory]))[0]
    returned = lax.all_to_all(served, "shard", split_axis=0, concat_axis=0, tiled=True)

    outgoing, hnew, hdst = call(
        run(gru_kernel, plan),
        [sds((owners * reps, plan.pad, piece), BF16), sds((events, width), F32), sds((events, width), BF16)],
        [VMEM] * 3 + [HBM] * (1 + 3 * reps),
        2 * events * width * 3 * width * 2,
        8 << 20,
        "gru",
        scratch=[
            pltpu.VMEM((events, 3 * width), F32),
            pltpu.VMEM((events, 3 * width), F32),
            pltpu.VMEM((events, width), BF16),
            pltpu.VMEM((events, width), BF16),
            pltpu.VMEM(encode.shape, BF16),
        ]
        + [pltpu.VMEM((reps,) + x.shape, BF16) for x in (w_input, w_hidden, w_time)]
        + [pltpu.SemaphoreType.DMA((1 + 3 * reps,))],
        limit=24,
    )(returned, rows, cols, *far([encode, *full_input, *full_hidden, *full_time]))
    landed = lax.all_to_all(outgoing, ("shard", "rep"), split_axis=0, concat_axis=0, tiled=True)

    embed, part = call(
        run(attend_kernel, plan),
        [sds((events, width), BF16), sds((stored, piece), BF16)],
        [SMEM] + [VMEM] * (3 + 2 * reps),
        2 * events * width * 3 * width,
        4 << 20,
        "attend",
        scratch=[
            pltpu.VMEM((events, width), BF16),
            pltpu.VMEM((events, 2 * width), BF16),
        ],
        limit=12,
    )(neighbour_blocks, hnew, hdst, memory, *full_query, *full_keyval)

    me = lax.axis_index("rep")
    stack = jnp.stack([x[:, : plan.pad] for x in everyone])
    order = me ^ jnp.arange(reps, dtype=I32)
    ids = jnp.swapaxes(stack[order], 0, 1).reshape(1, owners * reps * plan.pad)
    quarter = call(
        run(apply_kernel, plan),
        [sds((stored, piece), BF16)],
        [VMEM] * 2 + [HBM],
        2 * stored * owners * reps * plan.pad * piece * 2,
        4 << 20,
        "apply",
        scratch=[pltpu.VMEM((stored, piece), BF16), pltpu.VMEM((stored, piece), F32), pltpu.SemaphoreType.DMA],
        limit=16,
    )(ids, landed.reshape(owners * reps * plan.pad, piece), *far([part]))[0]
    new_memory = call(
        run(join_kernel, plan), [sds((stored, width), BF16)], [VMEM] * reps, 1 << 20, 2 << 20, "join",
        scratch=[pltpu.SemaphoreType.DMA((reps,))], out_specs=[HBM],
    )(*spread([quarter], reps)[0])[0]
    return (embed, new_memory)


def solution(mesh):
    placed = (
        P("shard", None),
        P(("shard", "rep"), None),
        P(("shard", "rep")),
        P(("shard", "rep")),
        P(("shard", "rep")),
        P(("shard", "rep")),
        P(("shard", "rep")),
        P(("shard", "rep"), None),
        P(),
        P(),
        P(None, "rep"),
        P(None, "rep"),
        P(None, "rep"),
        P(None, "rep"),
        P(None, "rep"),
    )
    return jax.shard_map(
        shards,
        mesh=mesh,
        in_specs=placed,
        out_specs=(P(("shard", "rep"), None), P("shard", None)),
        check_vma=False,
    )
```

```python
import functools
import math

import jax
import jax.numpy as jnp
from jax import lax
from jax.experimental import pallas as pl
from jax.experimental.pallas import tpu as pltpu
from jax.sharding import PartitionSpec as P

H = 4
BLK = 128
NB = 2
LANES = 128
F32 = jnp.float32
BF16 = jnp.bfloat16
I32 = jnp.int32
VMEM = pl.BlockSpec(memory_space=pltpu.VMEM)
SMEM = pl.BlockSpec(memory_space=pltpu.SMEM)
HBM = pl.BlockSpec(memory_space=pltpu.HBM)


def iota(shape, dim):
    return lax.broadcasted_iota(I32, shape, dim)


def dot(a, b):
    return jnp.dot(a, b, preferred_element_type=F32)


def call(body, outs, specs, flops, bytes_, name, scratch=(), limit=8, out_specs=None):
    return pl.pallas_call(
        body,
        out_shape=outs,
        in_specs=specs,
        out_specs=out_specs or [VMEM] * len(outs),
        scratch_shapes=list(scratch),
        compiler_params=pltpu.CompilerParams(vmem_limit_bytes=limit << 20),
        cost_estimate=pl.CostEstimate(flops=flops, bytes_accessed=bytes_, transcendentals=0),
        name=name,
    )


def far(arrays):
    return [pltpu.with_memory_space_constraint(x, pltpu.HBM) for x in arrays]


class Plan:
    def __init__(self, owners, reps, entries):
        self.owners = owners
        self.reps = reps
        self.entries = entries
        self.cap = 2 * entries // owners + 2
        self.tail = self.cap % 16 if self.cap % 16 * 4 == 8 else 0
        self.main = self.cap - self.tail if self.tail else -(-self.cap // 16) * 16
        self.rows = self.owners * (self.main + self.tail)
        self.pad = -(-self.cap // 8) * 8


def rank_of(own_col, own_row, entries):
    earlier = (own_col == own_row) & (iota((entries, entries), 0) < iota((entries, entries), 1))
    later = (own_col == own_row) & (iota((entries, entries), 1) < iota((entries, entries), 0))
    place_row = jnp.sum(jnp.where(earlier, 1, 0), axis=0, keepdims=True)
    place_col = jnp.sum(jnp.where(later, 1, 0), axis=1, keepdims=True)
    return place_row, place_col


def to_col(row, size):
    eye = iota((size, size), 0) == iota((size, size), 1)
    return jnp.sum(jnp.where(eye, row, 0), axis=1, keepdims=True)


def request_kernel(plan, owner_ref, row_ref, out_ref):
    own_row = owner_ref[...]
    own_col = to_col(own_row, plan.entries)
    _, place_col = rank_of(own_col, own_row, plan.entries)
    row = row_ref[...]
    mine = iota((plan.owners, plan.entries), 0) == own_row
    spot = jnp.where(place_col == iota((plan.entries, LANES), 1), 1.0, 0.0).astype(BF16)
    high = jnp.where(mine, row >> 5, 0).astype(F32).astype(BF16)
    low = jnp.where(mine, row & 31, 0).astype(F32).astype(BF16)
    out_ref[...] = (dot(high, spot) * 32.0 + dot(low, spot)).astype(I32)


def index_kernel(plan, owner_ref, packed_ref, freq_ref, phase_ref, enc_ref, col_ref, row_ref):
    events = enc_ref.shape[0]
    ends = [plan.entries + i * events for i in range(4)]
    tick_row = packed_ref[:, : ends[0]]
    src_row, dst_row, stamp_row = (packed_ref[:, a : a + events] for a in ends[:3])
    own_row = owner_ref[...]
    own_col = to_col(own_row, plan.entries)
    _, place = rank_of(own_col, own_row, plan.entries)
    tick = to_col(tick_row, plan.entries)
    spot = own_col * plan.main + place
    if plan.tail:
        spare = plan.owners * plan.main + (place - plan.main) * plan.owners + own_col
        spot = jnp.where(place < plan.main, spot, spare)
    back = own_col * plan.pad + place
    isrc = iota((plan.entries, events), 0) == src_row
    idst = iota((plan.entries, events), 0) == dst_row

    def pick(mask, values):
        return jnp.sum(jnp.where(mask, values, 0), axis=0, keepdims=True)

    src_spot = pick(isrc, spot)
    dst_spot = pick(idst, spot)
    src_back = pick(isrc, back)
    span = stamp_row - pick(isrc, tick)
    zero = jnp.zeros((8 - 3, events), I32)
    rows = jnp.concatenate([src_spot, dst_spot, span, zero], axis=0)
    row_ref[...] = jnp.concatenate([src_back, jnp.zeros((7, events), I32)], axis=0)
    cols = rows.astype(F32).T
    col_ref[...] = cols
    enc_ref[...] = jnp.cos(cols[:, 2:3] * freq_ref[...] + phase_ref[...]).astype(BF16)


def tail_order(plan, forward):
    count = 4 * plan.tail * plan.owners
    across = 0 if forward else 1
    there = iota((count, count), across)
    here = iota((count, count), 1 - across)
    part = 4 * plan.tail
    owner, inner = there // part, there % part
    return jnp.where((inner * plan.owners + owner) == here, 1.0, 0.0).astype(BF16)


def serve_kernel(plan, asked_ref, memory_ref, after_ref, out_ref, held, hot_ref, sems):
    stored, width = memory_ref.shape
    piece = width // 4
    step = stored // 4
    copies = [
        pltpu.make_async_copy(memory_ref.at[pl.ds(i * step, step)], held.at[pl.ds(i * step, step)], sems.at[i])
        for i in range(4)
    ]
    for copy in copies:
        copy.start()
    asked = asked_ref[...]
    turned = asked.astype(F32).T
    blocks = [
        jnp.where(turned[: plan.main, s : s + 1].astype(I32) == iota((plan.main, stored), 1), 1.0, 0.0)
        for s in range(plan.owners)
    ]
    for i in range(plan.tail):
        spare = asked[:, plan.main + i : plan.main + i + 1]
        blocks.append(jnp.where(spare == iota((plan.owners, stored), 1), 1.0, 0.0))
    hot_ref[...] = jnp.concatenate(blocks, axis=0).astype(BF16)
    rows = 0.0
    for i, copy in enumerate(copies):
        copy.wait()
        rows += dot(hot_ref[:, i * step : (i + 1) * step], held[i * step : (i + 1) * step, :])
    main = plan.main
    for s in range(plan.owners):
        for c in range(4):
            out_ref[s, c * main : (c + 1) * main, :] = rows[
                s * main : (s + 1) * main, c * piece : (c + 1) * piece
            ].astype(BF16)
    if plan.tail:
        spare = rows[plan.owners * main :]
        stack = jnp.concatenate([spare[:, c * piece : (c + 1) * piece] for c in range(4)], axis=0)
        ordered = dot(tail_order(plan, True), stack.astype(BF16))
        for s in range(plan.owners):
            out_ref[s, 4 * main : 4 * (main + plan.tail), :] = ordered[
                s * 4 * plan.tail : (s + 1) * 4 * plan.tail
            ].astype(BF16)


def table_of(plan, ret_ref):
    main = plan.main
    pieces = [
        jnp.concatenate([ret_ref[s, c * main : (c + 1) * main, :] for s in range(plan.owners)], axis=0)
        for c in range(4)
    ]
    table = jnp.concatenate(pieces, axis=1)
    if plan.tail:
        stack = jnp.concatenate(
            [ret_ref[s, 4 * main : 4 * (main + plan.tail), :].astype(F32) for s in range(plan.owners)], axis=0
        )
        ordered = dot(tail_order(plan, False), stack.astype(BF16))
        count = plan.tail * plan.owners
        spare = jnp.concatenate([ordered[c * count : (c + 1) * count] for c in range(4)], axis=1)
        table = jnp.concatenate([table, spare.astype(BF16)], axis=0)
    return table


def gru_kernel(plan, ret_ref, row_ref, col_ref, far_enc, *refs):
    reps = plan.reps
    parts = refs[: 3 * reps]
    out_ref, hnew_ref, hdst_ref, gin, ghid, delta, hsrc_ref, enc_ref, w_in, w_hid, w_time, sems = refs[3 * reps :]
    copies = [pltpu.make_async_copy(far_enc, enc_ref, sems.at[0])]
    for g, held in ((1, w_hid), (0, w_in), (2, w_time)):
        for k in range(reps):
            copies.append(pltpu.make_async_copy(parts[g * reps + k], held.at[k], sems.at[1 + g * reps + k]))
    for copy in copies:
        copy.start()
    me = lax.axis_index("rep")
    events, width = hnew_ref.shape
    piece = width // reps
    cols = col_ref[...].astype(I32)
    spots = iota((events, plan.rows), 1)
    table = table_of(plan, ret_ref)
    source = dot(jnp.where(cols[:, 0:1] == spots, 1.0, 0.0).astype(BF16), table).astype(BF16)
    hsrc_ref[...] = source
    target = dot(jnp.where(cols[:, 1:2] == spots, 1.0, 0.0).astype(BF16), table).astype(BF16)
    hdst_ref[...] = target
    for copy in copies:
        copy.wait()
    source, target = hsrc_ref[...], hdst_ref[...]
    enc = enc_ref[...]
    part = w_in.shape[2]
    for k in range(0, reps, 2):
        both = [jnp.concatenate([w[k], w[k + 1]], axis=1) for w in (w_in, w_time, w_hid)]
        into = dot(target, both[0]) + dot(enc, both[1])
        hidden = dot(source, both[2])
        for j in range(2):
            at = pl.ds(pl.multiple_of((me ^ (k + j)) * part, LANES), part)
            gin[:, at] = into[:, j * part : (j + 1) * part]
            ghid[:, at] = hidden[:, j * part : (j + 1) * part]
    step = 64
    for i in range(0, events, step):
        at = slice(i, i + step)
        reset = 0.5 * jnp.tanh(0.5 * (gin[at, :width] + ghid[at, :width])) + 0.5
        update = 0.5 * jnp.tanh(0.5 * (gin[at, width : 2 * width] + ghid[at, width : 2 * width])) + 0.5
        fresh = jnp.tanh(gin[at, 2 * width :] + reset * ghid[at, 2 * width :])
        hold = hsrc_ref[at, :].astype(F32)
        new = (1.0 - update) * fresh + update * hold
        hnew_ref[at, :] = new
        delta[at, :] = (new - hold).astype(BF16)
    slots = plan.owners * plan.pad
    hits = jnp.where(row_ref[0:1, :] == iota((slots, events), 0), 1.0, 0.0)
    counts = jnp.maximum(jnp.sum(hits, axis=1, keepdims=True), 1.0)
    hits = hits.astype(BF16)
    mean = dot(hits, delta[...]) / counts
    for o in range(plan.owners):
        for q in range(reps):
            out_ref[o * reps + q] = mean[o * plan.pad : (o + 1) * plan.pad, q * piece : (q + 1) * piece].astype(BF16)


def attend_kernel(plan, listed_ref, hnew_ref, hdst_ref, memory_ref, *refs):
    reps = plan.reps
    w_query, w_keyval = refs[:reps], refs[reps : 2 * reps]
    out_ref, quarter_ref, query, keyval = refs[2 * reps :]
    me = lax.axis_index("rep")
    events, width = hnew_ref.shape
    piece = quarter_ref.shape[1]
    quarter_ref[...] = memory_ref[:, pl.ds(pl.multiple_of(me * piece, LANES), piece)]
    head = width // H
    hround = hnew_ref[...].astype(BF16)
    target = hdst_ref[...]
    first = width // reps
    for k in range(reps):
        query[:, pl.ds(pl.multiple_of((me ^ k) * first, LANES), first)] = dot(hround, w_query[k][...]).astype(BF16)
        at = pl.ds(pl.multiple_of((me ^ k) * 2 * first, LANES), 2 * first)
        keyval[:, at] = dot(target, w_keyval[k][...]).astype(BF16)
    for i in range(events // BLK):
        spans = [pl.ds(pl.multiple_of(listed_ref[i, j] * BLK, BLK), BLK) for j in range(NB)]
        at = slice(i * BLK, (i + 1) * BLK)
        for h in range(H):
            lane = slice(h * head, (h + 1) * head)
            keys = jnp.concatenate([keyval[s, lane] for s in spans], axis=0)
            values = jnp.concatenate([keyval[s, width + h * head : width + (h + 1) * head] for s in spans], axis=0)
            scores = lax.dot_general(
                query[at, lane], keys, (((1,), (1,)), ((), ())), preferred_element_type=F32
            ) * (1.0 / math.sqrt(head))
            peak = jnp.max(scores, axis=1, keepdims=True)
            power = jnp.exp(scores - peak)
            prob = (power / jnp.sum(power, axis=1, keepdims=True)).astype(BF16)
            out_ref[at, lane] = (hnew_ref[at, lane] + dot(prob, values)).astype(BF16)


def apply_kernel(plan, ids_ref, landed_ref, part_ref, out_ref, held, total, sem):
    copy = pltpu.make_async_copy(part_ref, held, sem)
    copy.start()
    stored = part_ref.shape[0]
    count = landed_ref.shape[0]
    landed = landed_ref[...]
    step = min(256, stored)
    ids = ids_ref[...]
    for i in range(0, stored, step):
        hot = jnp.where(iota((step, count), 0) + i == ids, 1.0, 0.0).astype(BF16)
        total[i : i + step, :] = dot(hot, landed)
    copy.wait()
    out_ref[...] = (held[...].astype(F32) + total[...]).astype(BF16)


def join_kernel(plan, *refs):
    me = lax.axis_index("rep")
    out_ref, sems = refs[plan.reps :]
    copies = []
    for k in range(plan.reps):
        piece = refs[k].shape[1]
        at = pl.ds(pl.multiple_of((me ^ k) * piece, LANES), piece)
        copies.append(pltpu.make_async_copy(refs[k], out_ref.at[:, at], sems.at[k]))
    for copy in copies:
        copy.start()
    for copy in copies:
        copy.wait()


def swap(x, bit, reps):
    return lax.ppermute(x, "rep", [(i, i ^ bit) for i in range(reps)])


def spread(arrays, reps):
    held = [{0: x} for x in arrays]
    bit = reps // 2
    while bit:
        for parts in held:
            for k in list(parts):
                parts[k ^ bit] = swap(parts[k], bit, reps)
        bit //= 2
    return [[parts[k] for k in range(reps)] for parts in held]


def shards(
    memory,
    touch_owner,
    touch_row,
    touch_time,
    src_slot,
    dst_slot,
    event_time,
    neighbour_blocks,
    time_freq,
    time_phase,
    w_input,
    w_time,
    w_hidden,
    w_query,
    w_keyval,
):
    owners = lax.axis_size("shard")
    reps = lax.axis_size("rep")
    entries = touch_row.shape[0]
    events = event_time.shape[0]
    stored, width = memory.shape
    plan = Plan(owners, reps, entries)
    piece = width // reps
    run = functools.partial
    sds = jax.ShapeDtypeStruct

    owner = touch_owner.reshape(1, entries)
    request = call(
        run(request_kernel, plan), [sds((owners, LANES), I32)], [VMEM] * 2, 1 << 20, 1 << 14, "request", limit=8
    )(owner, touch_row.reshape(1, entries))[0]

    asked = lax.all_to_all(request, "shard", split_axis=0, concat_axis=0, tiled=True)
    packed = jnp.concatenate([touch_time, src_slot, dst_slot, event_time]).reshape(1, -1)
    _, owner, packed = lax.optimization_barrier((request, owner, packed))
    encode, cols, rows = call(
        run(index_kernel, plan),
        [sds((events, time_freq.shape[0]), BF16), sds((events, 8), F32), sds((8, events), I32)],
        [VMEM] * 4,
        8 << 30,
        1 << 18,
        "index",
    )(owner, packed, time_freq.reshape(1, -1), time_phase.reshape(1, -1))
    encode, w_time, w_hidden, w_input, w_keyval, w_query = lax.optimization_barrier(
        (encode, w_time, w_hidden, w_input, w_keyval, w_query)
    )
    full_time, full_hidden, full_input, full_keyval, full_query = spread(
        [w_time, w_hidden, w_input, w_keyval, w_query], reps
    )
    everyone = [x for x in spread([asked], reps)[0]]

    served = call(
        run(serve_kernel, plan),
        [sds((owners, 4 * (plan.main + plan.tail), width // 4), BF16)],
        [VMEM, HBM, HBM],
        2 * plan.rows * stored * width,
        2 * stored * width + 2 * plan.rows * width,
        "serve",
        scratch=[
            pltpu.VMEM((stored, width), BF16),
            pltpu.VMEM((plan.rows, stored), BF16),
            pltpu.SemaphoreType.DMA((4,)),
        ],
        limit=16,
    )(asked, *far([memory, encode]))[0]
    returned = lax.all_to_all(served, "shard", split_axis=0, concat_axis=0, tiled=True)

    outgoing, hnew, hdst = call(
        run(gru_kernel, plan),
        [sds((owners * reps, plan.pad, piece), BF16), sds((events, width), F32), sds((events, width), BF16)],
        [VMEM] * 3 + [HBM] * (1 + 3 * reps),
        2 * events * width * 3 * width * 2,
        8 << 20,
        "gru",
        scratch=[
            pltpu.VMEM((events, 3 * width), F32),
            pltpu.VMEM((events, 3 * width), F32),
            pltpu.VMEM((events, width), BF16),
            pltpu.VMEM((events, width), BF16),
            pltpu.VMEM(encode.shape, BF16),
        ]
        + [pltpu.VMEM((reps,) + x.shape, BF16) for x in (w_input, w_hidden, w_time)]
        + [pltpu.SemaphoreType.DMA((1 + 3 * reps,))],
        limit=24,
    )(returned, rows, cols, *far([encode, *full_input, *full_hidden, *full_time]))
    landed = lax.all_to_all(outgoing, ("shard", "rep"), split_axis=0, concat_axis=0, tiled=True)

    embed, part = call(
        run(attend_kernel, plan),
        [sds((events, width), BF16), sds((stored, piece), BF16)],
        [SMEM] + [VMEM] * (3 + 2 * reps),
        2 * events * width * 3 * width,
        4 << 20,
        "attend",
        scratch=[
            pltpu.VMEM((events, width), BF16),
            pltpu.VMEM((events, 2 * width), BF16),
        ],
        limit=12,
    )(neighbour_blocks, hnew, hdst, memory, *full_query, *full_keyval)

    me = lax.axis_index("rep")
    stack = jnp.stack([x[:, : plan.pad] for x in everyone])
    order = me ^ jnp.arange(reps, dtype=I32)
    ids = jnp.swapaxes(stack[order], 0, 1).reshape(1, owners * reps * plan.pad)
    quarter = call(
        run(apply_kernel, plan),
        [sds((stored, piece), BF16)],
        [VMEM] * 2 + [HBM],
        2 * stored * owners * reps * plan.pad * piece * 2,
        4 << 20,
        "apply",
        scratch=[pltpu.VMEM((stored, piece), BF16), pltpu.VMEM((stored, piece), F32), pltpu.SemaphoreType.DMA],
        limit=16,
    )(ids, landed.reshape(owners * reps * plan.pad, piece), *far([part]))[0]
    new_memory = call(
        run(join_kernel, plan), [sds((stored, width), BF16)], [VMEM] * reps, 1 << 20, 2 << 20, "join",
        scratch=[pltpu.SemaphoreType.DMA((reps,))], out_specs=[HBM],
    )(*spread([quarter], reps)[0])[0]
    return (embed, new_memory)


def solution(mesh):
    placed = (
        P("shard", None),
        P(("shard", "rep"), None),
        P(("shard", "rep")),
        P(("shard", "rep")),
        P(("shard", "rep")),
        P(("shard", "rep")),
        P(("shard", "rep")),
        P(("shard", "rep"), None),
        P(),
        P(),
        P(None, "rep"),
        P(None, "rep"),
        P(None, "rep"),
        P(None, "rep"),
        P(None, "rep"),
    )
    return jax.shard_map(
        shards,
        mesh=mesh,
        in_specs=placed,
        out_specs=(P(("shard", "rep"), None), P("shard", None)),
        check_vma=False,
    )
```

```python
import functools
import math

import jax
import jax.numpy as jnp
from jax import lax
from jax.experimental import pallas as pl
from jax.experimental.pallas import tpu as pltpu
from jax.sharding import PartitionSpec as P

H = 4
BLK = 128
NB = 2
LANES = 128
F32 = jnp.float32
BF16 = jnp.bfloat16
I32 = jnp.int32
VMEM = pl.BlockSpec(memory_space=pltpu.VMEM)
SMEM = pl.BlockSpec(memory_space=pltpu.SMEM)
HBM = pl.BlockSpec(memory_space=pltpu.HBM)


def iota(shape, dim):
    return lax.broadcasted_iota(I32, shape, dim)


def dot(a, b):
    return jnp.dot(a, b, preferred_element_type=F32)


def call(body, outs, specs, flops, bytes_, name, scratch=(), limit=8, out_specs=None):
    return pl.pallas_call(
        body,
        out_shape=outs,
        in_specs=specs,
        out_specs=out_specs or [VMEM] * len(outs),
        scratch_shapes=list(scratch),
        compiler_params=pltpu.CompilerParams(vmem_limit_bytes=limit << 20),
        cost_estimate=pl.CostEstimate(flops=flops, bytes_accessed=bytes_, transcendentals=0),
        name=name,
    )


def far(arrays):
    return [pltpu.with_memory_space_constraint(x, pltpu.HBM) for x in arrays]


class Plan:
    def __init__(self, owners, reps, entries):
        self.owners = owners
        self.reps = reps
        self.entries = entries
        self.cap = 2 * entries // owners + 2
        self.tail = self.cap % 16 if self.cap % 16 * 4 == 8 else 0
        self.main = self.cap - self.tail if self.tail else -(-self.cap // 16) * 16
        self.rows = self.owners * (self.main + self.tail)
        self.pad = -(-self.cap // 8) * 8


def rank_of(own_col, own_row, entries):
    earlier = (own_col == own_row) & (iota((entries, entries), 0) < iota((entries, entries), 1))
    later = (own_col == own_row) & (iota((entries, entries), 1) < iota((entries, entries), 0))
    place_row = jnp.sum(jnp.where(earlier, 1, 0), axis=0, keepdims=True)
    place_col = jnp.sum(jnp.where(later, 1, 0), axis=1, keepdims=True)
    return place_row, place_col


def to_col(row, size):
    eye = iota((size, size), 0) == iota((size, size), 1)
    return jnp.sum(jnp.where(eye, row, 0), axis=1, keepdims=True)


def request_kernel(plan, owner_ref, row_ref, out_ref):
    own_row = owner_ref[...]
    own_col = to_col(own_row, plan.entries)
    _, place_col = rank_of(own_col, own_row, plan.entries)
    row = row_ref[...]
    mine = iota((plan.owners, plan.entries), 0) == own_row
    spot = jnp.where(place_col == iota((plan.entries, LANES), 1), 1.0, 0.0).astype(BF16)
    high = jnp.where(mine, row >> 5, 0).astype(F32).astype(BF16)
    low = jnp.where(mine, row & 31, 0).astype(F32).astype(BF16)
    out_ref[...] = (dot(high, spot) * 32.0 + dot(low, spot)).astype(I32)


def index_kernel(plan, owner_ref, packed_ref, col_ref, row_ref):
    events = col_ref.shape[0]
    ends = [plan.entries + i * events for i in range(4)]
    tick_row = packed_ref[:, : ends[0]]
    src_row, dst_row, stamp_row = (packed_ref[:, a : a + events] for a in ends[:3])
    own_row = owner_ref[...]
    own_col = to_col(own_row, plan.entries)
    _, place = rank_of(own_col, own_row, plan.entries)
    tick = to_col(tick_row, plan.entries)
    spot = own_col * plan.main + place
    if plan.tail:
        spare = plan.owners * plan.main + (place - plan.main) * plan.owners + own_col
        spot = jnp.where(place < plan.main, spot, spare)
    back = own_col * plan.pad + place
    isrc = iota((plan.entries, events), 0) == src_row
    idst = iota((plan.entries, events), 0) == dst_row

    def pick(mask, values):
        return jnp.sum(jnp.where(mask, values, 0), axis=0, keepdims=True)

    src_spot = pick(isrc, spot)
    dst_spot = pick(idst, spot)
    src_back = pick(isrc, back)
    span = stamp_row - pick(isrc, tick)
    zero = jnp.zeros((8 - 3, events), I32)
    rows = jnp.concatenate([src_spot, dst_spot, span, zero], axis=0)
    row_ref[...] = jnp.concatenate([src_back, jnp.zeros((7, events), I32)], axis=0)
    col_ref[...] = rows.astype(F32).T


def encode_kernel(col_ref, freq_ref, phase_ref, enc_ref):
    enc_ref[...] = jnp.cos(col_ref[:, 2:3] * freq_ref[...] + phase_ref[...]).astype(BF16)


def tail_order(plan, forward):
    count = 4 * plan.tail * plan.owners
    across = 0 if forward else 1
    there = iota((count, count), across)
    here = iota((count, count), 1 - across)
    part = 4 * plan.tail
    owner, inner = there // part, there % part
    return jnp.where((inner * plan.owners + owner) == here, 1.0, 0.0).astype(BF16)


def serve_kernel(plan, asked_ref, memory_ref, after_ref, out_ref, held, hot_ref, sems):
    stored, width = memory_ref.shape
    piece = width // 4
    step = stored // 4
    copies = [
        pltpu.make_async_copy(memory_ref.at[pl.ds(i * step, step)], held.at[pl.ds(i * step, step)], sems.at[i])
        for i in range(4)
    ]
    for copy in copies:
        copy.start()
    asked = asked_ref[...]
    turned = asked.astype(F32).T
    blocks = [
        jnp.where(turned[: plan.main, s : s + 1].astype(I32) == iota((plan.main, stored), 1), 1.0, 0.0)
        for s in range(plan.owners)
    ]
    for i in range(plan.tail):
        spare = asked[:, plan.main + i : plan.main + i + 1]
        blocks.append(jnp.where(spare == iota((plan.owners, stored), 1), 1.0, 0.0))
    hot_ref[...] = jnp.concatenate(blocks, axis=0).astype(BF16)
    rows = 0.0
    for i, copy in enumerate(copies):
        copy.wait()
        rows += dot(hot_ref[:, i * step : (i + 1) * step], held[i * step : (i + 1) * step, :])
    main = plan.main
    for s in range(plan.owners):
        for c in range(4):
            out_ref[s, c * main : (c + 1) * main, :] = rows[
                s * main : (s + 1) * main, c * piece : (c + 1) * piece
            ].astype(BF16)
    if plan.tail:
        spare = rows[plan.owners * main :]
        stack = jnp.concatenate([spare[:, c * piece : (c + 1) * piece] for c in range(4)], axis=0)
        ordered = dot(tail_order(plan, True), stack.astype(BF16))
        for s in range(plan.owners):
            out_ref[s, 4 * main : 4 * (main + plan.tail), :] = ordered[
                s * 4 * plan.tail : (s + 1) * 4 * plan.tail
            ].astype(BF16)


def table_of(plan, ret_ref):
    main = plan.main
    pieces = [
        jnp.concatenate([ret_ref[s, c * main : (c + 1) * main, :] for s in range(plan.owners)], axis=0)
        for c in range(4)
    ]
    table = jnp.concatenate(pieces, axis=1)
    if plan.tail:
        stack = jnp.concatenate(
            [ret_ref[s, 4 * main : 4 * (main + plan.tail), :].astype(F32) for s in range(plan.owners)], axis=0
        )
        ordered = dot(tail_order(plan, False), stack.astype(BF16))
        count = plan.tail * plan.owners
        spare = jnp.concatenate([ordered[c * count : (c + 1) * count] for c in range(4)], axis=1)
        table = jnp.concatenate([table, spare.astype(BF16)], axis=0)
    return table


def gru_kernel(plan, ret_ref, row_ref, col_ref, far_enc, *refs):
    reps = plan.reps
    parts = refs[: 3 * reps]
    out_ref, hnew_ref, hdst_ref, gin, ghid, delta, hsrc_ref, enc_ref, w_in, w_hid, w_time, sems = refs[3 * reps :]
    copies = [pltpu.make_async_copy(far_enc, enc_ref, sems.at[0])]
    for g, held in ((1, w_hid), (0, w_in), (2, w_time)):
        for k in range(reps):
            copies.append(pltpu.make_async_copy(parts[g * reps + k], held.at[k], sems.at[1 + g * reps + k]))
    for copy in copies:
        copy.start()
    me = lax.axis_index("rep")
    events, width = hnew_ref.shape
    piece = width // reps
    cols = col_ref[...].astype(I32)
    spots = iota((events, plan.rows), 1)
    table = table_of(plan, ret_ref)
    source = dot(jnp.where(cols[:, 0:1] == spots, 1.0, 0.0).astype(BF16), table).astype(BF16)
    hsrc_ref[...] = source
    target = dot(jnp.where(cols[:, 1:2] == spots, 1.0, 0.0).astype(BF16), table).astype(BF16)
    hdst_ref[...] = target
    for copy in copies:
        copy.wait()
    source, target = hsrc_ref[...], hdst_ref[...]
    enc = enc_ref[...]
    part = w_in.shape[2]
    for k in range(0, reps, 2):
        both = [jnp.concatenate([w[k], w[k + 1]], axis=1) for w in (w_in, w_time, w_hid)]
        into = dot(target, both[0]) + dot(enc, both[1])
        hidden = dot(source, both[2])
        for j in range(2):
            at = pl.ds(pl.multiple_of((me ^ (k + j)) * part, LANES), part)
            gin[:, at] = into[:, j * part : (j + 1) * part]
            ghid[:, at] = hidden[:, j * part : (j + 1) * part]
    step = 64
    for i in range(0, events, step):
        at = slice(i, i + step)
        reset = 0.5 * jnp.tanh(0.5 * (gin[at, :width] + ghid[at, :width])) + 0.5
        update = 0.5 * jnp.tanh(0.5 * (gin[at, width : 2 * width] + ghid[at, width : 2 * width])) + 0.5
        fresh = jnp.tanh(gin[at, 2 * width :] + reset * ghid[at, 2 * width :])
        hold = hsrc_ref[at, :].astype(F32)
        new = (1.0 - update) * fresh + update * hold
        hnew_ref[at, :] = new
        delta[at, :] = (new - hold).astype(BF16)
    slots = plan.owners * plan.pad
    hits = jnp.where(row_ref[0:1, :] == iota((slots, events), 0), 1.0, 0.0)
    counts = jnp.maximum(jnp.sum(hits, axis=1, keepdims=True), 1.0)
    hits = hits.astype(BF16)
    mean = dot(hits, delta[...]) / counts
    for o in range(plan.owners):
        for q in range(reps):
            out_ref[o * reps + q] = mean[o * plan.pad : (o + 1) * plan.pad, q * piece : (q + 1) * piece].astype(BF16)


def attend_kernel(plan, listed_ref, hnew_ref, hdst_ref, memory_ref, *refs):
    reps = plan.reps
    w_query, w_keyval = refs[:reps], refs[reps : 2 * reps]
    out_ref, quarter_ref, query, keyval = refs[2 * reps :]
    me = lax.axis_index("rep")
    events, width = hnew_ref.shape
    piece = quarter_ref.shape[1]
    quarter_ref[...] = memory_ref[:, pl.ds(pl.multiple_of(me * piece, LANES), piece)]
    head = width // H
    hround = hnew_ref[...].astype(BF16)
    target = hdst_ref[...]
    first = width // reps
    for k in range(reps):
        query[:, pl.ds(pl.multiple_of((me ^ k) * first, LANES), first)] = dot(hround, w_query[k][...]).astype(BF16)
        at = pl.ds(pl.multiple_of((me ^ k) * 2 * first, LANES), 2 * first)
        keyval[:, at] = dot(target, w_keyval[k][...]).astype(BF16)
    for i in range(events // BLK):
        spans = [pl.ds(pl.multiple_of(listed_ref[i, j] * BLK, BLK), BLK) for j in range(NB)]
        at = slice(i * BLK, (i + 1) * BLK)
        for h in range(H):
            lane = slice(h * head, (h + 1) * head)
            keys = jnp.concatenate([keyval[s, lane] for s in spans], axis=0)
            values = jnp.concatenate([keyval[s, width + h * head : width + (h + 1) * head] for s in spans], axis=0)
            scores = lax.dot_general(
                query[at, lane], keys, (((1,), (1,)), ((), ())), preferred_element_type=F32
            ) * (1.0 / math.sqrt(head))
            peak = jnp.max(scores, axis=1, keepdims=True)
            power = jnp.exp(scores - peak)
            prob = (power / jnp.sum(power, axis=1, keepdims=True)).astype(BF16)
            out_ref[at, lane] = (hnew_ref[at, lane] + dot(prob, values)).astype(BF16)


def apply_kernel(plan, ids_ref, landed_ref, part_ref, out_ref, held, total, sem):
    copy = pltpu.make_async_copy(part_ref, held, sem)
    copy.start()
    stored = part_ref.shape[0]
    count = landed_ref.shape[0]
    landed = landed_ref[...]
    step = min(256, stored)
    ids = ids_ref[...]
    for i in range(0, stored, step):
        hot = jnp.where(iota((step, count), 0) + i == ids, 1.0, 0.0).astype(BF16)
        total[i : i + step, :] = dot(hot, landed)
    copy.wait()
    out_ref[...] = (held[...].astype(F32) + total[...]).astype(BF16)


def join_kernel(plan, *refs):
    me = lax.axis_index("rep")
    out_ref, sems = refs[plan.reps :]
    copies = []
    for k in range(plan.reps):
        piece = refs[k].shape[1]
        at = pl.ds(pl.multiple_of((me ^ k) * piece, LANES), piece)
        copies.append(pltpu.make_async_copy(refs[k], out_ref.at[:, at], sems.at[k]))
    for copy in copies:
        copy.start()
    for copy in copies:
        copy.wait()


def swap(x, bit, reps):
    return lax.ppermute(x, "rep", [(i, i ^ bit) for i in range(reps)])


def spread(arrays, reps):
    held = [{0: x} for x in arrays]
    bit = reps // 2
    while bit:
        for parts in held:
            for k in list(parts):
                parts[k ^ bit] = swap(parts[k], bit, reps)
        bit //= 2
    return [[parts[k] for k in range(reps)] for parts in held]


def shards(
    memory,
    touch_owner,
    touch_row,
    touch_time,
    src_slot,
    dst_slot,
    event_time,
    neighbour_blocks,
    time_freq,
    time_phase,
    w_input,
    w_time,
    w_hidden,
    w_query,
    w_keyval,
):
    owners = lax.axis_size("shard")
    reps = lax.axis_size("rep")
    entries = touch_row.shape[0]
    events = event_time.shape[0]
    stored, width = memory.shape
    plan = Plan(owners, reps, entries)
    piece = width // reps
    run = functools.partial
    sds = jax.ShapeDtypeStruct

    owner = touch_owner.reshape(1, entries)
    request = call(
        run(request_kernel, plan), [sds((owners, LANES), I32)], [VMEM] * 2, 1 << 20, 1 << 14, "request", limit=8
    )(owner, touch_row.reshape(1, entries))[0]

    asked = lax.all_to_all(request, "shard", split_axis=0, concat_axis=0, tiled=True)
    packed = jnp.concatenate([touch_time, src_slot, dst_slot, event_time]).reshape(1, -1)
    _, owner, packed = lax.optimization_barrier((request, owner, packed))
    cols, rows = call(
        run(index_kernel, plan),
        [sds((events, 8), F32), sds((8, events), I32)],
        [VMEM] * 2,
        8 << 30,
        1 << 18,
        "index",
    )(owner, packed)
    cols, w_time, w_hidden, w_input, w_keyval, w_query = lax.optimization_barrier(
        (cols, w_time, w_hidden, w_input, w_keyval, w_query)
    )
    encode = call(
        encode_kernel, [sds((events, time_freq.shape[0]), BF16)], [VMEM] * 3, 8 << 30, 1 << 18, "encode"
    )(cols, time_freq.reshape(1, -1), time_phase.reshape(1, -1))[0]
    full_time, full_hidden, full_input, full_keyval, full_query = spread(
        [w_time, w_hidden, w_input, w_keyval, w_query], reps
    )
    everyone = [x for x in spread([asked], reps)[0]]

    served = call(
        run(serve_kernel, plan),
        [sds((owners, 4 * (plan.main + plan.tail), width // 4), BF16)],
        [VMEM, HBM, HBM],
        2 * plan.rows * stored * width,
        2 * stored * width + 2 * plan.rows * width,
        "serve",
        scratch=[
            pltpu.VMEM((stored, width), BF16),
            pltpu.VMEM((plan.rows, stored), BF16),
            pltpu.SemaphoreType.DMA((4,)),
        ],
        limit=16,
    )(asked, *far([memory, cols]))[0]
    returned = lax.all_to_all(served, "shard", split_axis=0, concat_axis=0, tiled=True)

    outgoing, hnew, hdst = call(
        run(gru_kernel, plan),
        [sds((owners * reps, plan.pad, piece), BF16), sds((events, width), F32), sds((events, width), BF16)],
        [VMEM] * 3 + [HBM] * (1 + 3 * reps),
        2 * events * width * 3 * width * 2,
        8 << 20,
        "gru",
        scratch=[
            pltpu.VMEM((events, 3 * width), F32),
            pltpu.VMEM((events, 3 * width), F32),
            pltpu.VMEM((events, width), BF16),
            pltpu.VMEM((events, width), BF16),
            pltpu.VMEM(encode.shape, BF16),
        ]
        + [pltpu.VMEM((reps,) + x.shape, BF16) for x in (w_input, w_hidden, w_time)]
        + [pltpu.SemaphoreType.DMA((1 + 3 * reps,))],
        limit=24,
    )(returned, rows, cols, *far([encode, *full_input, *full_hidden, *full_time]))
    landed = lax.all_to_all(outgoing, ("shard", "rep"), split_axis=0, concat_axis=0, tiled=True)

    embed, part = call(
        run(attend_kernel, plan),
        [sds((events, width), BF16), sds((stored, piece), BF16)],
        [SMEM] + [VMEM] * (3 + 2 * reps),
        2 * events * width * 3 * width,
        4 << 20,
        "attend",
        scratch=[
            pltpu.VMEM((events, width), BF16),
            pltpu.VMEM((events, 2 * width), BF16),
        ],
        limit=12,
    )(neighbour_blocks, hnew, hdst, memory, *full_query, *full_keyval)

    me = lax.axis_index("rep")
    stack = jnp.stack([x[:, : plan.pad] for x in everyone])
    order = me ^ jnp.arange(reps, dtype=I32)
    ids = jnp.swapaxes(stack[order], 0, 1).reshape(1, owners * reps * plan.pad)
    quarter = call(
        run(apply_kernel, plan),
        [sds((stored, piece), BF16)],
        [VMEM] * 2 + [HBM],
        2 * stored * owners * reps * plan.pad * piece * 2,
        4 << 20,
        "apply",
        scratch=[pltpu.VMEM((stored, piece), BF16), pltpu.VMEM((stored, piece), F32), pltpu.SemaphoreType.DMA],
        limit=16,
    )(ids, landed.reshape(owners * reps * plan.pad, piece), *far([part]))[0]
    new_memory = call(
        run(join_kernel, plan), [sds((stored, width), BF16)], [VMEM] * reps, 1 << 20, 2 << 20, "join",
        scratch=[pltpu.SemaphoreType.DMA((reps,))], out_specs=[HBM],
    )(*spread([quarter], reps)[0])[0]
    return (embed, new_memory)


def solution(mesh):
    placed = (
        P("shard", None),
        P(("shard", "rep"), None),
        P(("shard", "rep")),
        P(("shard", "rep")),
        P(("shard", "rep")),
        P(("shard", "rep")),
        P(("shard", "rep")),
        P(("shard", "rep"), None),
        P(),
        P(),
        P(None, "rep"),
        P(None, "rep"),
        P(None, "rep"),
        P(None, "rep"),
        P(None, "rep"),
    )
    return jax.shard_map(
        shards,
        mesh=mesh,
        in_specs=placed,
        out_specs=(P(("shard", "rep"), None), P("shard", None)),
        check_vma=False,
    )
```

```python
import functools
import math

import jax
import jax.numpy as jnp
from jax import lax
from jax.experimental import pallas as pl
from jax.experimental.pallas import tpu as pltpu
from jax.sharding import PartitionSpec as P

H = 4
BLK = 128
NB = 2
LANES = 128
F32 = jnp.float32
BF16 = jnp.bfloat16
I32 = jnp.int32
VMEM = pl.BlockSpec(memory_space=pltpu.VMEM)
SMEM = pl.BlockSpec(memory_space=pltpu.SMEM)
HBM = pl.BlockSpec(memory_space=pltpu.HBM)


def iota(shape, dim):
    return lax.broadcasted_iota(I32, shape, dim)


def dot(a, b):
    return jnp.dot(a, b, preferred_element_type=F32)


def call(body, outs, specs, flops, bytes_, name, scratch=(), limit=8, out_specs=None):
    return pl.pallas_call(
        body,
        out_shape=outs,
        in_specs=specs,
        out_specs=out_specs or [VMEM] * len(outs),
        scratch_shapes=list(scratch),
        compiler_params=pltpu.CompilerParams(vmem_limit_bytes=limit << 20),
        cost_estimate=pl.CostEstimate(flops=flops, bytes_accessed=bytes_, transcendentals=0),
        name=name,
    )


def far(arrays):
    return [pltpu.with_memory_space_constraint(x, pltpu.HBM) for x in arrays]


class Plan:
    def __init__(self, owners, reps, entries):
        self.owners = owners
        self.reps = reps
        self.entries = entries
        self.cap = 2 * entries // owners + 2
        self.tail = self.cap % 16 if self.cap % 16 * 4 == 8 else 0
        self.main = self.cap - self.tail if self.tail else -(-self.cap // 16) * 16
        self.rows = self.owners * (self.main + self.tail)
        self.pad = -(-self.cap // 8) * 8


def rank_of(own_col, own_row, entries):
    earlier = (own_col == own_row) & (iota((entries, entries), 0) < iota((entries, entries), 1))
    later = (own_col == own_row) & (iota((entries, entries), 1) < iota((entries, entries), 0))
    place_row = jnp.sum(jnp.where(earlier, 1, 0), axis=0, keepdims=True)
    place_col = jnp.sum(jnp.where(later, 1, 0), axis=1, keepdims=True)
    return place_row, place_col


def to_col(row, size):
    eye = iota((size, size), 0) == iota((size, size), 1)
    return jnp.sum(jnp.where(eye, row, 0), axis=1, keepdims=True)


def request_kernel(plan, owner_ref, row_ref, out_ref):
    own_row = owner_ref[...]
    own_col = to_col(own_row, plan.entries)
    _, place_col = rank_of(own_col, own_row, plan.entries)
    row = row_ref[...]
    mine = iota((plan.owners, plan.entries), 0) == own_row
    spot = jnp.where(place_col == iota((plan.entries, LANES), 1), 1.0, 0.0).astype(BF16)
    high = jnp.where(mine, row >> 5, 0).astype(F32).astype(BF16)
    low = jnp.where(mine, row & 31, 0).astype(F32).astype(BF16)
    out_ref[...] = (dot(high, spot) * 32.0 + dot(low, spot)).astype(I32)


def index_kernel(plan, owner_ref, packed_ref, freq_ref, phase_ref, enc_ref, col_ref, row_ref):
    events = enc_ref.shape[0]
    ends = [plan.entries + i * events for i in range(4)]
    tick_row = packed_ref[:, : ends[0]]
    src_row, dst_row, stamp_row = (packed_ref[:, a : a + events] for a in ends[:3])
    own_row = owner_ref[...]
    own_col = to_col(own_row, plan.entries)
    _, place = rank_of(own_col, own_row, plan.entries)
    tick = to_col(tick_row, plan.entries)
    spot = own_col * plan.main + place
    if plan.tail:
        spare = plan.owners * plan.main + (place - plan.main) * plan.owners + own_col
        spot = jnp.where(place < plan.main, spot, spare)
    back = own_col * plan.pad + place
    isrc = iota((plan.entries, events), 0) == src_row
    idst = iota((plan.entries, events), 0) == dst_row

    def pick(mask, values):
        return jnp.sum(jnp.where(mask, values, 0), axis=0, keepdims=True)

    src_spot = pick(isrc, spot)
    dst_spot = pick(idst, spot)
    src_back = pick(isrc, back)
    span = stamp_row - pick(isrc, tick)
    zero = jnp.zeros((8 - 3, events), I32)
    rows = jnp.concatenate([src_spot, dst_spot, span, zero], axis=0)
    row_ref[...] = jnp.concatenate([src_back, jnp.zeros((7, events), I32)], axis=0)
    cols = rows.astype(F32).T
    col_ref[...] = cols
    enc_ref[...] = jnp.cos(cols[:, 2:3] * freq_ref[...] + phase_ref[...]).astype(BF16)


def tail_order(plan, forward):
    count = 4 * plan.tail * plan.owners
    across = 0 if forward else 1
    there = iota((count, count), across)
    here = iota((count, count), 1 - across)
    part = 4 * plan.tail
    owner, inner = there // part, there % part
    return jnp.where((inner * plan.owners + owner) == here, 1.0, 0.0).astype(BF16)


def serve_kernel(plan, asked_ref, memory_ref, out_ref, held, hot_ref, sems):
    stored, width = memory_ref.shape
    piece = width // 4
    step = stored // 4
    copies = [
        pltpu.make_async_copy(memory_ref.at[pl.ds(i * step, step)], held.at[pl.ds(i * step, step)], sems.at[i])
        for i in range(4)
    ]
    for copy in copies:
        copy.start()
    asked = asked_ref[...]
    turned = asked.astype(F32).T
    blocks = [
        jnp.where(turned[: plan.main, s : s + 1].astype(I32) == iota((plan.main, stored), 1), 1.0, 0.0)
        for s in range(plan.owners)
    ]
    for i in range(plan.tail):
        spare = asked[:, plan.main + i : plan.main + i + 1]
        blocks.append(jnp.where(spare == iota((plan.owners, stored), 1), 1.0, 0.0))
    hot_ref[...] = jnp.concatenate(blocks, axis=0).astype(BF16)
    for copy in copies:
        copy.wait()
    rows = dot(hot_ref[...], held[...])
    main = plan.main
    for s in range(plan.owners):
        for c in range(4):
            out_ref[s, c * main : (c + 1) * main, :] = rows[
                s * main : (s + 1) * main, c * piece : (c + 1) * piece
            ].astype(BF16)
    if plan.tail:
        spare = rows[plan.owners * main :]
        stack = jnp.concatenate([spare[:, c * piece : (c + 1) * piece] for c in range(4)], axis=0)
        ordered = dot(tail_order(plan, True), stack.astype(BF16))
        for s in range(plan.owners):
            out_ref[s, 4 * main : 4 * (main + plan.tail), :] = ordered[
                s * 4 * plan.tail : (s + 1) * 4 * plan.tail
            ].astype(BF16)


def table_of(plan, ret_ref):
    main = plan.main
    pieces = [
        jnp.concatenate([ret_ref[s, c * main : (c + 1) * main, :] for s in range(plan.owners)], axis=0)
        for c in range(4)
    ]
    table = jnp.concatenate(pieces, axis=1)
    if plan.tail:
        stack = jnp.concatenate(
            [ret_ref[s, 4 * main : 4 * (main + plan.tail), :].astype(F32) for s in range(plan.owners)], axis=0
        )
        ordered = dot(tail_order(plan, False), stack.astype(BF16))
        count = plan.tail * plan.owners
        spare = jnp.concatenate([ordered[c * count : (c + 1) * count] for c in range(4)], axis=1)
        table = jnp.concatenate([table, spare.astype(BF16)], axis=0)
    return table


def gru_kernel(plan, ret_ref, row_ref, col_ref, far_enc, *refs):
    reps = plan.reps
    parts = refs[: 3 * reps]
    out_ref, hnew_ref, hdst_ref, gin, ghid, delta, hsrc_ref, enc_ref, w_in, w_hid, w_time, sems = refs[3 * reps :]
    copies = [pltpu.make_async_copy(far_enc, enc_ref, sems.at[0])]
    for g, held in ((1, w_hid), (0, w_in), (2, w_time)):
        for k in range(reps):
            copies.append(pltpu.make_async_copy(parts[g * reps + k], held.at[k], sems.at[1 + g * reps + k]))
    for copy in copies:
        copy.start()
    me = lax.axis_index("rep")
    events, width = hnew_ref.shape
    piece = width // reps
    cols = col_ref[...].astype(I32)
    spots = iota((events, plan.rows), 1)
    table = table_of(plan, ret_ref)
    source = dot(jnp.where(cols[:, 0:1] == spots, 1.0, 0.0).astype(BF16), table).astype(BF16)
    hsrc_ref[...] = source
    target = dot(jnp.where(cols[:, 1:2] == spots, 1.0, 0.0).astype(BF16), table).astype(BF16)
    hdst_ref[...] = target
    for copy in copies:
        copy.wait()
    source, target = hsrc_ref[...], hdst_ref[...]
    enc = enc_ref[...]
    part = w_in.shape[2]
    for k in range(0, reps, 2):
        both = [jnp.concatenate([w[k], w[k + 1]], axis=1) for w in (w_in, w_time, w_hid)]
        into = dot(target, both[0]) + dot(enc, both[1])
        hidden = dot(source, both[2])
        for j in range(2):
            at = pl.ds(pl.multiple_of((me ^ (k + j)) * part, LANES), part)
            gin[:, at] = into[:, j * part : (j + 1) * part]
            ghid[:, at] = hidden[:, j * part : (j + 1) * part]
    step = 64
    for i in range(0, events, step):
        at = slice(i, i + step)
        reset = 0.5 * jnp.tanh(0.5 * (gin[at, :width] + ghid[at, :width])) + 0.5
        update = 0.5 * jnp.tanh(0.5 * (gin[at, width : 2 * width] + ghid[at, width : 2 * width])) + 0.5
        fresh = jnp.tanh(gin[at, 2 * width :] + reset * ghid[at, 2 * width :])
        hold = hsrc_ref[at, :].astype(F32)
        new = (1.0 - update) * fresh + update * hold
        hnew_ref[at, :] = new
        delta[at, :] = (new - hold).astype(BF16)
    slots = plan.owners * plan.pad
    hits = jnp.where(row_ref[0:1, :] == iota((slots, events), 0), 1.0, 0.0)
    counts = jnp.maximum(jnp.sum(hits, axis=1, keepdims=True), 1.0)
    hits = hits.astype(BF16)
    mean = dot(hits, delta[...]) / counts
    for o in range(plan.owners):
        for q in range(reps):
            out_ref[o * reps + q] = mean[o * plan.pad : (o + 1) * plan.pad, q * piece : (q + 1) * piece].astype(BF16)


def attend_kernel(plan, listed_ref, hnew_ref, hdst_ref, memory_ref, *refs):
    reps = plan.reps
    w_query, w_keyval = refs[:reps], refs[reps : 2 * reps]
    out_ref, upper_ref, lower_ref, query, keyval = refs[2 * reps :]
    me = lax.axis_index("rep")
    events, width = hnew_ref.shape
    half, piece = upper_ref.shape
    lane = pl.ds(pl.multiple_of(me * piece, LANES), piece)
    upper_ref[...] = memory_ref[:half, lane]
    lower_ref[...] = memory_ref[half:, lane]
    head = width // H
    hround = hnew_ref[...].astype(BF16)
    target = hdst_ref[...]
    first = width // reps
    for k in range(reps):
        query[:, pl.ds(pl.multiple_of((me ^ k) * first, LANES), first)] = dot(hround, w_query[k][...]).astype(BF16)
        at = pl.ds(pl.multiple_of((me ^ k) * 2 * first, LANES), 2 * first)
        keyval[:, at] = dot(target, w_keyval[k][...]).astype(BF16)
    for i in range(events // BLK):
        spans = [pl.ds(pl.multiple_of(listed_ref[i, j] * BLK, BLK), BLK) for j in range(NB)]
        at = slice(i * BLK, (i + 1) * BLK)
        for h in range(H):
            lane = slice(h * head, (h + 1) * head)
            keys = jnp.concatenate([keyval[s, lane] for s in spans], axis=0)
            values = jnp.concatenate([keyval[s, width + h * head : width + (h + 1) * head] for s in spans], axis=0)
            scores = lax.dot_general(
                query[at, lane], keys, (((1,), (1,)), ((), ())), preferred_element_type=F32
            ) * (1.0 / math.sqrt(head))
            peak = jnp.max(scores, axis=1, keepdims=True)
            power = jnp.exp(scores - peak)
            prob = (power / jnp.sum(power, axis=1, keepdims=True)).astype(BF16)
            out_ref[at, lane] = (hnew_ref[at, lane] + dot(prob, values)).astype(BF16)


def apply_kernel(plan, first, ids_ref, landed_ref, part_ref, out_ref, held, total, sem):
    copy = pltpu.make_async_copy(part_ref, held, sem)
    copy.start()
    rows = part_ref.shape[0]
    count = landed_ref.shape[0]
    landed = landed_ref[...]
    step = min(256, rows)
    ids = ids_ref[...].astype(jnp.int16)
    for i in range(0, rows, step):
        here = lax.broadcasted_iota(jnp.int16, (step, count), 0) + jnp.int16(first + i)
        hot = jnp.where(here == ids, jnp.ones((), BF16), jnp.zeros((), BF16))
        total[i : i + step, :] = dot(hot, landed)
    copy.wait()
    out_ref[...] = (held[...].astype(F32) + total[...]).astype(BF16)


def join_kernel(plan, *refs):
    me = lax.axis_index("rep")
    out_ref, sems = refs[2 * plan.reps :]
    copies = []
    for h in range(2):
        for k in range(plan.reps):
            ref = refs[h * plan.reps + k]
            rows, piece = ref.shape
            at = pl.ds(pl.multiple_of((me ^ k) * piece, LANES), piece)
            copies.append(pltpu.make_async_copy(ref, out_ref.at[pl.ds(h * rows, rows), at], sems.at[h, k]))
    for copy in copies:
        copy.start()
    for copy in copies:
        copy.wait()


def swap(x, bit, reps):
    return lax.ppermute(x, "rep", [(i, i ^ bit) for i in range(reps)])


def spread(arrays, reps):
    held = [{0: x} for x in arrays]
    bit = reps // 2
    while bit:
        for parts in held:
            for k in list(parts):
                parts[k ^ bit] = swap(parts[k], bit, reps)
        bit //= 2
    return [[parts[k] for k in range(reps)] for parts in held]


def shards(
    memory,
    touch_owner,
    touch_row,
    touch_time,
    src_slot,
    dst_slot,
    event_time,
    neighbour_blocks,
    time_freq,
    time_phase,
    w_input,
    w_time,
    w_hidden,
    w_query,
    w_keyval,
):
    owners = lax.axis_size("shard")
    reps = lax.axis_size("rep")
    entries = touch_row.shape[0]
    events = event_time.shape[0]
    stored, width = memory.shape
    plan = Plan(owners, reps, entries)
    piece = width // reps
    run = functools.partial
    sds = jax.ShapeDtypeStruct

    owner = touch_owner.reshape(1, entries)
    request = call(
        run(request_kernel, plan), [sds((owners, LANES), I32)], [VMEM] * 2, 1 << 20, 1 << 14, "request", limit=8
    )(owner, touch_row.reshape(1, entries))[0]

    request, w_time, w_hidden, w_input, w_keyval, w_query = lax.optimization_barrier(
        (request, w_time, w_hidden, w_input, w_keyval, w_query)
    )
    full_time, full_hidden, full_input, full_keyval, full_query = spread(
        [w_time, w_hidden, w_input, w_keyval, w_query], reps
    )

    asked = lax.all_to_all(request, "shard", split_axis=0, concat_axis=0, tiled=True)
    encode, cols, rows = call(
        run(index_kernel, plan),
        [sds((events, time_freq.shape[0]), BF16), sds((events, 8), F32), sds((8, events), I32)],
        [VMEM] * 4,
        8 << 30,
        1 << 18,
        "index",
        limit=8,
    )(
        owner,
        jnp.concatenate([touch_time, src_slot, dst_slot, event_time]).reshape(1, -1),
        time_freq.reshape(1, -1),
        time_phase.reshape(1, -1),
    )
    everyone = [x for x in spread([asked], reps)[0]]

    served = call(
        run(serve_kernel, plan),
        [sds((owners, 4 * (plan.main + plan.tail), width // 4), BF16)],
        [VMEM, HBM],
        2 * plan.rows * stored * width,
        2 * stored * width + 2 * plan.rows * width,
        "serve",
        scratch=[
            pltpu.VMEM((stored, width), BF16),
            pltpu.VMEM((plan.rows, stored), BF16),
            pltpu.SemaphoreType.DMA((4,)),
        ],
        limit=16,
    )(asked, *far([memory]))[0]
    returned = lax.all_to_all(served, "shard", split_axis=0, concat_axis=0, tiled=True)

    outgoing, hnew, hdst = call(
        run(gru_kernel, plan),
        [sds((owners * reps, plan.pad, piece), BF16), sds((events, width), F32), sds((events, width), BF16)],
        [VMEM] * 3 + [HBM] * (1 + 3 * reps),
        2 * events * width * 3 * width * 2,
        8 << 20,
        "gru",
        scratch=[
            pltpu.VMEM((events, 3 * width), F32),
            pltpu.VMEM((events, 3 * width), F32),
            pltpu.VMEM((events, width), BF16),
            pltpu.VMEM((events, width), BF16),
            pltpu.VMEM(encode.shape, BF16),
        ]
        + [pltpu.VMEM((reps,) + x.shape, BF16) for x in (w_input, w_hidden, w_time)]
        + [pltpu.SemaphoreType.DMA((1 + 3 * reps,))],
        limit=24,
    )(returned, rows, cols, *far([encode, *full_input, *full_hidden, *full_time]))
    landed = lax.all_to_all(outgoing, ("shard", "rep"), split_axis=0, concat_axis=0, tiled=True)

    embed, *part = call(
        run(attend_kernel, plan),
        [sds((events, width), BF16)] + [sds((stored // 2, piece), BF16)] * 2,
        [SMEM] + [VMEM] * (3 + 2 * reps),
        2 * events * width * 3 * width,
        4 << 20,
        "attend",
        scratch=[
            pltpu.VMEM((events, width), BF16),
            pltpu.VMEM((events, 2 * width), BF16),
        ],
        limit=12,
    )(neighbour_blocks, hnew, hdst, memory, *full_query, *full_keyval)

    me = lax.axis_index("rep")
    stack = jnp.stack([x[:, : plan.pad] for x in everyone])
    order = me ^ jnp.arange(reps, dtype=I32)
    ids = jnp.swapaxes(stack[order], 0, 1).reshape(1, owners * reps * plan.pad)
    landed = landed.reshape(owners * reps * plan.pad, piece)
    half = stored // 2
    quarters = [
        call(
            run(apply_kernel, plan, h * half),
            [sds((half, piece), BF16)],
            [VMEM] * 2 + [HBM],
            4 << 30,
            1 << 20,
            "apply",
            scratch=[pltpu.VMEM((half, piece), BF16), pltpu.VMEM((half, piece), F32), pltpu.SemaphoreType.DMA],
            limit=16,
        )(ids, landed, *far([part[h]]))[0]
        for h in range(2)
    ]
    upper, lower = spread(quarters, reps)
    new_memory = call(
        run(join_kernel, plan),
        [sds((stored, width), BF16)],
        [VMEM] * (2 * reps),
        1 << 20,
        2 << 20,
        "join",
        scratch=[pltpu.SemaphoreType.DMA((2, reps))],
        out_specs=[HBM],
    )(*upper, *lower)[0]
    return (embed, new_memory)


def solution(mesh):
    placed = (
        P("shard", None),
        P(("shard", "rep"), None),
        P(("shard", "rep")),
        P(("shard", "rep")),
        P(("shard", "rep")),
        P(("shard", "rep")),
        P(("shard", "rep")),
        P(("shard", "rep"), None),
        P(),
        P(),
        P(None, "rep"),
        P(None, "rep"),
        P(None, "rep"),
        P(None, "rep"),
        P(None, "rep"),
    )
    return jax.shard_map(
        shards,
        mesh=mesh,
        in_specs=placed,
        out_specs=(P(("shard", "rep"), None), P("shard", None)),
        check_vma=False,
    )
```

```python
import functools
import math

import jax
import jax.numpy as jnp
from jax import lax
from jax.experimental import pallas as pl
from jax.experimental.pallas import tpu as pltpu
from jax.sharding import PartitionSpec as P

H = 4
BLK = 128
NB = 2
LANES = 128
F32 = jnp.float32
BF16 = jnp.bfloat16
I32 = jnp.int32
VMEM = pl.BlockSpec(memory_space=pltpu.VMEM)
SMEM = pl.BlockSpec(memory_space=pltpu.SMEM)
HBM = pl.BlockSpec(memory_space=pltpu.HBM)


def iota(shape, dim):
    return lax.broadcasted_iota(I32, shape, dim)


def dot(a, b):
    return jnp.dot(a, b, preferred_element_type=F32)


def call(body, outs, specs, flops, bytes_, name, scratch=(), limit=8, out_specs=None):
    return pl.pallas_call(
        body,
        out_shape=outs,
        in_specs=specs,
        out_specs=out_specs or [VMEM] * len(outs),
        scratch_shapes=list(scratch),
        compiler_params=pltpu.CompilerParams(vmem_limit_bytes=limit << 20),
        cost_estimate=pl.CostEstimate(flops=flops, bytes_accessed=bytes_, transcendentals=0),
        name=name,
    )


def far(arrays):
    return [pltpu.with_memory_space_constraint(x, pltpu.HBM) for x in arrays]


class Plan:
    def __init__(self, owners, reps, entries):
        self.owners = owners
        self.reps = reps
        self.entries = entries
        self.cap = 2 * entries // owners + 2
        self.tail = self.cap % 16 if self.cap % 16 * 4 == 8 else 0
        self.main = self.cap - self.tail if self.tail else -(-self.cap // 16) * 16
        self.rows = self.owners * (self.main + self.tail)
        self.pad = -(-self.cap // 8) * 8


def rank_of(own_col, own_row, entries):
    earlier = (own_col == own_row) & (iota((entries, entries), 0) < iota((entries, entries), 1))
    later = (own_col == own_row) & (iota((entries, entries), 1) < iota((entries, entries), 0))
    place_row = jnp.sum(jnp.where(earlier, 1, 0), axis=0, keepdims=True)
    place_col = jnp.sum(jnp.where(later, 1, 0), axis=1, keepdims=True)
    return place_row, place_col


def to_col(row, size):
    eye = iota((size, size), 0) == iota((size, size), 1)
    return jnp.sum(jnp.where(eye, row, 0), axis=1, keepdims=True)


def request_kernel(plan, owner_ref, row_ref, out_ref):
    own_row = owner_ref[...]
    own_col = to_col(own_row, plan.entries)
    _, place_col = rank_of(own_col, own_row, plan.entries)
    row = row_ref[...]
    mine = iota((plan.owners, plan.entries), 0) == own_row
    spot = jnp.where(place_col == iota((plan.entries, LANES), 1), 1.0, 0.0).astype(BF16)
    high = jnp.where(mine, row >> 5, 0).astype(F32).astype(BF16)
    low = jnp.where(mine, row & 31, 0).astype(F32).astype(BF16)
    out_ref[...] = (dot(high, spot) * 32.0 + dot(low, spot)).astype(I32)


def index_kernel(plan, owner_ref, packed_ref, freq_ref, phase_ref, enc_ref, col_ref, row_ref):
    events = enc_ref.shape[0]
    ends = [plan.entries + i * events for i in range(4)]
    tick_row = packed_ref[:, : ends[0]]
    src_row, dst_row, stamp_row = (packed_ref[:, a : a + events] for a in ends[:3])
    own_row = owner_ref[...]
    own_col = to_col(own_row, plan.entries)
    _, place = rank_of(own_col, own_row, plan.entries)
    tick = to_col(tick_row, plan.entries)
    spot = own_col * plan.main + place
    if plan.tail:
        spare = plan.owners * plan.main + (place - plan.main) * plan.owners + own_col
        spot = jnp.where(place < plan.main, spot, spare)
    back = own_col * plan.pad + place
    isrc = iota((plan.entries, events), 0) == src_row
    idst = iota((plan.entries, events), 0) == dst_row

    def pick(mask, values):
        return jnp.sum(jnp.where(mask, values, 0), axis=0, keepdims=True)

    src_spot = pick(isrc, spot)
    dst_spot = pick(idst, spot)
    src_back = pick(isrc, back)
    span = stamp_row - pick(isrc, tick)
    zero = jnp.zeros((8 - 3, events), I32)
    rows = jnp.concatenate([src_spot, dst_spot, span, zero], axis=0)
    row_ref[...] = jnp.concatenate([src_back, jnp.zeros((7, events), I32)], axis=0)
    cols = rows.astype(F32).T
    col_ref[...] = cols
    enc_ref[...] = jnp.cos(cols[:, 2:3] * freq_ref[...] + phase_ref[...]).astype(BF16)


def tail_order(plan, forward):
    count = 4 * plan.tail * plan.owners
    across = 0 if forward else 1
    there = iota((count, count), across)
    here = iota((count, count), 1 - across)
    part = 4 * plan.tail
    owner, inner = there // part, there % part
    return jnp.where((inner * plan.owners + owner) == here, 1.0, 0.0).astype(BF16)


def serve_kernel(plan, asked_ref, memory_ref, out_ref, held, hot_ref, sems):
    stored, width = memory_ref.shape
    piece = width // 4
    step = stored // 4
    copies = [
        pltpu.make_async_copy(memory_ref.at[pl.ds(i * step, step)], held.at[pl.ds(i * step, step)], sems.at[i])
        for i in range(4)
    ]
    for copy in copies:
        copy.start()
    asked = asked_ref[...]
    turned = asked.astype(F32).T
    blocks = [
        jnp.where(turned[: plan.main, s : s + 1].astype(I32) == iota((plan.main, stored), 1), 1.0, 0.0)
        for s in range(plan.owners)
    ]
    for i in range(plan.tail):
        spare = asked[:, plan.main + i : plan.main + i + 1]
        blocks.append(jnp.where(spare == iota((plan.owners, stored), 1), 1.0, 0.0))
    hot_ref[...] = jnp.concatenate(blocks, axis=0).astype(BF16)
    for copy in copies:
        copy.wait()
    rows = dot(hot_ref[...], held[...])
    main = plan.main
    for s in range(plan.owners):
        for c in range(4):
            out_ref[s, c * main : (c + 1) * main, :] = rows[
                s * main : (s + 1) * main, c * piece : (c + 1) * piece
            ].astype(BF16)
    if plan.tail:
        spare = rows[plan.owners * main :]
        stack = jnp.concatenate([spare[:, c * piece : (c + 1) * piece] for c in range(4)], axis=0)
        ordered = dot(tail_order(plan, True), stack.astype(BF16))
        for s in range(plan.owners):
            out_ref[s, 4 * main : 4 * (main + plan.tail), :] = ordered[
                s * 4 * plan.tail : (s + 1) * 4 * plan.tail
            ].astype(BF16)


def table_of(plan, ret_ref):
    main = plan.main
    pieces = [
        jnp.concatenate([ret_ref[s, c * main : (c + 1) * main, :] for s in range(plan.owners)], axis=0)
        for c in range(4)
    ]
    table = jnp.concatenate(pieces, axis=1)
    if plan.tail:
        stack = jnp.concatenate(
            [ret_ref[s, 4 * main : 4 * (main + plan.tail), :].astype(F32) for s in range(plan.owners)], axis=0
        )
        ordered = dot(tail_order(plan, False), stack.astype(BF16))
        count = plan.tail * plan.owners
        spare = jnp.concatenate([ordered[c * count : (c + 1) * count] for c in range(4)], axis=1)
        table = jnp.concatenate([table, spare.astype(BF16)], axis=0)
    return table


def gru_kernel(plan, ret_ref, row_ref, col_ref, far_enc, *refs):
    reps = plan.reps
    parts = refs[: 3 * reps]
    out_ref, hnew_ref, hdst_ref, gin, ghid, delta, hsrc_ref, enc_ref, w_in, w_hid, w_time, sems = refs[3 * reps :]
    copies = [pltpu.make_async_copy(far_enc, enc_ref, sems.at[0])]
    for g, held in ((1, w_hid), (0, w_in), (2, w_time)):
        for k in range(reps):
            copies.append(pltpu.make_async_copy(parts[g * reps + k], held.at[k], sems.at[1 + g * reps + k]))
    for copy in copies:
        copy.start()
    me = lax.axis_index("rep")
    events, width = hnew_ref.shape
    piece = width // reps
    cols = col_ref[...].astype(I32)
    spots = iota((events, plan.rows), 1)
    table = table_of(plan, ret_ref)
    source = dot(jnp.where(cols[:, 0:1] == spots, 1.0, 0.0).astype(BF16), table).astype(BF16)
    hsrc_ref[...] = source
    target = dot(jnp.where(cols[:, 1:2] == spots, 1.0, 0.0).astype(BF16), table).astype(BF16)
    hdst_ref[...] = target
    for copy in copies:
        copy.wait()
    source, target = hsrc_ref[...], hdst_ref[...]
    enc = enc_ref[...]
    part = w_in.shape[2]
    for k in range(0, reps, 2):
        both = [jnp.concatenate([w[k], w[k + 1]], axis=1) for w in (w_in, w_time, w_hid)]
        into = dot(target, both[0]) + dot(enc, both[1])
        hidden = dot(source, both[2])
        for j in range(2):
            at = pl.ds(pl.multiple_of((me ^ (k + j)) * part, LANES), part)
            gin[:, at] = into[:, j * part : (j + 1) * part]
            ghid[:, at] = hidden[:, j * part : (j + 1) * part]
    step = 64
    for i in range(0, events, step):
        at = slice(i, i + step)
        reset = 0.5 * jnp.tanh(0.5 * (gin[at, :width] + ghid[at, :width])) + 0.5
        update = 0.5 * jnp.tanh(0.5 * (gin[at, width : 2 * width] + ghid[at, width : 2 * width])) + 0.5
        fresh = jnp.tanh(gin[at, 2 * width :] + reset * ghid[at, 2 * width :])
        hold = hsrc_ref[at, :].astype(F32)
        new = (1.0 - update) * fresh + update * hold
        hnew_ref[at, :] = new
        delta[at, :] = (new - hold).astype(BF16)
    slots = plan.owners * plan.pad
    hits = jnp.where(row_ref[0:1, :] == iota((slots, events), 0), 1.0, 0.0)
    counts = jnp.maximum(jnp.sum(hits, axis=1, keepdims=True), 1.0)
    hits = hits.astype(BF16)
    mean = dot(hits, delta[...]) / counts
    for o in range(plan.owners):
        for q in range(reps):
            out_ref[o * reps + q] = mean[o * plan.pad : (o + 1) * plan.pad, q * piece : (q + 1) * piece].astype(BF16)


def attend_kernel(plan, listed_ref, hnew_ref, hdst_ref, memory_ref, *refs):
    reps = plan.reps
    w_query, w_keyval = refs[:reps], refs[reps : 2 * reps]
    out_ref, upper_ref, lower_ref, query, keyval = refs[2 * reps :]
    me = lax.axis_index("rep")
    events, width = hnew_ref.shape
    half, piece = upper_ref.shape
    lane = pl.ds(pl.multiple_of(me * piece, LANES), piece)
    upper_ref[...] = memory_ref[:half, lane]
    lower_ref[...] = memory_ref[half:, lane]
    head = width // H
    hround = hnew_ref[...].astype(BF16)
    target = hdst_ref[...]
    first = width // reps
    for k in range(reps):
        query[:, pl.ds(pl.multiple_of((me ^ k) * first, LANES), first)] = dot(hround, w_query[k][...]).astype(BF16)
        at = pl.ds(pl.multiple_of((me ^ k) * 2 * first, LANES), 2 * first)
        keyval[:, at] = dot(target, w_keyval[k][...]).astype(BF16)
    for i in range(events // BLK):
        spans = [pl.ds(pl.multiple_of(listed_ref[i, j] * BLK, BLK), BLK) for j in range(NB)]
        at = slice(i * BLK, (i + 1) * BLK)
        for h in range(H):
            lane = slice(h * head, (h + 1) * head)
            keys = jnp.concatenate([keyval[s, lane] for s in spans], axis=0)
            values = jnp.concatenate([keyval[s, width + h * head : width + (h + 1) * head] for s in spans], axis=0)
            scores = lax.dot_general(
                query[at, lane], keys, (((1,), (1,)), ((), ())), preferred_element_type=F32
            ) * (1.0 / math.sqrt(head))
            peak = jnp.max(scores, axis=1, keepdims=True)
            power = jnp.exp(scores - peak)
            prob = (power / jnp.sum(power, axis=1, keepdims=True)).astype(BF16)
            out_ref[at, lane] = (hnew_ref[at, lane] + dot(prob, values)).astype(BF16)


def total_of(first, rows, ids_ref, landed_ref, out):
    count = landed_ref.shape[0]
    landed = landed_ref[...]
    step = min(256, rows)
    ids = ids_ref[...].astype(jnp.int16)
    for i in range(0, rows, step):
        here = lax.broadcasted_iota(jnp.int16, (step, count), 0) + jnp.int16(first + i)
        hot = jnp.where(here == ids, jnp.ones((), BF16), jnp.zeros((), BF16))
        out[i : i + step, :] = dot(hot, landed)


def upper_kernel(plan, ids_ref, landed_ref, part_ref, next_ref, out_ref, kept_ref, held, total, sems):
    copies = [pltpu.make_async_copy(part_ref, held, sems.at[0]), pltpu.make_async_copy(next_ref, kept_ref, sems.at[1])]
    for copy in copies:
        copy.start()
    total_of(0, part_ref.shape[0], ids_ref, landed_ref, total)
    for copy in copies:
        copy.wait()
    out_ref[...] = (held[...].astype(F32) + total[...]).astype(BF16)


def lower_kernel(plan, ids_ref, landed_ref, part_ref, out_ref, total):
    rows = part_ref.shape[0]
    total_of(rows, rows, ids_ref, landed_ref, total)
    out_ref[...] = (part_ref[...].astype(F32) + total[...]).astype(BF16)


def join_kernel(plan, *refs):
    me = lax.axis_index("rep")
    out_ref, sems = refs[2 * plan.reps :]
    copies = []
    for h in range(2):
        for k in range(plan.reps):
            ref = refs[h * plan.reps + k]
            rows, piece = ref.shape
            at = pl.ds(pl.multiple_of((me ^ k) * piece, LANES), piece)
            copies.append(pltpu.make_async_copy(ref, out_ref.at[pl.ds(h * rows, rows), at], sems.at[h, k]))
    for copy in copies:
        copy.start()
    for copy in copies:
        copy.wait()


def swap(x, bit, reps):
    return lax.ppermute(x, "rep", [(i, i ^ bit) for i in range(reps)])


def spread(arrays, reps):
    held = [{0: x} for x in arrays]
    bit = reps // 2
    while bit:
        for parts in held:
            for k in list(parts):
                parts[k ^ bit] = swap(parts[k], bit, reps)
        bit //= 2
    return [[parts[k] for k in range(reps)] for parts in held]


def shards(
    memory,
    touch_owner,
    touch_row,
    touch_time,
    src_slot,
    dst_slot,
    event_time,
    neighbour_blocks,
    time_freq,
    time_phase,
    w_input,
    w_time,
    w_hidden,
    w_query,
    w_keyval,
):
    owners = lax.axis_size("shard")
    reps = lax.axis_size("rep")
    entries = touch_row.shape[0]
    events = event_time.shape[0]
    stored, width = memory.shape
    plan = Plan(owners, reps, entries)
    piece = width // reps
    run = functools.partial
    sds = jax.ShapeDtypeStruct

    owner = touch_owner.reshape(1, entries)
    request = call(
        run(request_kernel, plan), [sds((owners, LANES), I32)], [VMEM] * 2, 1 << 20, 1 << 14, "request", limit=8
    )(owner, touch_row.reshape(1, entries))[0]

    request, w_time, w_hidden, w_input, w_keyval, w_query = lax.optimization_barrier(
        (request, w_time, w_hidden, w_input, w_keyval, w_query)
    )
    full_time, full_hidden, full_input, full_keyval, full_query = spread(
        [w_time, w_hidden, w_input, w_keyval, w_query], reps
    )

    asked = lax.all_to_all(request, "shard", split_axis=0, concat_axis=0, tiled=True)
    encode, cols, rows = call(
        run(index_kernel, plan),
        [sds((events, time_freq.shape[0]), BF16), sds((events, 8), F32), sds((8, events), I32)],
        [VMEM] * 4,
        8 << 30,
        1 << 18,
        "index",
        limit=8,
    )(
        owner,
        jnp.concatenate([touch_time, src_slot, dst_slot, event_time]).reshape(1, -1),
        time_freq.reshape(1, -1),
        time_phase.reshape(1, -1),
    )
    everyone = [x for x in spread([asked], reps)[0]]

    served = call(
        run(serve_kernel, plan),
        [sds((owners, 4 * (plan.main + plan.tail), width // 4), BF16)],
        [VMEM, HBM],
        8 << 30,
        2 * stored * width + 2 * plan.rows * width,
        "serve",
        scratch=[
            pltpu.VMEM((stored, width), BF16),
            pltpu.VMEM((plan.rows, stored), BF16),
            pltpu.SemaphoreType.DMA((4,)),
        ],
        limit=16,
    )(asked, *far([memory]))[0]
    returned = lax.all_to_all(served, "shard", split_axis=0, concat_axis=0, tiled=True)

    outgoing, hnew, hdst = call(
        run(gru_kernel, plan),
        [sds((owners * reps, plan.pad, piece), BF16), sds((events, width), F32), sds((events, width), BF16)],
        [VMEM] * 3 + [HBM] * (1 + 3 * reps),
        2 * events * width * 3 * width * 2,
        8 << 20,
        "gru",
        scratch=[
            pltpu.VMEM((events, 3 * width), F32),
            pltpu.VMEM((events, 3 * width), F32),
            pltpu.VMEM((events, width), BF16),
            pltpu.VMEM((events, width), BF16),
            pltpu.VMEM(encode.shape, BF16),
        ]
        + [pltpu.VMEM((reps,) + x.shape, BF16) for x in (w_input, w_hidden, w_time)]
        + [pltpu.SemaphoreType.DMA((1 + 3 * reps,))],
        limit=24,
    )(returned, rows, cols, *far([encode, *full_input, *full_hidden, *full_time]))
    landed = lax.all_to_all(outgoing, ("shard", "rep"), split_axis=0, concat_axis=0, tiled=True)

    embed, *part = call(
        run(attend_kernel, plan),
        [sds((events, width), BF16)] + [sds((stored // 2, piece), BF16)] * 2,
        [SMEM] + [VMEM] * (3 + 2 * reps),
        2 * events * width * 3 * width,
        4 << 20,
        "attend",
        scratch=[
            pltpu.VMEM((events, width), BF16),
            pltpu.VMEM((events, 2 * width), BF16),
        ],
        limit=12,
    )(neighbour_blocks, hnew, hdst, memory, *full_query, *full_keyval)

    me = lax.axis_index("rep")
    stack = jnp.stack([x[:, : plan.pad] for x in everyone])
    order = me ^ jnp.arange(reps, dtype=I32)
    ids = jnp.swapaxes(stack[order], 0, 1).reshape(1, owners * reps * plan.pad)
    landed = landed.reshape(owners * reps * plan.pad, piece)
    half = stored // 2
    sums = pltpu.VMEM((half, piece), F32)
    first, kept = call(
        run(upper_kernel, plan),
        [sds((half, piece), BF16)] * 2,
        [VMEM] * 2 + [HBM] * 2,
        4 << 30,
        1 << 20,
        "upper",
        scratch=[pltpu.VMEM((half, piece), BF16), sums, pltpu.SemaphoreType.DMA((2,))],
        limit=16,
    )(ids, landed, *far(part))
    second = call(
        run(lower_kernel, plan),
        [sds((half, piece), BF16)],
        [VMEM] * 3,
        4 << 30,
        1 << 20,
        "lower",
        scratch=[sums],
        limit=16,
    )(ids, landed, kept)[0]
    upper, lower = spread([first, second], reps)
    new_memory = call(
        run(join_kernel, plan),
        [sds((stored, width), BF16)],
        [VMEM] * (2 * reps),
        1 << 20,
        2 << 20,
        "join",
        scratch=[pltpu.SemaphoreType.DMA((2, reps))],
        out_specs=[HBM],
    )(*upper, *lower)[0]
    return (embed, new_memory)


def solution(mesh):
    placed = (
        P("shard", None),
        P(("shard", "rep"), None),
        P(("shard", "rep")),
        P(("shard", "rep")),
        P(("shard", "rep")),
        P(("shard", "rep")),
        P(("shard", "rep")),
        P(("shard", "rep"), None),
        P(),
        P(),
        P(None, "rep"),
        P(None, "rep"),
        P(None, "rep"),
        P(None, "rep"),
        P(None, "rep"),
    )
    return jax.shard_map(
        shards,
        mesh=mesh,
        in_specs=placed,
        out_specs=(P(("shard", "rep"), None), P("shard", None)),
        check_vma=False,
    )
```

```python
import functools
import math

import jax
import jax.numpy as jnp
from jax import lax
from jax.experimental import pallas as pl
from jax.experimental.pallas import tpu as pltpu
from jax.sharding import PartitionSpec as P

H = 4
BLK = 128
NB = 2
LANES = 128
F32 = jnp.float32
BF16 = jnp.bfloat16
I32 = jnp.int32
VMEM = pl.BlockSpec(memory_space=pltpu.VMEM)
SMEM = pl.BlockSpec(memory_space=pltpu.SMEM)
HBM = pl.BlockSpec(memory_space=pltpu.HBM)


def iota(shape, dim):
    return lax.broadcasted_iota(I32, shape, dim)


def dot(a, b):
    return jnp.dot(a, b, preferred_element_type=F32)


def call(body, outs, specs, flops, bytes_, name, scratch=(), limit=8, out_specs=None):
    return pl.pallas_call(
        body,
        out_shape=outs,
        in_specs=specs,
        out_specs=out_specs or [VMEM] * len(outs),
        scratch_shapes=list(scratch),
        compiler_params=pltpu.CompilerParams(vmem_limit_bytes=limit << 20),
        cost_estimate=pl.CostEstimate(flops=flops, bytes_accessed=bytes_, transcendentals=0),
        name=name,
    )


def far(arrays):
    return [pltpu.with_memory_space_constraint(x, pltpu.HBM) for x in arrays]


class Plan:
    def __init__(self, owners, reps, entries):
        self.owners = owners
        self.reps = reps
        self.entries = entries
        self.cap = 2 * entries // owners + 2
        self.tail = self.cap % 16 if self.cap % 16 * 4 == 8 else 0
        self.main = self.cap - self.tail if self.tail else -(-self.cap // 16) * 16
        self.rows = self.owners * (self.main + self.tail)
        self.pad = -(-self.cap // 8) * 8


def rank_of(own_col, own_row, entries):
    earlier = (own_col == own_row) & (iota((entries, entries), 0) < iota((entries, entries), 1))
    later = (own_col == own_row) & (iota((entries, entries), 1) < iota((entries, entries), 0))
    place_row = jnp.sum(jnp.where(earlier, 1, 0), axis=0, keepdims=True)
    place_col = jnp.sum(jnp.where(later, 1, 0), axis=1, keepdims=True)
    return place_row, place_col


def to_col(row, size):
    eye = iota((size, size), 0) == iota((size, size), 1)
    return jnp.sum(jnp.where(eye, row, 0), axis=1, keepdims=True)


def request_kernel(plan, owner_ref, row_ref, out_ref):
    own_row = owner_ref[...]
    own_col = to_col(own_row, plan.entries)
    _, place_col = rank_of(own_col, own_row, plan.entries)
    row = row_ref[...]
    mine = iota((plan.owners, plan.entries), 0) == own_row
    spot = jnp.where(place_col == iota((plan.entries, LANES), 1), 1.0, 0.0).astype(BF16)
    high = jnp.where(mine, row >> 5, 0).astype(F32).astype(BF16)
    low = jnp.where(mine, row & 31, 0).astype(F32).astype(BF16)
    out_ref[...] = (dot(high, spot) * 32.0 + dot(low, spot)).astype(I32)


def index_kernel(plan, owner_ref, packed_ref, col_ref, row_ref):
    events = col_ref.shape[0]
    ends = [plan.entries + i * events for i in range(4)]
    tick_row = packed_ref[:, : ends[0]]
    src_row, dst_row, stamp_row = (packed_ref[:, a : a + events] for a in ends[:3])
    own_row = owner_ref[...]
    own_col = to_col(own_row, plan.entries)
    _, place = rank_of(own_col, own_row, plan.entries)
    tick = to_col(tick_row, plan.entries)
    spot = own_col * plan.main + place
    if plan.tail:
        spare = plan.owners * plan.main + (place - plan.main) * plan.owners + own_col
        spot = jnp.where(place < plan.main, spot, spare)
    back = own_col * plan.pad + place
    isrc = iota((plan.entries, events), 0) == src_row
    idst = iota((plan.entries, events), 0) == dst_row

    def pick(mask, values):
        return jnp.sum(jnp.where(mask, values, 0), axis=0, keepdims=True)

    src_spot = pick(isrc, spot)
    dst_spot = pick(idst, spot)
    src_back = pick(isrc, back)
    span = stamp_row - pick(isrc, tick)
    zero = jnp.zeros((8 - 3, events), I32)
    rows = jnp.concatenate([src_spot, dst_spot, span, zero], axis=0)
    row_ref[...] = jnp.concatenate([src_back, jnp.zeros((7, events), I32)], axis=0)
    col_ref[...] = rows.astype(F32).T


def encode_kernel(col_ref, freq_ref, phase_ref, enc_ref):
    enc_ref[...] = jnp.cos(col_ref[:, 2:3] * freq_ref[...] + phase_ref[...]).astype(BF16)


def tail_order(plan, forward):
    count = 4 * plan.tail * plan.owners
    across = 0 if forward else 1
    there = iota((count, count), across)
    here = iota((count, count), 1 - across)
    part = 4 * plan.tail
    owner, inner = there // part, there % part
    return jnp.where((inner * plan.owners + owner) == here, 1.0, 0.0).astype(BF16)


def serve_kernel(plan, asked_ref, memory_ref, after_ref, out_ref, held, hot_ref, sems):
    stored, width = memory_ref.shape
    piece = width // 4
    step = stored // 4
    copies = [
        pltpu.make_async_copy(memory_ref.at[pl.ds(i * step, step)], held.at[pl.ds(i * step, step)], sems.at[i])
        for i in range(4)
    ]
    for copy in copies:
        copy.start()
    asked = asked_ref[...]
    turned = asked.astype(F32).T
    blocks = [
        jnp.where(turned[: plan.main, s : s + 1].astype(I32) == iota((plan.main, stored), 1), 1.0, 0.0)
        for s in range(plan.owners)
    ]
    for i in range(plan.tail):
        spare = asked[:, plan.main + i : plan.main + i + 1]
        blocks.append(jnp.where(spare == iota((plan.owners, stored), 1), 1.0, 0.0))
    hot_ref[...] = jnp.concatenate(blocks, axis=0).astype(BF16)
    for copy in copies:
        copy.wait()
    rows = dot(hot_ref[...], held[...])
    main = plan.main
    for s in range(plan.owners):
        for c in range(4):
            out_ref[s, c * main : (c + 1) * main, :] = rows[
                s * main : (s + 1) * main, c * piece : (c + 1) * piece
            ].astype(BF16)
    if plan.tail:
        spare = rows[plan.owners * main :]
        stack = jnp.concatenate([spare[:, c * piece : (c + 1) * piece] for c in range(4)], axis=0)
        ordered = dot(tail_order(plan, True), stack.astype(BF16))
        for s in range(plan.owners):
            out_ref[s, 4 * main : 4 * (main + plan.tail), :] = ordered[
                s * 4 * plan.tail : (s + 1) * 4 * plan.tail
            ].astype(BF16)


def table_of(plan, ret_ref):
    main = plan.main
    pieces = [
        jnp.concatenate([ret_ref[s, c * main : (c + 1) * main, :] for s in range(plan.owners)], axis=0)
        for c in range(4)
    ]
    table = jnp.concatenate(pieces, axis=1)
    if plan.tail:
        stack = jnp.concatenate(
            [ret_ref[s, 4 * main : 4 * (main + plan.tail), :].astype(F32) for s in range(plan.owners)], axis=0
        )
        ordered = dot(tail_order(plan, False), stack.astype(BF16))
        count = plan.tail * plan.owners
        spare = jnp.concatenate([ordered[c * count : (c + 1) * count] for c in range(4)], axis=1)
        table = jnp.concatenate([table, spare.astype(BF16)], axis=0)
    return table


def gru_kernel(plan, ret_ref, row_ref, col_ref, far_enc, *refs):
    reps = plan.reps
    parts = refs[: 3 * reps]
    out_ref, hnew_ref, hdst_ref, gin, ghid, delta, hsrc_ref, enc_ref, w_in, w_hid, w_time, sems = refs[3 * reps :]
    copies = [pltpu.make_async_copy(far_enc, enc_ref, sems.at[0])]
    for g, held in ((1, w_hid), (0, w_in), (2, w_time)):
        for k in range(reps):
            copies.append(pltpu.make_async_copy(parts[g * reps + k], held.at[k], sems.at[1 + g * reps + k]))
    for copy in copies:
        copy.start()
    me = lax.axis_index("rep")
    events, width = hnew_ref.shape
    piece = width // reps
    cols = col_ref[...].astype(I32)
    spots = iota((events, plan.rows), 1)
    table = table_of(plan, ret_ref)
    source = dot(jnp.where(cols[:, 0:1] == spots, 1.0, 0.0).astype(BF16), table).astype(BF16)
    hsrc_ref[...] = source
    target = dot(jnp.where(cols[:, 1:2] == spots, 1.0, 0.0).astype(BF16), table).astype(BF16)
    hdst_ref[...] = target
    for copy in copies:
        copy.wait()
    source, target = hsrc_ref[...], hdst_ref[...]
    enc = enc_ref[...]
    part = w_in.shape[2]
    for k in range(0, reps, 2):
        both = [jnp.concatenate([w[k], w[k + 1]], axis=1) for w in (w_in, w_time, w_hid)]
        into = dot(target, both[0]) + dot(enc, both[1])
        hidden = dot(source, both[2])
        for j in range(2):
            at = pl.ds(pl.multiple_of((me ^ (k + j)) * part, LANES), part)
            gin[:, at] = into[:, j * part : (j + 1) * part]
            ghid[:, at] = hidden[:, j * part : (j + 1) * part]
    step = 64
    for i in range(0, events, step):
        at = slice(i, i + step)
        reset = 0.5 * jnp.tanh(0.5 * (gin[at, :width] + ghid[at, :width])) + 0.5
        update = 0.5 * jnp.tanh(0.5 * (gin[at, width : 2 * width] + ghid[at, width : 2 * width])) + 0.5
        fresh = jnp.tanh(gin[at, 2 * width :] + reset * ghid[at, 2 * width :])
        hold = hsrc_ref[at, :].astype(F32)
        new = (1.0 - update) * fresh + update * hold
        hnew_ref[at, :] = new
        delta[at, :] = (new - hold).astype(BF16)
    slots = plan.owners * plan.pad
    hits = jnp.where(row_ref[0:1, :] == iota((slots, events), 0), 1.0, 0.0)
    counts = jnp.maximum(jnp.sum(hits, axis=1, keepdims=True), 1.0)
    hits = hits.astype(BF16)
    mean = dot(hits, delta[...]) / counts
    for o in range(plan.owners):
        for q in range(reps):
            out_ref[o * reps + q] = mean[o * plan.pad : (o + 1) * plan.pad, q * piece : (q + 1) * piece].astype(BF16)


def attend_kernel(plan, listed_ref, hnew_ref, hdst_ref, memory_ref, *refs):
    reps = plan.reps
    w_query, w_keyval = refs[:reps], refs[reps : 2 * reps]
    out_ref, upper_ref, lower_ref, query, keyval = refs[2 * reps :]
    me = lax.axis_index("rep")
    events, width = hnew_ref.shape
    half, piece = upper_ref.shape
    lane = pl.ds(pl.multiple_of(me * piece, LANES), piece)
    upper_ref[...] = memory_ref[:half, lane]
    lower_ref[...] = memory_ref[half:, lane]
    head = width // H
    hround = hnew_ref[...].astype(BF16)
    target = hdst_ref[...]
    first = width // reps
    for k in range(reps):
        query[:, pl.ds(pl.multiple_of((me ^ k) * first, LANES), first)] = dot(hround, w_query[k][...]).astype(BF16)
        at = pl.ds(pl.multiple_of((me ^ k) * 2 * first, LANES), 2 * first)
        keyval[:, at] = dot(target, w_keyval[k][...]).astype(BF16)
    for i in range(events // BLK):
        spans = [pl.ds(pl.multiple_of(listed_ref[i, j] * BLK, BLK), BLK) for j in range(NB)]
        at = slice(i * BLK, (i + 1) * BLK)
        for h in range(H):
            lane = slice(h * head, (h + 1) * head)
            keys = jnp.concatenate([keyval[s, lane] for s in spans], axis=0)
            values = jnp.concatenate([keyval[s, width + h * head : width + (h + 1) * head] for s in spans], axis=0)
            scores = lax.dot_general(
                query[at, lane], keys, (((1,), (1,)), ((), ())), preferred_element_type=F32
            ) * (1.0 / math.sqrt(head))
            peak = jnp.max(scores, axis=1, keepdims=True)
            power = jnp.exp(scores - peak)
            prob = (power / jnp.sum(power, axis=1, keepdims=True)).astype(BF16)
            out_ref[at, lane] = (hnew_ref[at, lane] + dot(prob, values)).astype(BF16)


def apply_kernel(plan, first, ids_ref, landed_ref, part_ref, out_ref, held, total, sem):
    copy = pltpu.make_async_copy(part_ref, held, sem)
    copy.start()
    rows = part_ref.shape[0]
    count = landed_ref.shape[0]
    landed = landed_ref[...]
    step = min(256, rows)
    ids = ids_ref[...].astype(jnp.int16)
    for i in range(0, rows, step):
        here = lax.broadcasted_iota(jnp.int16, (step, count), 0) + jnp.int16(first + i)
        hot = jnp.where(here == ids, jnp.ones((), BF16), jnp.zeros((), BF16))
        total[i : i + step, :] = dot(hot, landed)
    copy.wait()
    out_ref[...] = (held[...].astype(F32) + total[...]).astype(BF16)


def join_kernel(plan, *refs):
    me = lax.axis_index("rep")
    out_ref, sems = refs[2 * plan.reps :]
    copies = []
    for h in range(2):
        for k in range(plan.reps):
            ref = refs[h * plan.reps + k]
            rows, piece = ref.shape
            at = pl.ds(pl.multiple_of((me ^ k) * piece, LANES), piece)
            copies.append(pltpu.make_async_copy(ref, out_ref.at[pl.ds(h * rows, rows), at], sems.at[h, k]))
    for copy in copies:
        copy.start()
    for copy in copies:
        copy.wait()


def swap(x, bit, reps):
    return lax.ppermute(x, "rep", [(i, i ^ bit) for i in range(reps)])


def spread(arrays, reps):
    held = [{0: x} for x in arrays]
    bit = reps // 2
    while bit:
        for parts in held:
            for k in list(parts):
                parts[k ^ bit] = swap(parts[k], bit, reps)
        bit //= 2
    return [[parts[k] for k in range(reps)] for parts in held]


def shards(
    memory,
    touch_owner,
    touch_row,
    touch_time,
    src_slot,
    dst_slot,
    event_time,
    neighbour_blocks,
    time_freq,
    time_phase,
    w_input,
    w_time,
    w_hidden,
    w_query,
    w_keyval,
):
    owners = lax.axis_size("shard")
    reps = lax.axis_size("rep")
    entries = touch_row.shape[0]
    events = event_time.shape[0]
    stored, width = memory.shape
    plan = Plan(owners, reps, entries)
    piece = width // reps
    run = functools.partial
    sds = jax.ShapeDtypeStruct

    owner = touch_owner.reshape(1, entries)
    request = call(
        run(request_kernel, plan), [sds((owners, LANES), I32)], [VMEM] * 2, 1 << 20, 1 << 14, "request", limit=8
    )(owner, touch_row.reshape(1, entries))[0]

    request, w_time, w_hidden, w_input, w_keyval, w_query = lax.optimization_barrier(
        (request, w_time, w_hidden, w_input, w_keyval, w_query)
    )
    full_time, full_hidden, full_input, full_keyval, full_query = spread(
        [w_time, w_hidden, w_input, w_keyval, w_query], reps
    )

    asked = lax.all_to_all(request, "shard", split_axis=0, concat_axis=0, tiled=True)
    packed = jnp.concatenate([touch_time, src_slot, dst_slot, event_time]).reshape(1, -1)
    _, owner, packed = lax.optimization_barrier((request, owner, packed))
    cols, rows = call(
        run(index_kernel, plan),
        [sds((events, 8), F32), sds((8, events), I32)],
        [VMEM] * 2,
        8 << 30,
        1 << 18,
        "index",
    )(owner, packed)
    encode = call(
        encode_kernel, [sds((events, time_freq.shape[0]), BF16)], [VMEM] * 3, 8 << 30, 1 << 18, "encode"
    )(cols, time_freq.reshape(1, -1), time_phase.reshape(1, -1))[0]
    everyone = [x for x in spread([asked], reps)[0]]

    served = call(
        run(serve_kernel, plan),
        [sds((owners, 4 * (plan.main + plan.tail), width // 4), BF16)],
        [VMEM, HBM, HBM],
        8 << 30,
        2 * stored * width + 2 * plan.rows * width,
        "serve",
        scratch=[
            pltpu.VMEM((stored, width), BF16),
            pltpu.VMEM((plan.rows, stored), BF16),
            pltpu.SemaphoreType.DMA((4,)),
        ],
        limit=16,
    )(asked, *far([memory, cols]))[0]
    returned = lax.all_to_all(served, "shard", split_axis=0, concat_axis=0, tiled=True)

    outgoing, hnew, hdst = call(
        run(gru_kernel, plan),
        [sds((owners * reps, plan.pad, piece), BF16), sds((events, width), F32), sds((events, width), BF16)],
        [VMEM] * 3 + [HBM] * (1 + 3 * reps),
        2 * events * width * 3 * width * 2,
        8 << 20,
        "gru",
        scratch=[
            pltpu.VMEM((events, 3 * width), F32),
            pltpu.VMEM((events, 3 * width), F32),
            pltpu.VMEM((events, width), BF16),
            pltpu.VMEM((events, width), BF16),
            pltpu.VMEM(encode.shape, BF16),
        ]
        + [pltpu.VMEM((reps,) + x.shape, BF16) for x in (w_input, w_hidden, w_time)]
        + [pltpu.SemaphoreType.DMA((1 + 3 * reps,))],
        limit=24,
    )(returned, rows, cols, *far([encode, *full_input, *full_hidden, *full_time]))
    landed = lax.all_to_all(outgoing, ("shard", "rep"), split_axis=0, concat_axis=0, tiled=True)

    embed, *part = call(
        run(attend_kernel, plan),
        [sds((events, width), BF16)] + [sds((stored // 2, piece), BF16)] * 2,
        [SMEM] + [VMEM] * (3 + 2 * reps),
        2 * events * width * 3 * width,
        4 << 20,
        "attend",
        scratch=[
            pltpu.VMEM((events, width), BF16),
            pltpu.VMEM((events, 2 * width), BF16),
        ],
        limit=12,
    )(neighbour_blocks, hnew, hdst, memory, *full_query, *full_keyval)

    me = lax.axis_index("rep")
    stack = jnp.stack([x[:, : plan.pad] for x in everyone])
    order = me ^ jnp.arange(reps, dtype=I32)
    ids = jnp.swapaxes(stack[order], 0, 1).reshape(1, owners * reps * plan.pad)
    landed = landed.reshape(owners * reps * plan.pad, piece)
    half = stored // 2
    quarters = [
        call(
            run(apply_kernel, plan, h * half),
            [sds((half, piece), BF16)],
            [VMEM] * 2 + [HBM],
            4 << 30,
            1 << 20,
            "apply",
            scratch=[pltpu.VMEM((half, piece), BF16), pltpu.VMEM((half, piece), F32), pltpu.SemaphoreType.DMA],
            limit=16,
        )(ids, landed, *far([part[h]]))[0]
        for h in range(2)
    ]
    upper, lower = spread(quarters, reps)
    new_memory = call(
        run(join_kernel, plan),
        [sds((stored, width), BF16)],
        [VMEM] * (2 * reps),
        1 << 20,
        2 << 20,
        "join",
        scratch=[pltpu.SemaphoreType.DMA((2, reps))],
        out_specs=[HBM],
    )(*upper, *lower)[0]
    return (embed, new_memory)


def solution(mesh):
    placed = (
        P("shard", None),
        P(("shard", "rep"), None),
        P(("shard", "rep")),
        P(("shard", "rep")),
        P(("shard", "rep")),
        P(("shard", "rep")),
        P(("shard", "rep")),
        P(("shard", "rep"), None),
        P(),
        P(),
        P(None, "rep"),
        P(None, "rep"),
        P(None, "rep"),
        P(None, "rep"),
        P(None, "rep"),
    )
    return jax.shard_map(
        shards,
        mesh=mesh,
        in_specs=placed,
        out_specs=(P(("shard", "rep"), None), P("shard", None)),
        check_vma=False,
    )
```

```python
import functools
import math

import jax
import jax.numpy as jnp
from jax import lax
from jax.experimental import pallas as pl
from jax.experimental.pallas import tpu as pltpu
from jax.sharding import PartitionSpec as P

H = 4
BLK = 128
NB = 2
LANES = 128
F32 = jnp.float32
BF16 = jnp.bfloat16
I32 = jnp.int32
VMEM = pl.BlockSpec(memory_space=pltpu.VMEM)
SMEM = pl.BlockSpec(memory_space=pltpu.SMEM)
HBM = pl.BlockSpec(memory_space=pltpu.HBM)


def iota(shape, dim):
    return lax.broadcasted_iota(I32, shape, dim)


def dot(a, b):
    return jnp.dot(a, b, preferred_element_type=F32)


def call(body, outs, specs, flops, bytes_, name, scratch=(), limit=8, out_specs=None):
    return pl.pallas_call(
        body,
        out_shape=outs,
        in_specs=specs,
        out_specs=out_specs or [VMEM] * len(outs),
        scratch_shapes=list(scratch),
        compiler_params=pltpu.CompilerParams(vmem_limit_bytes=limit << 20),
        cost_estimate=pl.CostEstimate(flops=flops, bytes_accessed=bytes_, transcendentals=0),
        name=name,
    )


def far(arrays):
    return [pltpu.with_memory_space_constraint(x, pltpu.HBM) for x in arrays]


class Plan:
    def __init__(self, owners, reps, entries):
        self.owners = owners
        self.reps = reps
        self.entries = entries
        self.cap = 2 * entries // owners + 2
        self.tail = self.cap % 16 if self.cap % 16 * 4 == 8 else 0
        self.main = self.cap - self.tail if self.tail else -(-self.cap // 16) * 16
        self.rows = self.owners * (self.main + self.tail)
        self.pad = -(-self.cap // 8) * 8


def rank_of(own_col, own_row, entries):
    earlier = (own_col == own_row) & (iota((entries, entries), 0) < iota((entries, entries), 1))
    later = (own_col == own_row) & (iota((entries, entries), 1) < iota((entries, entries), 0))
    place_row = jnp.sum(jnp.where(earlier, 1, 0), axis=0, keepdims=True)
    place_col = jnp.sum(jnp.where(later, 1, 0), axis=1, keepdims=True)
    return place_row, place_col


def to_col(row, size):
    eye = iota((size, size), 0) == iota((size, size), 1)
    return jnp.sum(jnp.where(eye, row, 0), axis=1, keepdims=True)


def request_kernel(plan, owner_ref, row_ref, out_ref):
    own_row = owner_ref[...]
    own_col = to_col(own_row, plan.entries)
    _, place_col = rank_of(own_col, own_row, plan.entries)
    row = row_ref[...]
    mine = iota((plan.owners, plan.entries), 0) == own_row
    spot = jnp.where(place_col == iota((plan.entries, LANES), 1), 1.0, 0.0).astype(BF16)
    high = jnp.where(mine, row >> 5, 0).astype(F32).astype(BF16)
    low = jnp.where(mine, row & 31, 0).astype(F32).astype(BF16)
    out_ref[...] = (dot(high, spot) * 32.0 + dot(low, spot)).astype(I32)


def index_kernel(plan, owner_ref, packed_ref, freq_ref, phase_ref, enc_ref, col_ref, row_ref):
    events = enc_ref.shape[0]
    ends = [plan.entries + i * events for i in range(4)]
    tick_row = packed_ref[:, : ends[0]]
    src_row, dst_row, stamp_row = (packed_ref[:, a : a + events] for a in ends[:3])
    own_row = owner_ref[...]
    own_col = to_col(own_row, plan.entries)
    _, place = rank_of(own_col, own_row, plan.entries)
    tick = to_col(tick_row, plan.entries)
    spot = own_col * plan.main + place
    if plan.tail:
        spare = plan.owners * plan.main + (place - plan.main) * plan.owners + own_col
        spot = jnp.where(place < plan.main, spot, spare)
    back = own_col * plan.pad + place
    isrc = iota((plan.entries, events), 0) == src_row
    idst = iota((plan.entries, events), 0) == dst_row

    def pick(mask, values):
        return jnp.sum(jnp.where(mask, values, 0), axis=0, keepdims=True)

    src_spot = pick(isrc, spot)
    dst_spot = pick(idst, spot)
    src_back = pick(isrc, back)
    span = stamp_row - pick(isrc, tick)
    zero = jnp.zeros((8 - 3, events), I32)
    rows = jnp.concatenate([src_spot, dst_spot, span, zero], axis=0)
    row_ref[...] = jnp.concatenate([src_back, jnp.zeros((7, events), I32)], axis=0)
    cols = rows.astype(F32).T
    col_ref[...] = cols
    enc_ref[...] = jnp.cos(cols[:, 2:3] * freq_ref[...] + phase_ref[...]).astype(BF16)


def tail_order(plan, forward):
    count = 4 * plan.tail * plan.owners
    across = 0 if forward else 1
    there = iota((count, count), across)
    here = iota((count, count), 1 - across)
    part = 4 * plan.tail
    owner, inner = there // part, there % part
    return jnp.where((inner * plan.owners + owner) == here, 1.0, 0.0).astype(BF16)


def serve_kernel(plan, asked_ref, memory_ref, far_ref, out_ref, held, hot_ref, sems, out_sems):
    stored, width = memory_ref.shape
    piece = width // 4
    step = stored // 4
    copies = [
        pltpu.make_async_copy(memory_ref.at[pl.ds(i * step, step)], held.at[pl.ds(i * step, step)], sems.at[i])
        for i in range(4)
    ]
    for copy in copies:
        copy.start()
    asked = asked_ref[...]
    turned = asked.astype(F32).T
    blocks = [
        jnp.where(turned[: plan.main, s : s + 1].astype(I32) == iota((plan.main, stored), 1), 1.0, 0.0)
        for s in range(plan.owners)
    ]
    for i in range(plan.tail):
        spare = asked[:, plan.main + i : plan.main + i + 1]
        blocks.append(jnp.where(spare == iota((plan.owners, stored), 1), 1.0, 0.0))
    hot_ref[...] = jnp.concatenate(blocks, axis=0).astype(BF16)
    for copy in copies:
        copy.wait()
    rows = dot(hot_ref[...], held[...])
    main = plan.main
    if plan.tail:
        spare = rows[plan.owners * main :]
        stack = jnp.concatenate([spare[:, c * piece : (c + 1) * piece] for c in range(4)], axis=0)
        ordered = dot(tail_order(plan, True), stack.astype(BF16))
    sends = []
    for s in range(plan.owners):
        for c in range(4):
            out_ref[s, c * main : (c + 1) * main, :] = rows[
                s * main : (s + 1) * main, c * piece : (c + 1) * piece
            ].astype(BF16)
        if plan.tail:
            out_ref[s, 4 * main : 4 * (main + plan.tail), :] = ordered[
                s * 4 * plan.tail : (s + 1) * 4 * plan.tail
            ].astype(BF16)
        sends.append(pltpu.make_async_copy(out_ref.at[s], far_ref.at[s], out_sems.at[s]))
        sends[-1].start()
    for send in sends:
        send.wait()


def table_of(plan, ret_ref):
    main = plan.main
    pieces = [
        jnp.concatenate([ret_ref[s, c * main : (c + 1) * main, :] for s in range(plan.owners)], axis=0)
        for c in range(4)
    ]
    table = jnp.concatenate(pieces, axis=1)
    if plan.tail:
        stack = jnp.concatenate(
            [ret_ref[s, 4 * main : 4 * (main + plan.tail), :].astype(F32) for s in range(plan.owners)], axis=0
        )
        ordered = dot(tail_order(plan, False), stack.astype(BF16))
        count = plan.tail * plan.owners
        spare = jnp.concatenate([ordered[c * count : (c + 1) * count] for c in range(4)], axis=1)
        table = jnp.concatenate([table, spare.astype(BF16)], axis=0)
    return table


def gru_kernel(plan, ret_ref, row_ref, col_ref, far_enc, *refs):
    reps = plan.reps
    parts = refs[: 3 * reps]
    far_ref, hnew_ref, hdst_ref, out_ref, gin, ghid, delta, hsrc_ref, enc_ref, w_in, w_hid, w_time, sems, out_sems = refs[3 * reps :]
    copies = [pltpu.make_async_copy(far_enc, enc_ref, sems.at[0])]
    for g, held in ((1, w_hid), (0, w_in), (2, w_time)):
        for k in range(reps):
            copies.append(pltpu.make_async_copy(parts[g * reps + k], held.at[k], sems.at[1 + g * reps + k]))
    for copy in copies:
        copy.start()
    me = lax.axis_index("rep")
    events, width = hnew_ref.shape
    piece = width // reps
    cols = col_ref[...].astype(I32)
    spots = iota((events, plan.rows), 1)
    table = table_of(plan, ret_ref)
    source = dot(jnp.where(cols[:, 0:1] == spots, 1.0, 0.0).astype(BF16), table).astype(BF16)
    hsrc_ref[...] = source
    target = dot(jnp.where(cols[:, 1:2] == spots, 1.0, 0.0).astype(BF16), table).astype(BF16)
    hdst_ref[...] = target
    for copy in copies:
        copy.wait()
    source, target = hsrc_ref[...], hdst_ref[...]
    enc = enc_ref[...]
    part = w_in.shape[2]
    for k in range(0, reps, 2):
        both = [jnp.concatenate([w[k], w[k + 1]], axis=1) for w in (w_in, w_time, w_hid)]
        into = dot(target, both[0]) + dot(enc, both[1])
        hidden = dot(source, both[2])
        for j in range(2):
            at = pl.ds(pl.multiple_of((me ^ (k + j)) * part, LANES), part)
            gin[:, at] = into[:, j * part : (j + 1) * part]
            ghid[:, at] = hidden[:, j * part : (j + 1) * part]
    step = 64
    for i in range(0, events, step):
        at = slice(i, i + step)
        reset = 0.5 * jnp.tanh(0.5 * (gin[at, :width] + ghid[at, :width])) + 0.5
        update = 0.5 * jnp.tanh(0.5 * (gin[at, width : 2 * width] + ghid[at, width : 2 * width])) + 0.5
        fresh = jnp.tanh(gin[at, 2 * width :] + reset * ghid[at, 2 * width :])
        hold = hsrc_ref[at, :].astype(F32)
        new = (1.0 - update) * fresh + update * hold
        hnew_ref[at, :] = new
        delta[at, :] = (new - hold).astype(BF16)
    slots = plan.owners * plan.pad
    hits = jnp.where(row_ref[0:1, :] == iota((slots, events), 0), 1.0, 0.0)
    counts = jnp.maximum(jnp.sum(hits, axis=1, keepdims=True), 1.0)
    hits = hits.astype(BF16)
    mean = dot(hits, delta[...]) / counts
    sends = []
    for o in range(plan.owners):
        for q in range(reps):
            out_ref[o * reps + q] = mean[o * plan.pad : (o + 1) * plan.pad, q * piece : (q + 1) * piece].astype(BF16)
        at = pl.ds(o * reps, reps)
        sends.append(pltpu.make_async_copy(out_ref.at[at], far_ref.at[at], out_sems.at[o]))
        sends[-1].start()
    for send in sends:
        send.wait()


def attend_kernel(plan, listed_ref, hnew_ref, hdst_ref, memory_ref, *refs):
    reps = plan.reps
    w_query, w_keyval = refs[:reps], refs[reps : 2 * reps]
    out_ref, upper_ref, lower_ref, query, keyval = refs[2 * reps :]
    me = lax.axis_index("rep")
    events, width = hnew_ref.shape
    half, piece = upper_ref.shape
    lane = pl.ds(pl.multiple_of(me * piece, LANES), piece)
    upper_ref[...] = memory_ref[:half, lane]
    lower_ref[...] = memory_ref[half:, lane]
    head = width // H
    hround = hnew_ref[...].astype(BF16)
    target = hdst_ref[...]
    first = width // reps
    for k in range(reps):
        query[:, pl.ds(pl.multiple_of((me ^ k) * first, LANES), first)] = dot(hround, w_query[k][...]).astype(BF16)
        at = pl.ds(pl.multiple_of((me ^ k) * 2 * first, LANES), 2 * first)
        keyval[:, at] = dot(target, w_keyval[k][...]).astype(BF16)
    for i in range(events // BLK):
        spans = [pl.ds(pl.multiple_of(listed_ref[i, j] * BLK, BLK), BLK) for j in range(NB)]
        at = slice(i * BLK, (i + 1) * BLK)
        for h in range(H):
            lane = slice(h * head, (h + 1) * head)
            keys = jnp.concatenate([keyval[s, lane] for s in spans], axis=0)
            values = jnp.concatenate([keyval[s, width + h * head : width + (h + 1) * head] for s in spans], axis=0)
            scores = lax.dot_general(
                query[at, lane], keys, (((1,), (1,)), ((), ())), preferred_element_type=F32
            ) * (1.0 / math.sqrt(head))
            peak = jnp.max(scores, axis=1, keepdims=True)
            power = jnp.exp(scores - peak)
            prob = (power / jnp.sum(power, axis=1, keepdims=True)).astype(BF16)
            out_ref[at, lane] = (hnew_ref[at, lane] + dot(prob, values)).astype(BF16)


def apply_kernel(plan, first, ids_ref, landed_ref, part_ref, out_ref, held, total, sem):
    copy = pltpu.make_async_copy(part_ref, held, sem)
    copy.start()
    rows = part_ref.shape[0]
    count = landed_ref.shape[0]
    landed = landed_ref[...]
    step = min(256, rows)
    ids = ids_ref[...].astype(jnp.int16)
    for i in range(0, rows, step):
        here = lax.broadcasted_iota(jnp.int16, (step, count), 0) + jnp.int16(first + i)
        hot = jnp.where(here == ids, jnp.ones((), BF16), jnp.zeros((), BF16))
        total[i : i + step, :] = dot(hot, landed)
    copy.wait()
    out_ref[...] = (held[...].astype(F32) + total[...]).astype(BF16)


def join_kernel(plan, *refs):
    me = lax.axis_index("rep")
    out_ref, sems = refs[2 * plan.reps :]
    copies = []
    for h in range(2):
        for k in range(plan.reps):
            ref = refs[h * plan.reps + k]
            rows, piece = ref.shape
            at = pl.ds(pl.multiple_of((me ^ k) * piece, LANES), piece)
            copies.append(pltpu.make_async_copy(ref, out_ref.at[pl.ds(h * rows, rows), at], sems.at[h, k]))
    for copy in copies:
        copy.start()
    for copy in copies:
        copy.wait()


def swap(x, bit, reps):
    return lax.ppermute(x, "rep", [(i, i ^ bit) for i in range(reps)])


def spread(arrays, reps):
    held = [{0: x} for x in arrays]
    bit = reps // 2
    while bit:
        for parts in held:
            for k in list(parts):
                parts[k ^ bit] = swap(parts[k], bit, reps)
        bit //= 2
    return [[parts[k] for k in range(reps)] for parts in held]


def shards(
    memory,
    touch_owner,
    touch_row,
    touch_time,
    src_slot,
    dst_slot,
    event_time,
    neighbour_blocks,
    time_freq,
    time_phase,
    w_input,
    w_time,
    w_hidden,
    w_query,
    w_keyval,
):
    owners = lax.axis_size("shard")
    reps = lax.axis_size("rep")
    entries = touch_row.shape[0]
    events = event_time.shape[0]
    stored, width = memory.shape
    plan = Plan(owners, reps, entries)
    piece = width // reps
    run = functools.partial
    sds = jax.ShapeDtypeStruct

    owner = touch_owner.reshape(1, entries)
    request = call(
        run(request_kernel, plan), [sds((owners, LANES), I32)], [VMEM] * 2, 1 << 20, 1 << 14, "request", limit=8
    )(owner, touch_row.reshape(1, entries))[0]

    request, w_time, w_hidden, w_input, w_keyval, w_query = lax.optimization_barrier(
        (request, w_time, w_hidden, w_input, w_keyval, w_query)
    )
    full_time, full_hidden, full_input, full_keyval, full_query = spread(
        [w_time, w_hidden, w_input, w_keyval, w_query], reps
    )

    asked = lax.all_to_all(request, "shard", split_axis=0, concat_axis=0, tiled=True)
    encode, cols, rows = call(
        run(index_kernel, plan),
        [sds((events, time_freq.shape[0]), BF16), sds((events, 8), F32), sds((8, events), I32)],
        [VMEM] * 4,
        8 << 30,
        1 << 18,
        "index",
        limit=8,
    )(
        owner,
        jnp.concatenate([touch_time, src_slot, dst_slot, event_time]).reshape(1, -1),
        time_freq.reshape(1, -1),
        time_phase.reshape(1, -1),
    )
    everyone = [x for x in spread([asked], reps)[0]]

    served = call(
        run(serve_kernel, plan),
        [sds((owners, 4 * (plan.main + plan.tail), width // 4), BF16)],
        [VMEM, HBM],
        2 * plan.rows * stored * width,
        2 * stored * width + 2 * plan.rows * width,
        "serve",
        scratch=[
            pltpu.VMEM((owners, 4 * (plan.main + plan.tail), width // 4), BF16),
            pltpu.VMEM((stored, width), BF16),
            pltpu.VMEM((plan.rows, stored), BF16),
            pltpu.SemaphoreType.DMA((4,)),
            pltpu.SemaphoreType.DMA((owners,)),
        ],
        out_specs=[HBM],
        limit=16,
    )(asked, *far([memory]))[0]
    returned = lax.all_to_all(served, "shard", split_axis=0, concat_axis=0, tiled=True)

    outgoing, hnew, hdst = call(
        run(gru_kernel, plan),
        [sds((owners * reps, plan.pad, piece), BF16), sds((events, width), F32), sds((events, width), BF16)],
        [VMEM] * 3 + [HBM] * (1 + 3 * reps),
        2 * events * width * 3 * width * 2,
        8 << 20,
        "gru",
        out_specs=[HBM, VMEM, VMEM],
        scratch=[
            pltpu.VMEM((owners * reps, plan.pad, piece), BF16),
            pltpu.VMEM((events, 3 * width), F32),
            pltpu.VMEM((events, 3 * width), F32),
            pltpu.VMEM((events, width), BF16),
            pltpu.VMEM((events, width), BF16),
            pltpu.VMEM(encode.shape, BF16),
        ]
        + [pltpu.VMEM((reps,) + x.shape, BF16) for x in (w_input, w_hidden, w_time)]
        + [pltpu.SemaphoreType.DMA((1 + 3 * reps,)), pltpu.SemaphoreType.DMA((owners,))],
        limit=24,
    )(returned, rows, cols, *far([encode, *full_input, *full_hidden, *full_time]))
    landed = lax.all_to_all(outgoing, ("shard", "rep"), split_axis=0, concat_axis=0, tiled=True)

    embed, *part = call(
        run(attend_kernel, plan),
        [sds((events, width), BF16)] + [sds((stored // 2, piece), BF16)] * 2,
        [SMEM] + [VMEM] * (3 + 2 * reps),
        2 * events * width * 3 * width,
        4 << 20,
        "attend",
        scratch=[
            pltpu.VMEM((events, width), BF16),
            pltpu.VMEM((events, 2 * width), BF16),
        ],
        limit=12,
    )(neighbour_blocks, hnew, hdst, memory, *full_query, *full_keyval)

    me = lax.axis_index("rep")
    stack = jnp.stack([x[:, : plan.pad] for x in everyone])
    order = me ^ jnp.arange(reps, dtype=I32)
    ids = jnp.swapaxes(stack[order], 0, 1).reshape(1, owners * reps * plan.pad)
    landed = landed.reshape(owners * reps * plan.pad, piece)
    half = stored // 2
    quarters = [
        call(
            run(apply_kernel, plan, h * half),
            [sds((half, piece), BF16)],
            [VMEM] * 2 + [HBM],
            4 << 30,
            1 << 20,
            "apply",
            scratch=[pltpu.VMEM((half, piece), BF16), pltpu.VMEM((half, piece), F32), pltpu.SemaphoreType.DMA],
            limit=16,
        )(ids, landed, *far([part[h]]))[0]
        for h in range(2)
    ]
    upper, lower = spread(quarters, reps)
    new_memory = call(
        run(join_kernel, plan),
        [sds((stored, width), BF16)],
        [VMEM] * (2 * reps),
        1 << 20,
        2 << 20,
        "join",
        scratch=[pltpu.SemaphoreType.DMA((2, reps))],
        out_specs=[HBM],
    )(*upper, *lower)[0]
    return (embed, new_memory)


def solution(mesh):
    placed = (
        P("shard", None),
        P(("shard", "rep"), None),
        P(("shard", "rep")),
        P(("shard", "rep")),
        P(("shard", "rep")),
        P(("shard", "rep")),
        P(("shard", "rep")),
        P(("shard", "rep"), None),
        P(),
        P(),
        P(None, "rep"),
        P(None, "rep"),
        P(None, "rep"),
        P(None, "rep"),
        P(None, "rep"),
    )
    return jax.shard_map(
        shards,
        mesh=mesh,
        in_specs=placed,
        out_specs=(P(("shard", "rep"), None), P("shard", None)),
        check_vma=False,
    )
```
